128 devices in a mesh: tm: 32 (over y, x, core), space: 4 (over z).
Axes of the slice: x: 4, y: 4, z: 4, core: 2. Of those that a mesh axis runs over, the one named last changes fastest.
Arguments:
- tokens: bfloat16 [64, 256, 512], P('tm', 'space'), may hold values from -6 to 6
- type_ids: int32 [64, 256], P('tm', 'space'), may hold values from 0 to 2
- clip_ids: int32 [64], P('tm'), may hold values from 0 to 1, as said below
- frame_mask: int32 [64], P('tm'), may hold values from 0 to 1, as said below
- type_table: bfloat16 [3, 512], replicated, may hold values from -3 to 3
- norm_gain: float32 [512], replicated, may hold values from 0.25 to 1.75
- qkv_weight: bfloat16 [512, 1536], replicated, may hold values from -0.25 to 0.25
- out_weight: bfloat16 [512, 512], replicated, may hold values from -6 to 6
- mlp_gain: float32 [512], replicated, may hold values from 0.25 to 1.75
- up_weight: bfloat16 [512, 2048], replicated, may hold values from -0.25 to 0.25
- down_weight: bfloat16 [2048, 512], replicated, may hold values from -0.125 to 0.125
- cotangent: bfloat16 [64, 256, 512], P('tm', 'space'), may hold values from -6 to 6
Outputs:
- output: bfloat16 [64, 256, 512], P('tm', 'space')
- input_grad: float32 [64, 256, 512], P('tm', 'space')
- type_table_grad: float32 [3, 512], replicated
- norm_gain_grad: float32 [512], replicated
- qkv_weight_grad: float32 [512, 1536], replicated
- out_weight_grad: float32 [512, 512], replicated
- mlp_gain_grad: float32 [512], replicated
- up_weight_grad: float32 [512, 2048], replicated
- down_weight_grad: float32 [2048, 512], replicated
The draws below stay inside these ranges and needn't reach their ends.
Inputs may be any that keep to these rules, and one draw needn't show every extreme that they name: `clip_ids`: slots 2t and 2t+1 hold frame t of the two clips, one of each, clip 0 and clip 1 in either order. `frame_mask`: in each clip the real frames come first; one of the two clips has all 32 frames real, the other exactly 8.
All inputs are finite; a program needn't handle non-finite values.
Results may differ from the reference program's by a relative error of at most 0.014.
Values may be sent and summed in bfloat16 or wider, within the bound.
No kernel may reach another device: no remote copies, remote signals or barrier semaphores. Data moves between devices by JAX's collectives and lax.ppermute only.
A program may use at most 192 MiB of HBM per device.

```python
import jax
import jax.numpy as jnp
from jax import lax

D = 512
HEADS = 8
HEAD_DIM = 64
FF = 2048
TYPES = 3
FRAME = 256
SLOTS = 64
N_TM = 32


def clip_layout(key):
    flips = jax.random.randint(jax.random.fold_in(key, 11), (N_TM,), 0, 2)
    full_clip = jax.random.randint(jax.random.fold_in(key, 12), (), 0, 2)
    short_len = N_TM // 4
    return (flips, full_clip, short_len)


def draw_clip_ids(key, part):
    flips, full_clip, short_len = clip_layout(key)
    return jnp.stack([flips, 1 - flips], axis=1).reshape(2 * N_TM).astype(jnp.int32)


def draw_frame_mask(key, part):
    flips, full_clip, short_len = clip_layout(key)
    lengths = jnp.where(jnp.arange(2) == full_clip, N_TM, short_len)
    slot_clips = jnp.stack([flips, 1 - flips], axis=1)
    frame_index = jnp.arange(N_TM)[:, None]
    frame_real = (frame_index < lengths[slot_clips]).astype(jnp.int32)
    return frame_real.reshape(2 * N_TM)


def place_ends(values, stream_key, least, largest):
    dims = values.shape
    index_at = [jax.random.randint(jax.random.fold_in(stream_key, axis), (), 0, dims[axis]) for axis in range(len(dims))]
    values = values.at[tuple(index_at)].set(least)
    longest = dims.index(max(dims))
    index_at[longest] = (index_at[longest] + 1) % dims[longest]
    return values.at[tuple(index_at)].set(largest)


def shard_levels(key, extent, pieces, low, top_value):
    level, own = 1.0, jax.random.fold_in(key, 6)
    for position, blocks in pieces:
        steps = jnp.exp(jax.random.uniform(jax.random.fold_in(own, position), (blocks,), jnp.float32, low / len(pieces), top_value / len(pieces)))
        level = level * jnp.repeat(steps, extent[position] // blocks).reshape([-1 if axis == position else 1 for axis in range(len(extent))])
    return level


def scatter_about(rng, dims, deviation, bound, pieces=(), kind=jnp.bfloat16):
    values = jax.random.normal(rng, dims, jnp.float32) * deviation
    if len(pieces) > 0:
        values = shard_levels(rng, dims, pieces, -0.22, 0.18) * values
    return jnp.clip(values, min=-bound, max=bound).astype(kind)


def setup_inputs(seed: int = 0) -> dict:
    seeds = jax.random.split(jax.random.key(seed), 13)
    return {
        "tokens": scatter_about(seeds[0], (SLOTS, FRAME, D), 1.0, 6.0, ((0, 32), (1, 4))),
        "type_ids": place_ends(jax.random.randint(seeds[1], (SLOTS, FRAME), 0, TYPES), jax.random.fold_in(seeds[1], 1), 0, TYPES - 1).astype(jnp.int32),
        "clip_ids": draw_clip_ids(jax.random.fold_in(seeds[12], 71), 0),
        "frame_mask": draw_frame_mask(jax.random.fold_in(seeds[12], 71), 0),
        "type_table": scatter_about(seeds[4], (TYPES, D), 0.5, 3.0),
        "norm_gain": jnp.clip(1.0 + 0.15 * jax.random.normal(seeds[5], (D,), jnp.float32), 0.25, 1.75),
        "qkv_weight": scatter_about(seeds[6], (D, 3 * D), D ** -0.5, 0.25),
        "out_weight": scatter_about(seeds[7], (D, D), (max(1, 8 * D // (N_TM * FRAME))) ** -0.5, 6.0),
        "mlp_gain": jnp.clip(1.0 + 0.15 * jax.random.normal(seeds[8], (D,), jnp.float32), 0.25, 1.75),
        "up_weight": scatter_about(seeds[9], (D, FF), D ** -0.5, 0.25),
        "down_weight": scatter_about(seeds[10], (FF, D), FF ** -0.5, 0.125),
        "cotangent": scatter_about(seeds[11], (SLOTS, FRAME, D), 1.0, 6.0, ((0, 32), (1, 4))),
    }


@jax.custom_vjp
def low(v):
    return lax.optimization_barrier(v.astype(jnp.bfloat16)).astype(jnp.float32)

@jax.custom_vjp
def low_back(v):
    return v

def low_keep(v):
    return (low(v), None)

def low_pass(kept, grad):
    return (grad,)

def back_keep(v):
    return (v, None)

def back_low(kept, grad):
    return (low(grad),)
low.defvjp(low_keep, low_pass)
low_back.defvjp(back_keep, back_low)
masked_score = -1e+30
epsilon = 1e-05
rotary_base = 10000.0
precise = lax.Precision.HIGHEST

def norm_rows(hidden, gain_row):
    centre = lax.optimization_barrier(jnp.mean(hidden, axis=-1, keepdims=True))
    shifted = hidden - centre
    spread = lax.optimization_barrier(jnp.mean(shifted * shifted, axis=-1, keepdims=True))
    return shifted * lax.rsqrt(spread + epsilon) * gain_row

def rotate(values_in, positions, direction):
    shape_in = values_in.shape
    half_dim = HEAD_DIM // 2
    split_heads = values_in.reshape(shape_in[:-1] + (shape_in[-1] // HEAD_DIM, HEAD_DIM))
    rate_list = rotary_base ** (-jnp.arange(half_dim, dtype=jnp.float32) / half_dim)
    angles = positions.astype(jnp.float32)[:, None] * rate_list[None, :]
    cosine = jnp.cos(angles)[:, None, :]
    sine_part = direction * jnp.sin(angles)[:, None, :]
    first_half = split_heads[..., :half_dim]
    second_half = split_heads[..., half_dim:]
    turned = jnp.concatenate([first_half * cosine - second_half * sine_part, first_half * sine_part + second_half * cosine], axis=-1)
    return turned.reshape(shape_in)

def reference(tokens, type_ids, clip_ids, frame_mask, type_table, norm_gain, qkv_weight, out_weight, mlp_gain, up_weight, down_weight, cotangent):
    swapped = clip_ids.reshape(N_TM, 2)[:, 0] != 0
    seq_len = N_TM * FRAME

    def to_clips(array_in):
        paired = array_in.reshape((N_TM, 2) + array_in.shape[1:])
        flag_swap = swapped.reshape((N_TM,) + (1,) * (array_in.ndim - 1))
        first_clip = jnp.where(flag_swap, paired[:, 1], paired[:, 0])
        second_clip = jnp.where(flag_swap, paired[:, 0], paired[:, 1])
        return jnp.stack([first_clip, second_clip])

    def from_clips(array_in):
        flag_swap = swapped.reshape((N_TM,) + (1,) * (array_in.ndim - 2))
        slot_even = jnp.where(flag_swap, array_in[1], array_in[0])
        slot_odd = jnp.where(flag_swap, array_in[0], array_in[1])
        return jnp.stack([slot_even, slot_odd], axis=1).reshape((2 * N_TM,) + array_in.shape[2:])
    onehot = (to_clips(type_ids)[..., None] == jnp.arange(TYPES)).astype(jnp.float32)
    real_clip = to_clips(frame_mask)

    def clip_attention(query_rows, key_rows, value_rows, real_frames):
        key_heads = key_rows.reshape(seq_len, HEADS, HEAD_DIM)
        value_heads = value_rows.reshape(seq_len, HEADS, HEAD_DIM)
        key_live = jnp.repeat(real_frames, FRAME) > 0
        key_index = jnp.arange(seq_len)
        key_frame = key_index // FRAME

        @jax.checkpoint
        def frame_block(block_args):
            query_block, first_row = block_args
            query_heads = query_block.reshape(FRAME, HEADS, HEAD_DIM)
            scores = low_back(HEAD_DIM ** (-0.5) * jnp.einsum('ihd,jhd->hij', query_heads, key_heads, precision=precise))
            query_index = first_row + jnp.arange(FRAME)
            own_frame = key_frame == first_row // FRAME
            allowed = (key_live | own_frame)[None, :] & (key_index[None, :] <= query_index[:, None])
            scores = jnp.where(allowed[None], scores, masked_score)
            top_score = lax.optimization_barrier(jnp.max(scores, axis=-1, keepdims=True))
            raised = jnp.exp(scores - top_score)
            weights = low(raised / lax.optimization_barrier(jnp.sum(raised, axis=-1, keepdims=True)))
            result = jnp.einsum('hij,jhd->ihd', weights, value_heads, precision=precise)
            return result.reshape(FRAME, D)
        blocks = lax.map(frame_block, (query_rows.reshape(N_TM, FRAME, D), jnp.arange(N_TM) * FRAME))
        return blocks.reshape(seq_len, D)

    def forward(inputs, type_embed, gain_one, weight_mix, weight_out, gain_two, weight_up, weight_down):
        start_h = inputs + jnp.einsum('cnpk,kd->cnpd', onehot, type_embed, precision=precise)
        normed = low(norm_rows(start_h, gain_one))
        mixed_rows = low_back(jnp.einsum('cnpd,de->cnpe', normed, weight_mix, precision=precise))
        flat_mix = mixed_rows.reshape(2, seq_len, 3 * D)
        positions = jnp.arange(seq_len)
        query_rows = low(rotate(flat_mix[..., :D], positions, 1.0))
        key_rows = low(rotate(flat_mix[..., D:2 * D], positions, 1.0))
        value_rows = low(flat_mix[..., 2 * D:])
        attended = jnp.stack([clip_attention(query_rows[clip_index], key_rows[clip_index], value_rows[clip_index], real_clip[clip_index]) for clip_index in range(2)])
        attended = low_back(low(attended))
        branch = low_back(jnp.einsum('cld,de->cle', attended, weight_out, precision=precise))
        middle = start_h + branch.reshape(2, N_TM, FRAME, D)
        normed_two = low(norm_rows(middle, gain_two))
        upper_in = low_back(jnp.einsum('cnpd,df->cnpf', normed_two, weight_up, precision=precise))
        activated = low(jax.nn.gelu(upper_in))
        return middle + low_back(jnp.einsum('cnpf,fd->cnpd', activated, weight_down, precision=precise))
    primals = (to_clips(tokens.astype(jnp.float32)), type_table.astype(jnp.float32), norm_gain, qkv_weight.astype(jnp.float32), out_weight.astype(jnp.float32), mlp_gain, up_weight.astype(jnp.float32), down_weight.astype(jnp.float32))
    final_rows, pullback = jax.vjp(forward, *primals)
    gradients = pullback(to_clips(cotangent.astype(jnp.float32)))
    return (from_clips(final_rows).astype(jnp.bfloat16), from_clips(gradients[0]), gradients[1], gradients[2], gradients[3], gradients[4], gradients[5], gradients[6], gradients[7])
```

```python
import functools

import jax
import jax.numpy as jnp
import numpy as np
from jax import lax
from jax.experimental import pallas as pl
from jax.experimental.pallas import tpu as pltpu
from jax.sharding import Mesh
from jax.sharding import PartitionSpec as P

HEADS = 8
HEAD_DIM = 64
TYPES = 3
TILE = 256
FRAMES = 16
ROWS = 64
LOCAL = FRAMES * ROWS
GROUPS = LOCAL // TILE
MASKED = -1e30
EPS = 1e-05
BASE = 10000.0
BF = jnp.bfloat16
F32 = jnp.float32
CHIPS = ("y", "x")


def mm(a, b):
    return jnp.dot(a, b, preferred_element_type=F32)


def mm_t(a, b):
    return lax.dot_general(a, b, (((0,), (0,)), ((), ())), preferred_element_type=F32)


def write_biases(bias_ref, key_block, row_block, parity, full):
    shape = (2 * TILE, TILE)
    key = lax.broadcasted_iota(jnp.int32, shape, 0)
    query = lax.broadcasted_iota(jnp.int32, shape, 1)
    other = key >= TILE
    key_frame = jnp.where(other, key - TILE, key) // ROWS
    query_frame = query // ROWS
    before = key_frame < query_frame + jnp.where(other, parity, 0)
    row_shift = jnp.where(key_block == row_block, 0, jnp.where(key_block < row_block, ROWS, -ROWS))
    own_rows = (key % ROWS) <= (query % ROWS) + row_shift
    own = jnp.logical_not(other) & (key_frame == query_frame) & own_rows
    late = jnp.where(full, 0.0, MASKED)
    bias_ref[0] = jnp.where(before | own, 0.0, MASKED)
    bias_ref[1] = jnp.where(own, 0.0, jnp.where(before, late, MASKED))


def unfold_pair(first, second):
    return jnp.concatenate([first[:, :HEAD_DIM], first[:, HEAD_DIM:], second[:, :HEAD_DIM], second[:, HEAD_DIM:]], axis=0)


def forward_kernel(stage, where_ref, *refs):
    first, last = stage == 0, stage == 2
    refs = list(refs)
    take = lambda count: [refs.pop(0) for _ in range(count)]
    got_ref, same_ref, other_ref = take(3)
    in_acc, in_top = (None, None) if first else take(2)
    outs = take(3) if last else take(2)
    acc_ref, top_ref = take(2) if last else outs
    qt_ref, bias_ref = take(2)
    full = where_ref[0] > 0
    row_block = where_ref[1]
    parity = where_ref[2]
    if first:
        top_ref[...] = jnp.full(top_ref.shape, MASKED, F32)
        acc_ref[...] = jnp.zeros(acc_ref.shape, F32)
    else:
        top_ref[...] = in_top[...]
        acc_ref[...] = in_acc[...]
    write_queries(got_ref, qt_ref)
    low_rows = lax.broadcasted_iota(jnp.int32, (128, 2 * TILE), 0) < HEAD_DIM
    for index in range(same_ref.shape[0]):
        key_block = lax.rem(row_block + (index if first else where_ref[3 + index]), 4)
        write_biases(bias_ref, key_block, row_block, parity, full)
        for kb in range(GROUPS):
            rows = pl.ds(kb * TILE, TILE)
            keys = jnp.concatenate([same_ref[index, rows, :], other_ref[index, rows, :]], axis=0)
            values = jnp.where(low_rows, jnp.ones((), BF), keys.T)

            def tile(group, bias):
                cols = pl.ds(group * TILE, TILE)
                scores = mm(keys, qt_ref[:, cols])
                if bias is not None:
                    scores = scores + bias_ref[bias]
                top_old = top_ref[:, cols]
                top_new = jnp.maximum(top_old, jnp.max(scores, axis=0, keepdims=True))
                weights = jnp.exp(scores - top_new).astype(BF)
                acc_ref[:, cols] = acc_ref[:, cols] * jnp.exp(top_old - top_new) + mm(values, weights)
                top_ref[:, cols] = top_new

            tile(kb, 0 if kb == 0 else 1)
            if kb + 1 < GROUPS:

                def later():
                    for group in range(kb + 1, GROUPS):
                        tile(group, None)

                if kb == 0:
                    later()
                else:
                    pl.when(full)(later)
    if last:
        packed_ref, ot_ref, lse_ref = outs
        total = acc_ref[0:1, :]
        out_t = acc_ref[HEAD_DIM:, :] / total
        ot_ref[...] = out_t
        lse_ref[...] = top_ref[...] + jnp.log(total)
        for frame in range(FRAMES):
            part = out_t[:, frame * ROWS : (frame + 1) * ROWS].T.astype(BF)
            packed_ref[frame] = jnp.concatenate([part[: ROWS // 2], part[ROWS // 2 :]], axis=1)


def write_queries(got_ref, qt_ref):
    for pair in range(FRAMES // 2):
        rows = unfold_pair(got_ref[2 * pair, ROWS : ROWS + ROWS // 2, :], got_ref[2 * pair + 1, ROWS : ROWS + ROWS // 2, :])
        qt_ref[:HEAD_DIM, pair * 128 : (pair + 1) * 128] = rows.T
    qt_ref[HEAD_DIM:, :] = jnp.zeros((HEAD_DIM, LOCAL), BF)


def backward_kernel(
    where_ref, got_ref, grad_ref, ot_ref, lse_ref, near_ref, nearo_ref, mid_ref, mido_ref, far_ref, faro_ref,
    dsame_ref, dother_ref, dq_ref,
    qt_ref, q_ref, dot_ref, do_ref, dqt_ref, delta_ref, keep_ref, bias_ref,
):
    full = where_ref[0] > 0
    row_block = where_ref[1]
    parity = where_ref[2]
    write_queries(got_ref, qt_ref)
    blank = jnp.zeros((2 * ROWS, HEAD_DIM), BF)
    for pair in range(FRAMES // 2):
        span = pl.ds(pair * 128, 128)
        query = unfold_pair(got_ref[2 * pair, ROWS : ROWS + ROWS // 2, :], got_ref[2 * pair + 1, ROWS : ROWS + ROWS // 2, :])
        grad = unfold_pair(grad_ref[2 * pair], grad_ref[2 * pair + 1])
        q_ref[span, :] = jnp.concatenate([query, blank], axis=1)
        do_ref[span, :] = jnp.concatenate([blank, grad], axis=1)
        dot_ref[HEAD_DIM:, pair * 128 : (pair + 1) * 128] = grad.T
    dot_ref[:HEAD_DIM, :] = jnp.zeros((HEAD_DIM, LOCAL), BF)
    delta_ref[...] = jnp.sum(dot_ref[HEAD_DIM:, :].astype(F32) * ot_ref[...], axis=0, keepdims=True)
    dqt_ref[...] = jnp.zeros(dqt_ref.shape, F32)
    places = ((near_ref, nearo_ref, 0, 0), (mid_ref, mido_ref, 0, 1), (mid_ref, mido_ref, 1, 3), (far_ref, faro_ref, 0, 2))
    for same_ref, other_ref, index, offset in places:
        key_block = lax.rem(row_block + offset, 4)
        write_biases(bias_ref, key_block, row_block, parity, full)
        for kb in range(GROUPS):
            rows = pl.ds(kb * TILE, TILE)
            keys = jnp.concatenate([same_ref[index, rows, :], other_ref[index, rows, :]], axis=0)
            keys_t = keys[:, :HEAD_DIM].T

            def tile(group, bias):
                cols = pl.ds(group * TILE, TILE)
                scores = mm(keys, qt_ref[:, cols])
                if bias is not None:
                    scores = scores + bias_ref[bias]
                weights = jnp.exp(scores - lse_ref[:, cols])
                slopes = (weights * (mm(keys, dot_ref[:, cols]) - delta_ref[:, cols])).astype(BF)
                dqt_ref[:, cols] += mm(keys_t, slopes)
                return mm(slopes, q_ref[cols, :]) + mm(weights.astype(BF), do_ref[cols, :])

            keep_ref[...] = tile(kb, 0 if kb == 0 else 1)
            if kb + 1 < GROUPS:

                def later():
                    for group in range(kb + 1, GROUPS):
                        keep_ref[...] += tile(group, None)

                if kb == 0:
                    later()
                else:
                    pl.when(full)(later)
            dsame_ref[key_block, rows, :] = keep_ref[:TILE, :].astype(BF)
            dother_ref[key_block, rows, :] = keep_ref[TILE:, :].astype(BF)
    for frame in range(FRAMES):
        part = (dqt_ref[:, frame * ROWS : (frame + 1) * ROWS].T * HEAD_DIM**-0.5).astype(BF)
        dq_ref[frame] = jnp.concatenate([part[: ROWS // 2], part[ROWS // 2 :]], axis=1)


def norm_parts(hidden):
    centre = jnp.mean(hidden, axis=-1, keepdims=True)
    shifted = hidden - centre
    spread = jnp.mean(shifted * shifted, axis=-1, keepdims=True)
    inverse = lax.rsqrt(spread + EPS)
    return shifted * inverse, inverse


def norm_back(raised, unit, inverse):
    mean = jnp.mean(raised, axis=-1, keepdims=True)
    along = jnp.mean(raised * unit, axis=-1, keepdims=True)
    return (raised - mean - unit * along) * inverse


def turns(where_ref, base_ref, row_ref):
    base = base_ref[pl.ds(where_ref[1], 1), :]
    cos_base, sin_base = base[:, :128], base[:, 128:]
    cos_row, sin_row = row_ref[:, :128], row_ref[:, 128:]
    cosine = cos_base * cos_row - sin_base * sin_row
    sine = sin_base * cos_row + cos_base * sin_row
    first = lax.broadcasted_iota(jnp.int32, sine.shape, 1) % HEAD_DIM < HEAD_DIM // 2
    return cosine, jnp.where(first, -sine, sine)


def turn(pair, cosine, sine):
    half = HEAD_DIM // 2
    first = lax.broadcasted_iota(jnp.int32, pair.shape, 1) % HEAD_DIM < half
    crossed = jnp.where(first, pltpu.roll(pair, 128 - half, 1), pltpu.roll(pair, half, 1))
    return pair * cosine + crossed * sine


def pre_kernel(where_ref, mask_ref, tok_ref, type_ref, table_ref, gain_ref, w_ref, base_ref, row_ref, sent_ref, start_ref, low_ref, mixed_ref):
    swapped = where_ref[0]
    cosine, sine = turns(where_ref, base_ref, row_ref)
    for clip in range(2):
        slot = jnp.where(swapped > 0, 1 - clip, clip)
        kinds = type_ref[pl.ds(slot, 1), :]
        onehot = (lax.broadcasted_iota(jnp.int32, (8, ROWS), 0) == kinds).astype(F32).astype(BF)
        hidden = tok_ref[slot].astype(F32) + mm_t(onehot, table_ref[...])
        unit, _ = norm_parts(hidden)
        start_ref[clip * ROWS : (clip + 1) * ROWS, :] = hidden
        low_ref[clip * ROWS : (clip + 1) * ROWS, :] = (unit * gain_ref[...]).astype(BF)
    width = 512
    for third in range(3):
        mixed_ref[:, third * width : (third + 1) * width] = mm(low_ref[...], w_ref[:, third * width : (third + 1) * width])
    for clip in range(2):
        slot = jnp.where(swapped > 0, 1 - clip, clip)
        rows = slice(clip * ROWS, (clip + 1) * ROWS)
        real = jnp.full((16, 128), mask_ref[slot], jnp.int32).astype(F32).astype(BF)
        for pair in range(HEADS // 2):
            query = (turn(mixed_ref[rows, pair * 128 : (pair + 1) * 128], cosine, sine).astype(BF) * HEAD_DIM**-0.5).astype(BF)
            key = turn(mixed_ref[rows, width + pair * 128 : width + (pair + 1) * 128], cosine, sine).astype(BF)
            value = mixed_ref[rows, 2 * width + pair * 128 : 2 * width + (pair + 1) * 128].astype(BF)
            for side in range(2):
                to = (2 * pair + side) * 2 + clip
                lanes = slice(side * HEAD_DIM, (side + 1) * HEAD_DIM)
                sent_ref[to, :ROWS, :] = jnp.concatenate([key[:, lanes], value[:, lanes]], axis=1)
                sent_ref[to, ROWS : ROWS + ROWS // 2, :] = jnp.concatenate([query[: ROWS // 2, lanes], query[ROWS // 2 :, lanes]], axis=1)
                sent_ref[to, ROWS + ROWS // 2 :, :] = real


def mm_nt(a, b):
    return lax.dot_general(a, b, (((1,), (1,)), ((), ())), preferred_element_type=F32)


FF_PART = 512
GELU_SCALE = float(np.sqrt(2.0 / np.pi))
GELU_CUBE = 0.044715
G_AT, DU_AT, N2_AT, DY_AT, AT_AT, DA_AT, ACT_WIDTH = 0, 1024, 2048, 2560, 3072, 3328, 3840


def mlp_kernel(
    where_ref, got_ref, start_ref, cot_ref, gain_ref, wo_ref, wu_ref, wd_ref, out_ref, packed_ref, mid_ref, gaing_ref, acts_ref,
    attn_ref, slope_ref,
):
    swapped, core = where_ref[0], where_ref[2]
    keep, send = 0, 1
    for clip in range(2):
        for pair in range(HEADS // 2):
            one, two = got_ref[4 * pair + clip], got_ref[4 * pair + 2 + clip]
            attn_ref[clip * ROWS : clip * ROWS + ROWS // 2, pair * 128 : (pair + 1) * 128] = jnp.concatenate([one[:, :HEAD_DIM], two[:, :HEAD_DIM]], axis=1)
            attn_ref[clip * ROWS + ROWS // 2 : (clip + 1) * ROWS, pair * 128 : (pair + 1) * 128] = jnp.concatenate([one[:, HEAD_DIM:], two[:, HEAD_DIM:]], axis=1)
    slots = [jnp.where(swapped > 0, 1 - clip, clip) for clip in range(2)]
    grad_low = jnp.concatenate([cot_ref[slots[0]], cot_ref[slots[1]]], axis=0)
    attn = attn_ref[...]
    middle = start_ref[...] + mm(attn, wo_ref[...])
    unit, inverse = norm_parts(middle)
    low = (unit * gain_ref[...]).astype(BF)
    final = middle
    for part in range(4):
        cols = slice(part * FF_PART, (part + 1) * FF_PART)
        upper = mm(low, wu_ref[:, cols])
        square = upper * upper
        bend = jnp.tanh(GELU_SCALE * (upper + GELU_CUBE * (square * upper)))
        act = (0.5 * upper * (1.0 + bend)).astype(BF)
        rise = 0.5 * (1.0 + bend) + 0.5 * upper * (1.0 - bend * bend) * (GELU_SCALE * (1.0 + 3.0 * GELU_CUBE * square))
        final = final + mm(act, wd_ref[cols, :])
        slope = (mm_nt(grad_low, wd_ref[cols, :]) * rise).astype(BF)
        slope_ref[:, cols] = slope
        side = jnp.where(core == part // 2, keep, send)
        at = (part % 2) * FF_PART
        acts_ref[side, :, G_AT + at : G_AT + at + FF_PART] = act
        acts_ref[side, :, DU_AT + at : DU_AT + at + FF_PART] = slope
    for clip in range(2):
        out_ref[slots[clip]] = final[clip * ROWS : (clip + 1) * ROWS].astype(BF)
    down = mm_nt(slope_ref[...], wu_ref[...])
    gaing_ref[...] = jnp.sum(down * unit, axis=0, keepdims=True)
    grad_mid = grad_low.astype(F32) + norm_back(down * gain_ref[...], unit, inverse)
    mid_ref[...] = grad_mid
    grad_mid_low = grad_mid.astype(BF)
    grad_attn = mm_nt(grad_mid_low, wo_ref[...]).astype(BF)
    for side in (keep, send):
        acts_ref[side, :, N2_AT : N2_AT + 512] = low
        acts_ref[side, :, DY_AT : DY_AT + 512] = grad_low
        acts_ref[side, :, DA_AT : DA_AT + 512] = grad_mid_low
    for half in range(2):
        acts_ref[jnp.where(core == half, keep, send), :, AT_AT : AT_AT + 256] = attn[:, half * 256 : (half + 1) * 256]
    for clip in range(2):
        for pair in range(HEADS // 2):
            rows = grad_attn[clip * ROWS : (clip + 1) * ROWS, pair * 128 : (pair + 1) * 128]
            upper_rows, lower_rows = rows[: ROWS // 2], rows[ROWS // 2 :]
            packed_ref[4 * pair + clip] = jnp.concatenate([upper_rows[:, :HEAD_DIM], lower_rows[:, :HEAD_DIM]], axis=1)
            packed_ref[4 * pair + 2 + clip] = jnp.concatenate([upper_rows[:, HEAD_DIM:], lower_rows[:, HEAD_DIM:]], axis=1)


def weight_kernel(acts_ref, theirs_ref, down_ref, up_ref, out_ref):
    def both(at, width):
        return jnp.concatenate([acts_ref[0, :, at : at + width], theirs_ref[:, at : at + width]], axis=0)

    grad_low, low, grad_mid = both(DY_AT, 512), both(N2_AT, 512), both(DA_AT, 512)
    for part in range(4):
        down_ref[part * 256 : (part + 1) * 256, :] = mm_t(both(G_AT + part * 256, 256), grad_low).astype(BF)
        up_ref[:, part * 256 : (part + 1) * 256] = mm_t(low, both(DU_AT + part * 256, 256)).astype(BF)
    out_ref[...] = mm_t(both(AT_AT, 256), grad_mid).astype(BF)


QKV_HALF = 768


def post_kernel(
    where_ref, back_ref, start_ref, mid_ref, low_ref, type_ref, mlp_ref, gain_ref, w_ref, base_ref, row_ref, grad_ref, acts_ref, raw_ref
):
    swapped, core = where_ref[0], where_ref[2]
    cosine, sine = turns(where_ref, base_ref, row_ref)
    half = ROWS // 2

    def unpack(one, two):
        upper_rows = jnp.concatenate([one[:, :HEAD_DIM], two[:, :HEAD_DIM]], axis=1)
        lower_rows = jnp.concatenate([one[:, HEAD_DIM:], two[:, HEAD_DIM:]], axis=1)
        return jnp.concatenate([upper_rows, lower_rows], axis=0)

    for clip in range(2):
        rows = slice(clip * ROWS, (clip + 1) * ROWS)
        for pair in range(HEADS // 2):
            one, two = 4 * pair + clip, 4 * pair + 2 + clip
            query = unpack(back_ref[one, ROWS : ROWS + half, :], back_ref[two, ROWS : ROWS + half, :]).astype(F32)
            first, second = back_ref[one, :ROWS, :], back_ref[two, :ROWS, :]
            key = jnp.concatenate([first[:, :HEAD_DIM], second[:, :HEAD_DIM]], axis=1).astype(F32)
            cols = pair * 128
            raw_ref[rows, cols : cols + 128] = turn(query, cosine, -sine).astype(BF)
            raw_ref[rows, 512 + cols : 512 + cols + 128] = turn(key, cosine, -sine).astype(BF)
            raw_ref[rows, 1024 + cols : 1024 + cols + 128] = jnp.concatenate([first[:, HEAD_DIM:], second[:, HEAD_DIM:]], axis=1)
    raw = raw_ref[...]
    down = mm_nt(raw, w_ref[...])
    unit, inverse = norm_parts(start_ref[...])
    grad = mid_ref[...] + norm_back(down * gain_ref[...], unit, inverse)
    gain_grad = jnp.sum(down * unit, axis=0, keepdims=True)
    slots = [jnp.where(swapped > 0, 1 - clip, clip) for clip in range(2)]
    table = jnp.zeros((8, 512), F32)
    for clip in range(2):
        part = grad[clip * ROWS : (clip + 1) * ROWS]
        grad_ref[slots[clip]] = part
        kinds = type_ref[pl.ds(slots[clip], 1), :]
        onehot = (lax.broadcasted_iota(jnp.int32, (8, ROWS), 0) == kinds).astype(F32)
        table = table + jnp.dot(onehot, part, precision=lax.Precision.HIGHEST, preferred_element_type=F32)
    row = lax.broadcasted_iota(jnp.int32, (16, 512), 0)
    small = jnp.concatenate([table, jnp.zeros((8, 512), F32)], axis=0)
    small = jnp.where(row == 3, gain_grad, jnp.where(row == 4, mlp_ref[...], small)).astype(BF)
    for side in range(2):
        acts_ref[side, :128, :512] = low_ref[...]
        acts_ref[side, 128:, :512] = small
        acts_ref[side, 128:, 512:] = jnp.zeros((16, QKV_HALF), BF)
    for part in range(2):
        side = jnp.where(core == part, 0, 1)
        acts_ref[side, :128, 512:] = raw[:, part * QKV_HALF : (part + 1) * QKV_HALF]


def mix_weight_kernel(acts_ref, theirs_ref, pieces_ref):
    low = jnp.concatenate([acts_ref[0, :128, :512], theirs_ref[:128, :512]], axis=0)
    raw = jnp.concatenate([acts_ref[0, :128, 512:], theirs_ref[:128, 512:]], axis=0)
    small = acts_ref[0, 128:, :512].astype(F32) + theirs_ref[128:, :512].astype(F32)
    for place in range(64):
        pieces_ref[place, :, 384:] = jnp.zeros((16, 128), BF)
    for side in range(2):
        grad = mm_t(low, raw[:, side * 384 : (side + 1) * 384]).astype(BF)
        for strip in range(32):
            pieces_ref[2 * strip + side, :, :384] = grad[strip * 16 : (strip + 1) * 16]
    for row in range(5):
        for part in range(4):
            value = jnp.broadcast_to(small[row : row + 1, part * 128 : (part + 1) * 128], (16, 128))
            pieces_ref[4 * row + part, :, 384:] = value.astype(BF)


VMEM_SPEC = pl.BlockSpec(memory_space=pltpu.VMEM)
SMEM_SPEC = pl.BlockSpec(memory_space=pltpu.SMEM)


def call(kernel, name, outs, args, scalars=1, scratch=(), megabytes=40, flops=10**9, nbytes=4 * 2**20, exps=0):
    shapes = tuple(jax.ShapeDtypeStruct(shape, dtype) for shape, dtype in outs)
    return pl.pallas_call(
        kernel,
        out_shape=shapes,
        in_specs=[SMEM_SPEC] * scalars + [VMEM_SPEC] * (len(args) - scalars),
        out_specs=(VMEM_SPEC,) * len(shapes),
        scratch_shapes=[pltpu.VMEM(shape, dtype) for shape, dtype in scratch],
        compiler_params=pltpu.CompilerParams(vmem_limit_bytes=megabytes * 2**20),
        cost_estimate=pl.CostEstimate(flops=flops, bytes_accessed=nbytes, transcendentals=exps),
        name=name,
    )(*args)


BIAS = ((2, 2 * TILE, TILE), F32)
WIDE = ((128, LOCAL), F32)
LINE = ((1, LOCAL), F32)


def attend(stage, where, got, same, other, state=()):
    outs = (((FRAMES, ROWS // 2, 128), BF), ((HEAD_DIM, LOCAL), F32), LINE) if stage == 2 else (WIDE, LINE)
    scratch = ((WIDE, LINE) if stage == 2 else ()) + (((128, LOCAL), BF), BIAS)
    return call(
        functools.partial(forward_kernel, stage), "attend_%d" % stage, outs, (where, got, same, other) + tuple(state),
        scratch=scratch, flops=10**9 * same.shape[0], exps=10**6 * same.shape[0],
    )


def attend_back(where, got, grad, ot, lse, chunks):
    parts = [array for pair in chunks for array in pair]
    outs = (((4, LOCAL, 128), BF), ((4, LOCAL, 128), BF), ((FRAMES, ROWS // 2, 128), BF))
    scratch = (((128, LOCAL), BF), ((LOCAL, 128), BF)) * 2 + (((HEAD_DIM, LOCAL), F32), LINE, ((2 * TILE, 128), F32), BIAS)
    return call(
        backward_kernel, "attend_back", outs, (where, got, grad, ot, lse) + tuple(parts),
        scratch=scratch, megabytes=48, flops=6 * 10**9, nbytes=8 * 2**20, exps=5 * 10**6,
    )


def swap(array, axes):
    return lax.all_to_all(array, axes, 0, 0, tiled=True)


def copies(array, axes, count):
    return swap(jnp.broadcast_to(array[None], (count,) + array.shape), axes)


def partner(array):
    return lax.ppermute(array, "c", [(0, 1), (1, 0)])


def along(array, step):
    return lax.ppermute(array, "z", [(place, (place - step) % 4) for place in range(4)])


def angle_tables():
    rates = BASE ** (-np.arange(HEAD_DIM // 2, dtype=np.float64) / (HEAD_DIM // 2))
    rates = np.tile(rates, 4)
    tables = []
    for places in (np.arange(128) * ROWS, np.arange(ROWS)):
        angles = places[:, None] * rates[None, :]
        tables.append(np.concatenate([np.cos(angles), np.sin(angles)], axis=1).astype(np.float32))
    return tables


def local(
    tokens, type_ids, clip_ids, frame_mask, type_table, norm_gain, qkv_weight, out_weight, mlp_gain, up_weight, down_weight, cotangent
):
    core, block = lax.axis_index("c"), lax.axis_index("z")
    frame_now = lax.axis_index(("y", "x", "c"))
    base_table, row_table = (jnp.asarray(table) for table in angle_tables())
    own_place = jnp.stack([(clip_ids[0] != 0).astype(jnp.int32), frame_now * 4 + block, core])
    table = jnp.pad(type_table, ((0, 8 - TYPES), (0, 0)))
    gain_one, gain_two = norm_gain[None], mlp_gain[None]
    tokens_here = 2 * ROWS
    sent, start, low = call(
        pre_kernel, "pre", (((2 * HEADS, 112, 128), BF), ((tokens_here, 512), F32), ((tokens_here, 512), BF)),
        (own_place, frame_mask, tokens, type_ids, table, gain_one, qkv_weight, base_table, row_table),
        scalars=2, scratch=(((tokens_here, 1536), F32),),
    )

    got = swap(sent, CHIPS)
    own = got[:, :ROWS].reshape(LOCAL, 128)
    full = got[FRAMES - 1, ROWS + ROWS // 2, 0] > 0.5
    where = jnp.stack([full.astype(jnp.int32), block, core, jnp.int32(1), jnp.int32(3)])
    where_far = jnp.stack([full.astype(jnp.int32), block, core, jnp.int32(2), jnp.int32(2)])
    near = (own[None], partner(own)[None])
    mid_same = jnp.stack([along(own, 1), along(own, 3)])
    far_same = along(own, 2)[None]
    state = attend(0, where, got, *near)
    mid_same, far_same, state = lax.optimization_barrier((mid_same, far_same, state))
    mid = (mid_same, partner(mid_same))
    far = (far_same, partner(far_same))
    state = attend(1, where, got, *mid, state)
    packed, out_t, lse = attend(2, where_far, got, *far, state)

    heads_out = swap(packed, CHIPS)
    output, grad_packed, grad_mid, mlp_part, acts = call(
        mlp_kernel, "mlp",
        (((2, ROWS, 512), BF), ((2 * HEADS, ROWS // 2, 128), BF), ((tokens_here, 512), F32), ((1, 512), F32), ((2, tokens_here, ACT_WIDTH), BF)),
        (own_place, heads_out, start, cotangent, gain_two, out_weight, up_weight, down_weight),
        scratch=(((tokens_here, 512), BF), ((tokens_here, 2048), BF)), flops=3 * 10**9, nbytes=8 * 2**20, exps=300000,
    )
    theirs = partner(acts[1])
    halves = call(
        weight_kernel, "weights", (((1024, 512), BF), ((512, 1024), BF), ((256, 512), BF)), (acts, theirs), scalars=0,
    )
    halves, grad_packed = lax.optimization_barrier((halves, grad_packed))
    halves = lax.psum(halves, ("y", "x", "z"))

    def attention_back(grad_packed):
        grad_out = swap(grad_packed, CHIPS)
        dsame, dother, dq = attend_back(where, got, grad_out, out_t, lse, (near, mid, far))
        summed = (dsame.astype(F32) + partner(dother).astype(F32)).astype(BF)
        own_grad = jnp.sum(swap(summed, "z").astype(F32), axis=0).astype(BF)
        back = swap(jnp.concatenate([own_grad.reshape(FRAMES, ROWS, 128), dq], axis=1), CHIPS)
        input_grad, mix_acts = call(
            post_kernel, "post", (((2, ROWS, 512), F32), ((2, tokens_here + 16, 512 + QKV_HALF), BF)),
            (own_place, back, start, grad_mid, low, type_ids, mlp_part, gain_one, qkv_weight, base_table, row_table),
            scratch=(((tokens_here, 1536), BF),),
        )
        (pieces,) = call(mix_weight_kernel, "mix_weights", (((64, 16, 512), BF),), (mix_acts, partner(mix_acts[1])), scalars=0)
        mine = jnp.sum(swap(pieces, ("y", "x", "z")).astype(F32), axis=0).astype(BF)
        return input_grad, copies(mine, ("y", "x", "z"), 64)

    def nothing(grad_packed):
        return jnp.zeros((2, ROWS, 512), F32), jnp.zeros((64, 16, 512), BF)

    one_of_each = clip_ids[0] + clip_ids[1] == 1
    input_grad, gathered = lax.cond(one_of_each, attention_back, nothing, grad_packed)
    gathered, halves = lax.optimization_barrier((gathered, halves))
    small = gathered[:20, 0, 384:].astype(F32).reshape(5, 512)

    def halves_of(array, axis):
        theirs_now = partner(array)
        first = jnp.where(core == 0, array, theirs_now)
        second = jnp.where(core == 0, theirs_now, array)
        return jnp.concatenate([first, second], axis=axis).astype(F32)

    strips = jnp.transpose(gathered[:, :, :384].reshape(32, 2, 16, 384), (0, 2, 1, 3)).reshape(512, QKV_HALF)
    qkv_sum = halves_of(strips, 1)
    down_sum, up_sum, out_sum = halves_of(halves[0], 0), halves_of(halves[1], 1), halves_of(halves[2], 0)
    return (output, input_grad, small[:3], small[3], qkv_sum, out_sum, small[4], up_sum, down_sum)


def solution(mesh):
    chips = Mesh(mesh.devices.reshape(4, 4, 2, 4), ("y", "x", "c", "z"))
    tm = ("y", "x", "c")
    rows = P(tm, "z", None)
    in_specs = (rows, P(tm, "z"), P(tm), P(tm)) + (P(),) * 7 + (rows,)
    out_specs = (rows, rows) + (P(),) * 7
    return jax.shard_map(local, mesh=chips, in_specs=in_specs, out_specs=out_specs, check_vma=False)
```

```python
import functools

import jax
import jax.numpy as jnp
import numpy as np
from jax import lax
from jax.experimental import pallas as pl
from jax.experimental.pallas import tpu as pltpu
from jax.sharding import Mesh
from jax.sharding import PartitionSpec as P

HEADS = 8
HEAD_DIM = 64
TYPES = 3
TILE = 256
FRAMES = 16
ROWS = 64
LOCAL = FRAMES * ROWS
GROUPS = LOCAL // TILE
MASKED = -1e30
EPS = 1e-05
BASE = 10000.0
BF = jnp.bfloat16
F32 = jnp.float32
CHIPS = ("y", "x")


def mm(a, b):
    return jnp.dot(a, b, preferred_element_type=F32)


def mm_t(a, b):
    return lax.dot_general(a, b, (((0,), (0,)), ((), ())), preferred_element_type=F32)


def write_biases(bias_ref, at, is_other, key_block, row_block, parity, full):
    key = lax.broadcasted_iota(jnp.int32, (TILE, TILE), 0)
    query = lax.broadcasted_iota(jnp.int32, (TILE, TILE), 1)
    late = jnp.where(full, 0.0, MASKED)
    if is_other:
        before = key // ROWS < query // ROWS + parity
        bias_ref[0, at : at + TILE, :] = jnp.where(before, 0.0, MASKED)
        bias_ref[1, at : at + TILE, :] = jnp.where(before, late, MASKED)
        return
    before = key // ROWS < query // ROWS
    row_shift = jnp.where(key_block == row_block, 0, jnp.where(key_block < row_block, ROWS, -ROWS))
    own = (key // ROWS == query // ROWS) & ((key % ROWS) <= (query % ROWS) + row_shift)
    bias_ref[0, at : at + TILE, :] = jnp.where(before | own, 0.0, MASKED)
    bias_ref[1, at : at + TILE, :] = jnp.where(own, 0.0, jnp.where(before, late, MASKED))


def key_tiles(arrays, kb):
    return jnp.concatenate([array[pl.ds(kb * TILE, TILE), :] for array in arrays], axis=0)


def biased(scores, bias_ref, kb):
    bias = bias_ref[0 if kb == 0 else 1]
    if scores.shape[1] == TILE:
        return scores + bias
    return jnp.concatenate([scores[:, :TILE] + bias, scores[:, TILE:]], axis=1)


def strips(full, tile):
    @pl.when(full)
    def _():
        for kb in range(GROUPS):
            tile(kb, LOCAL - kb * TILE)

    @pl.when(jnp.logical_not(full))
    def _():
        for kb in range(GROUPS):
            tile(kb, TILE if kb else LOCAL)


def unfold_pair(first, second):
    return jnp.concatenate([first[:, :HEAD_DIM], first[:, HEAD_DIM:], second[:, :HEAD_DIM], second[:, HEAD_DIM:]], axis=0)


def forward_kernel(blocks, first, last, got_ref, *refs):
    arrays, rest = refs[: len(blocks)], refs[len(blocks) :]
    if first:
        acc_ref, top_ref, qt_ref, bias_ref = rest
        top_ref[...] = jnp.full(top_ref.shape, MASKED, F32)
        acc_ref[...] = jnp.zeros(acc_ref.shape, F32)
        write_queries(got_ref, qt_ref)
    else:
        in_acc, in_top, qt_ref = rest[:3]
        acc_ref, top_ref, bias_ref = rest[6:] if last else rest[3:]
        top_ref[...] = in_top[...]
        acc_ref[...] = in_acc[...]
    full, row_block, parity = places(got_ref)
    for place, (is_other, offset) in enumerate(blocks):
        write_biases(bias_ref, place * TILE, is_other, lax.rem(row_block + offset, 4), row_block, parity, full)

    def tile(kb, width):
        cols = pl.ds(kb * TILE, width)
        keys = key_tiles(arrays, kb)
        flipped = keys.T
        values = jnp.where(lax.broadcasted_iota(jnp.int32, flipped.shape, 0) < HEAD_DIM, jnp.ones((), BF), flipped)
        scores = biased(mm(keys, qt_ref[:, cols]), bias_ref, kb)
        top_old = top_ref[:, cols]
        top_new = jnp.maximum(top_old, jnp.max(scores, axis=0, keepdims=True))
        weights = jnp.exp(scores - top_new).astype(BF)
        acc_ref[:, cols] = acc_ref[:, cols] * jnp.exp(top_old - top_new) + mm(values, weights)
        top_ref[:, cols] = top_new

    strips(full, tile)
    if last:
        packed_ref, ot_ref, lse_ref = rest[3:6]
        total = acc_ref[0:1, :]
        out_t = acc_ref[HEAD_DIM:, :] / total
        ot_ref[...] = out_t
        lse_ref[...] = top_ref[...] + jnp.log(total)
        pack_frames(out_t.astype(BF), packed_ref)


def places(got_ref):
    full = jnp.max(got_ref[FRAMES - 1, ROWS + ROWS // 2 :, :].astype(F32)) > 0.5
    return full, lax.axis_index("z"), lax.axis_index("c")


def pack_frames(flipped, packed_ref):
    half = ROWS // 2
    for pair in range(FRAMES // 2):
        part = flipped[:, pair * 128 : (pair + 1) * 128].T
        packed_ref[2 * pair] = jnp.concatenate([part[:half], part[half:ROWS]], axis=1)
        packed_ref[2 * pair + 1] = jnp.concatenate([part[ROWS : ROWS + half], part[ROWS + half :]], axis=1)


def write_queries(got_ref, qt_ref):
    for pair in range(FRAMES // 2):
        rows = unfold_pair(got_ref[2 * pair, ROWS : ROWS + ROWS // 2, :], got_ref[2 * pair + 1, ROWS : ROWS + ROWS // 2, :])
        qt_ref[:HEAD_DIM, pair * 128 : (pair + 1) * 128] = rows.T
    qt_ref[HEAD_DIM:, :] = jnp.zeros((HEAD_DIM, LOCAL), BF)


def backward_kernel(offsets, first, got_ref, grad_ref, ot_ref, lse_ref, *refs):
    arrays, rest = refs[: 2 * len(offsets)], refs[2 * len(offsets) :]
    if first:
        dsame_ref, dother_ref, dqt_ref, qt_ref, q_ref, dot_ref, do_ref, delta_ref, bias_ref = rest
        write_queries(got_ref, qt_ref)
        blank = jnp.zeros((2 * ROWS, HEAD_DIM), BF)
        for pair in range(FRAMES // 2):
            span = pl.ds(pair * 128, 128)
            query = unfold_pair(got_ref[2 * pair, ROWS : ROWS + ROWS // 2, :], got_ref[2 * pair + 1, ROWS : ROWS + ROWS // 2, :])
            grad = unfold_pair(grad_ref[2 * pair], grad_ref[2 * pair + 1])
            q_ref[span, :] = jnp.concatenate([query, blank], axis=1)
            do_ref[span, :] = jnp.concatenate([blank, grad], axis=1)
            dot_ref[HEAD_DIM:, pair * 128 : (pair + 1) * 128] = grad.T
        dot_ref[:HEAD_DIM, :] = jnp.zeros((HEAD_DIM, LOCAL), BF)
        delta_ref[...] = jnp.sum(dot_ref[HEAD_DIM:, :].astype(F32) * ot_ref[...], axis=0, keepdims=True)
        dqt_ref[...] = jnp.zeros(dqt_ref.shape, F32)
    else:
        in_dqt, qt_ref, q_ref, dot_ref, do_ref, delta_ref, dsame_ref, dother_ref, packed_ref, dqt_ref, bias_ref = rest
        dqt_ref[...] = in_dqt[...]
    full, row_block, parity = places(got_ref)
    for block, offset in enumerate(offsets):
        key_block = lax.rem(row_block + offset, 4)
        for is_other in range(2):
            write_biases(bias_ref, is_other * TILE, is_other, key_block, row_block, parity, full)

        def tile(kb, width):
            cols = pl.ds(kb * TILE, width)
            rows = pl.ds(kb * TILE, TILE)
            keys = key_tiles(arrays[2 * block : 2 * block + 2], kb)
            scores = biased(mm(keys, qt_ref[:, cols]), bias_ref, kb)
            weights = jnp.exp(scores - lse_ref[:, cols])
            slopes = (weights * (mm(keys, dot_ref[:, cols]) - delta_ref[:, cols])).astype(BF)
            dqt_ref[:, cols] += mm(keys[:, :HEAD_DIM].T, slopes)
            both = mm(slopes, q_ref[cols, :]) + mm(weights.astype(BF), do_ref[cols, :])
            dsame_ref[block, rows, :] = both[:TILE, :].astype(BF)
            dother_ref[block, rows, :] = both[TILE:, :].astype(BF)

        strips(full, tile)
    if not first:
        pack_frames((dqt_ref[...] * HEAD_DIM**-0.5).astype(BF), packed_ref)


def norm_parts(hidden):
    centre = jnp.mean(hidden, axis=-1, keepdims=True)
    shifted = hidden - centre
    spread = jnp.mean(shifted * shifted, axis=-1, keepdims=True)
    inverse = lax.rsqrt(spread + EPS)
    return shifted * inverse, inverse


def norm_back(raised, unit, inverse):
    mean = jnp.mean(raised, axis=-1, keepdims=True)
    along = jnp.mean(raised * unit, axis=-1, keepdims=True)
    return (raised - mean - unit * along) * inverse


def turns(base_ref, row_ref):
    place = lax.axis_index(("y", "x", "c")) * 4 + lax.axis_index("z")
    base = base_ref[pl.ds(place, 1), :]
    cos_base, sin_base = base[:, :128], base[:, 128:]
    cos_row, sin_row = row_ref[:, :128], row_ref[:, 128:]
    cosine = cos_base * cos_row - sin_base * sin_row
    sine = sin_base * cos_row + cos_base * sin_row
    first = lax.broadcasted_iota(jnp.int32, sine.shape, 1) % HEAD_DIM < HEAD_DIM // 2
    return cosine, jnp.where(first, -sine, sine)


def turn(pair, cosine, sine):
    half = HEAD_DIM // 2
    first = lax.broadcasted_iota(jnp.int32, pair.shape, 1) % HEAD_DIM < half
    crossed = jnp.where(first, pltpu.roll(pair, 128 - half, 1), pltpu.roll(pair, half, 1))
    return pair * cosine + crossed * sine


def pre_kernel(clip_ref, mask_ref, tok_ref, type_ref, table_ref, gain_ref, w_ref, base_ref, row_ref, sent_ref, start_ref, low_ref, mixed_ref, kinds_ref):
    swapped = clip_ref[0]
    cosine, sine = turns(base_ref, row_ref)
    kinds_ref[...] = jnp.zeros(kinds_ref.shape, BF)
    kinds_ref[:TYPES, :] = table_ref[...]
    for clip in range(2):
        slot = jnp.where(swapped > 0, 1 - clip, clip)
        kinds = type_ref[pl.ds(slot, 1), :]
        onehot = (lax.broadcasted_iota(jnp.int32, (16, ROWS), 0) == kinds).astype(F32).astype(BF)
        hidden = tok_ref[slot].astype(F32) + mm_t(onehot, kinds_ref[...])
        unit, _ = norm_parts(hidden)
        start_ref[clip * ROWS : (clip + 1) * ROWS, :] = hidden
        low_ref[clip * ROWS : (clip + 1) * ROWS, :] = (unit * gain_ref[...]).astype(BF)
    width = 512
    for third in range(3):
        mixed_ref[:, third * width : (third + 1) * width] = mm(low_ref[...], w_ref[:, third * width : (third + 1) * width])
    for clip in range(2):
        slot = jnp.where(swapped > 0, 1 - clip, clip)
        rows = slice(clip * ROWS, (clip + 1) * ROWS)
        real = jnp.full((16, 128), mask_ref[slot], jnp.int32).astype(F32).astype(BF)
        for pair in range(HEADS // 2):
            query = (turn(mixed_ref[rows, pair * 128 : (pair + 1) * 128], cosine, sine).astype(BF) * HEAD_DIM**-0.5).astype(BF)
            key = turn(mixed_ref[rows, width + pair * 128 : width + (pair + 1) * 128], cosine, sine).astype(BF)
            value = mixed_ref[rows, 2 * width + pair * 128 : 2 * width + (pair + 1) * 128].astype(BF)
            for side in range(2):
                to = (2 * pair + side) * 2 + clip
                lanes = slice(side * HEAD_DIM, (side + 1) * HEAD_DIM)
                sent_ref[to, :ROWS, :] = jnp.concatenate([key[:, lanes], value[:, lanes]], axis=1)
                sent_ref[to, ROWS : ROWS + ROWS // 2, :] = jnp.concatenate([query[: ROWS // 2, lanes], query[ROWS // 2 :, lanes]], axis=1)
                sent_ref[to, ROWS + ROWS // 2 :, :] = real


def mm_nt(a, b):
    return lax.dot_general(a, b, (((1,), (1,)), ((), ())), preferred_element_type=F32)


FF_PART = 512
GELU_SCALE = float(np.sqrt(2.0 / np.pi))
GELU_CUBE = 0.044715
G_AT, DU_AT, N2_AT, DY_AT, AT_AT, DA_AT, ACT_WIDTH = 0, 1024, 2048, 2560, 3072, 3328, 3840


def mlp_kernel(
    clip_ref, got_ref, start_ref, cot_ref, gain_ref, wo_ref, wu_ref, wd_ref, out_ref, packed_ref, mid_ref, gaing_ref, acts_ref,
    attn_ref, slope_ref,
):
    swapped, core = clip_ref[0], lax.axis_index("c")
    keep, send = 0, 1
    for clip in range(2):
        for pair in range(HEADS // 2):
            one, two = got_ref[4 * pair + clip], got_ref[4 * pair + 2 + clip]
            attn_ref[clip * ROWS : clip * ROWS + ROWS // 2, pair * 128 : (pair + 1) * 128] = jnp.concatenate([one[:, :HEAD_DIM], two[:, :HEAD_DIM]], axis=1)
            attn_ref[clip * ROWS + ROWS // 2 : (clip + 1) * ROWS, pair * 128 : (pair + 1) * 128] = jnp.concatenate([one[:, HEAD_DIM:], two[:, HEAD_DIM:]], axis=1)
    slots = [jnp.where(swapped > 0, 1 - clip, clip) for clip in range(2)]
    grad_low = jnp.concatenate([cot_ref[slots[0]], cot_ref[slots[1]]], axis=0)
    attn = attn_ref[...]
    middle = start_ref[...] + mm(attn, wo_ref[...])
    unit, inverse = norm_parts(middle)
    low = (unit * gain_ref[...]).astype(BF)
    final = middle
    for part in range(4):
        cols = slice(part * FF_PART, (part + 1) * FF_PART)
        upper = mm(low, wu_ref[:, cols])
        square = upper * upper
        bend = jnp.tanh(GELU_SCALE * (upper + GELU_CUBE * (square * upper)))
        act = (0.5 * upper * (1.0 + bend)).astype(BF)
        rise = 0.5 * (1.0 + bend) + 0.5 * upper * (1.0 - bend * bend) * (GELU_SCALE * (1.0 + 3.0 * GELU_CUBE * square))
        final = final + mm(act, wd_ref[cols, :])
        slope = (mm_nt(grad_low, wd_ref[cols, :]) * rise).astype(BF)
        slope_ref[:, cols] = slope
        side = jnp.where(core == part // 2, keep, send)
        at = (part % 2) * FF_PART
        acts_ref[side, :, G_AT + at : G_AT + at + FF_PART] = act
        acts_ref[side, :, DU_AT + at : DU_AT + at + FF_PART] = slope
    for clip in range(2):
        out_ref[slots[clip]] = final[clip * ROWS : (clip + 1) * ROWS].astype(BF)
    down = mm_nt(slope_ref[...], wu_ref[...])
    gaing_ref[...] = jnp.sum(down * unit, axis=0, keepdims=True)
    grad_mid = grad_low.astype(F32) + norm_back(down * gain_ref[...], unit, inverse)
    mid_ref[...] = grad_mid
    grad_mid_low = grad_mid.astype(BF)
    grad_attn = mm_nt(grad_mid_low, wo_ref[...]).astype(BF)
    for side in (keep, send):
        acts_ref[side, :, N2_AT : N2_AT + 512] = low
        acts_ref[side, :, DY_AT : DY_AT + 512] = grad_low
        acts_ref[side, :, DA_AT : DA_AT + 512] = grad_mid_low
    for half in range(2):
        acts_ref[jnp.where(core == half, keep, send), :, AT_AT : AT_AT + 256] = attn[:, half * 256 : (half + 1) * 256]
    for clip in range(2):
        for pair in range(HEADS // 2):
            rows = grad_attn[clip * ROWS : (clip + 1) * ROWS, pair * 128 : (pair + 1) * 128]
            upper_rows, lower_rows = rows[: ROWS // 2], rows[ROWS // 2 :]
            packed_ref[4 * pair + clip] = jnp.concatenate([upper_rows[:, :HEAD_DIM], lower_rows[:, :HEAD_DIM]], axis=1)
            packed_ref[4 * pair + 2 + clip] = jnp.concatenate([upper_rows[:, HEAD_DIM:], lower_rows[:, HEAD_DIM:]], axis=1)


UP_AT, OUT_AT, PIECE_ROWS = 1024, 2048, 2304


def weight_kernel(acts_ref, theirs_ref, *piece_refs):
    block = lax.axis_index("z")

    def both(at, width):
        return jnp.concatenate([acts_ref[0, :, pl.ds(at, width)], theirs_ref[:, pl.ds(at, width)]], axis=0)

    grad_low, low, attn = both(DY_AT, 512), both(N2_AT, 512), both(AT_AT, 256)
    for step, piece_ref in enumerate(piece_refs):
        piece = lax.rem(block + step, 4)
        units = pl.multiple_of(piece * 256, 256)
        down = mm_t(both(G_AT + units, 256), grad_low).astype(BF)
        for part in range(4):
            piece_ref[part * 256 : (part + 1) * 256, :] = down[:, part * 128 : (part + 1) * 128]
        up = mm_t(low, both(DU_AT + units, 256)).astype(BF)
        for part in range(2):
            piece_ref[UP_AT + part * 512 : UP_AT + (part + 1) * 512, :] = up[:, part * 128 : (part + 1) * 128]
        piece_ref[OUT_AT:, :] = mm_t(attn, both(DA_AT + pl.multiple_of(piece * 128, 128), 128)).astype(BF)


QKV_HALF = 768


def post_kernel(
    clip_ref, back_ref, start_ref, mid_ref, low_ref, type_ref, mlp_ref, gain_ref, w_ref, base_ref, row_ref, grad_ref, acts_ref, raw_ref
):
    swapped, core = clip_ref[0], lax.axis_index("c")
    cosine, sine = turns(base_ref, row_ref)
    half = ROWS // 2

    def unpack(one, two):
        upper_rows = jnp.concatenate([one[:, :HEAD_DIM], two[:, :HEAD_DIM]], axis=1)
        lower_rows = jnp.concatenate([one[:, HEAD_DIM:], two[:, HEAD_DIM:]], axis=1)
        return jnp.concatenate([upper_rows, lower_rows], axis=0)

    for clip in range(2):
        rows = slice(clip * ROWS, (clip + 1) * ROWS)
        for pair in range(HEADS // 2):
            one, two = 4 * pair + clip, 4 * pair + 2 + clip
            query = unpack(back_ref[one, ROWS : ROWS + half, :], back_ref[two, ROWS : ROWS + half, :]).astype(F32)
            first, second = back_ref[one, :ROWS, :], back_ref[two, :ROWS, :]
            key = jnp.concatenate([first[:, :HEAD_DIM], second[:, :HEAD_DIM]], axis=1).astype(F32)
            cols = pair * 128
            raw_ref[rows, cols : cols + 128] = turn(query, cosine, -sine).astype(BF)
            raw_ref[rows, 512 + cols : 512 + cols + 128] = turn(key, cosine, -sine).astype(BF)
            raw_ref[rows, 1024 + cols : 1024 + cols + 128] = jnp.concatenate([first[:, HEAD_DIM:], second[:, HEAD_DIM:]], axis=1)
    raw = raw_ref[...]
    down = mm_nt(raw, w_ref[...])
    unit, inverse = norm_parts(start_ref[...])
    grad = mid_ref[...] + norm_back(down * gain_ref[...], unit, inverse)
    gain_grad = jnp.sum(down * unit, axis=0, keepdims=True)
    slots = [jnp.where(swapped > 0, 1 - clip, clip) for clip in range(2)]
    table = jnp.zeros((8, 512), F32)
    for clip in range(2):
        part = grad[clip * ROWS : (clip + 1) * ROWS]
        grad_ref[slots[clip]] = part
        kinds = type_ref[pl.ds(slots[clip], 1), :]
        onehot = (lax.broadcasted_iota(jnp.int32, (8, ROWS), 0) == kinds).astype(F32)
        table = table + jnp.dot(onehot, part, precision=lax.Precision.HIGHEST, preferred_element_type=F32)
    row = lax.broadcasted_iota(jnp.int32, (16, 512), 0)
    small = jnp.concatenate([table, jnp.zeros((8, 512), F32)], axis=0)
    small = jnp.where(row == 3, gain_grad, jnp.where(row == 4, mlp_ref[...], small)).astype(BF)
    for side in range(2):
        acts_ref[side, :128, :512] = low_ref[...]
        acts_ref[side, 128:, :512] = small
        acts_ref[side, 128:, 512:] = jnp.zeros((16, QKV_HALF), BF)
    for part in range(2):
        side = jnp.where(core == part, 0, 1)
        acts_ref[side, :128, 512:] = raw[:, part * QKV_HALF : (part + 1) * QKV_HALF]


def mix_weight_kernel(acts_ref, theirs_ref, pieces_ref):
    low = jnp.concatenate([acts_ref[0, :128, :512], theirs_ref[:128, :512]], axis=0)
    raw = jnp.concatenate([acts_ref[0, :128, 512:], theirs_ref[:128, 512:]], axis=0)
    small = acts_ref[0, 128:, :512].astype(F32) + theirs_ref[128:, :512].astype(F32)
    for place in range(64):
        pieces_ref[place, :, 384:] = jnp.zeros((16, 128), BF)
    for side in range(2):
        grad = mm_t(low, raw[:, side * 384 : (side + 1) * 384]).astype(BF)
        for strip in range(32):
            pieces_ref[2 * strip + side, :, :384] = grad[strip * 16 : (strip + 1) * 16]
    for row in range(5):
        for part in range(4):
            value = jnp.broadcast_to(small[row : row + 1, part * 128 : (part + 1) * 128], (16, 128))
            pieces_ref[4 * row + part, :, 384:] = value.astype(BF)


def mix_sum_kernel(own_ref, theirs_ref, qkv_ref, table_ref, gain_one_ref, gain_two_ref):
    core = lax.axis_index("c")
    for half in range(2):

        def write(pieces_ref):
            for place in range(64):
                strip, side = place // 2, place % 2
                cols = half * QKV_HALF + side * 384
                qkv_ref[strip * 16 : (strip + 1) * 16, cols : cols + 384] = pieces_ref[place, :, :384].astype(F32)

        pl.when(core == half)(functools.partial(write, own_ref))
        pl.when(core != half)(functools.partial(write, theirs_ref))
    for row in range(5):
        target, line = ((table_ref, row), (table_ref, row), (table_ref, row), (gain_one_ref, 0), (gain_two_ref, 0))[row]
        for part in range(4):
            target[line : line + 1, part * 128 : (part + 1) * 128] = own_ref[4 * row + part, 0:1, 384:].astype(F32)


def spread_kernel(all_ref, down, up, out, low, down_stage, up_stage, out_stage, in_sems, out_sems):
    places_in = [(core, piece) for core in range(2) for piece in range(4)]
    reads = []
    for at, (core, piece) in enumerate(places_in):
        reads.append(pltpu.make_async_copy(all_ref.at[piece, :, core], low.at[core, piece], in_sems.at[at]))
        reads[-1].start()
    writes = []

    def write(source, target):
        writes.append(pltpu.make_async_copy(source, target, out_sems.at[len(writes)]))
        writes[-1].start()

    for at, (core, piece) in enumerate(places_in):
        reads[at].wait()
        whole = low[core, piece].reshape(PIECE_ROWS, 128).astype(F32)
        units = pl.ds(core * 1024 + piece * 256, 256)
        for part in range(4):
            down_stage[units, part * 128 : (part + 1) * 128] = whole[part * 256 : (part + 1) * 256]
        write(down_stage.at[units, :], down.at[units, :])
        for part in range(2):
            cols = pl.ds(core * 1024 + piece * 256 + part * 128, 128)
            up_stage[:, cols] = whole[UP_AT + part * 512 : UP_AT + (part + 1) * 512]
        out_stage[core * 256 : (core + 1) * 256, piece * 128 : (piece + 1) * 128] = whole[OUT_AT:]
        write(up_stage.at[:, units], up.at[:, units])
        if piece == 3:
            rows = pl.ds(core * 256, 256)
            write(out_stage.at[rows, :], out.at[rows, :])
    for copy in writes:
        copy.wait()


VMEM_SPEC = pl.BlockSpec(memory_space=pltpu.VMEM)
SMEM_SPEC = pl.BlockSpec(memory_space=pltpu.SMEM)


def call(kernel, name, outs, args, scalars=1, scratch=(), megabytes=28, flops=10**9, nbytes=4 * 2**20, exps=0):
    shapes = tuple(jax.ShapeDtypeStruct(shape, dtype) for shape, dtype in outs)
    return pl.pallas_call(
        kernel,
        out_shape=shapes,
        in_specs=[SMEM_SPEC] * scalars + [VMEM_SPEC] * (len(args) - scalars),
        out_specs=(VMEM_SPEC,) * len(shapes),
        scratch_shapes=[pltpu.VMEM(shape, dtype) for shape, dtype in scratch],
        compiler_params=pltpu.CompilerParams(vmem_limit_bytes=megabytes * 2**20),
        cost_estimate=pl.CostEstimate(flops=flops, bytes_accessed=nbytes, transcendentals=exps),
        name=name,
    )(*args)


WIDE = ((128, LOCAL), F32)
LINE = ((1, LOCAL), F32)


QUERIES = ((128, LOCAL), BF)
GRADS = ((64, LOCAL), F32)
PACKED = ((FRAMES, ROWS // 2, 128), BF)


def attend(name, got, blocks, arrays, state=(), last=False, flops=10**9):
    first = not state
    outs = (PACKED, GRADS, LINE) if last else (WIDE, LINE) + ((QUERIES,) if first else ())
    scratch = ((WIDE, LINE) if last else ()) + (((2, len(blocks) * TILE, TILE), F32),)
    return call(
        functools.partial(forward_kernel, blocks, first, last), name, outs, (got,) + tuple(arrays) + tuple(state),
        scalars=0, scratch=scratch, flops=flops, nbytes=10**5,
    )


def attend_back(name, got, grad, ot, lse, offsets, arrays, state=(), flops=10**8):
    first, blocks = not state, ((len(offsets), LOCAL, 128), BF)
    flat = ((LOCAL, 128), BF)
    outs = (blocks, blocks) + ((GRADS, QUERIES, flat, QUERIES, flat, LINE) if first else (PACKED,))
    scratch = (() if first else (GRADS,)) + (((2, 2 * TILE, TILE), F32),)
    return call(
        functools.partial(backward_kernel, offsets, first), name, outs, (got, grad, ot, lse) + tuple(arrays) + tuple(state),
        scalars=0, scratch=scratch, megabytes=28, flops=flops, nbytes=10**5,
    )


MIXED = (((512, 1536), F32), ((TYPES, 512), F32), ((1, 512), F32), ((1, 512), F32))


def spread(gathered):
    hbm = pl.BlockSpec(memory_space=pltpu.HBM)
    wholes = tuple(jax.ShapeDtypeStruct(shape, F32) for shape in ((2048, 512), (512, 2048), (512, 512)))
    return pl.pallas_call(
        spread_kernel,
        out_shape=wholes,
        in_specs=[hbm],
        out_specs=(hbm,) * 3,
        scratch_shapes=[pltpu.VMEM((2, 4, 16, PIECE_ROWS // 16, 128), BF)]
        + [pltpu.VMEM(whole.shape, F32) for whole in wholes]
        + [pltpu.SemaphoreType.DMA((8,)), pltpu.SemaphoreType.DMA((18,))],
        compiler_params=pltpu.CompilerParams(vmem_limit_bytes=60 * 2**20),
        cost_estimate=pl.CostEstimate(flops=10**7, bytes_accessed=15 * 2**20, transcendentals=0),
        name="spread",
    )(gathered)


def swap(array, axes):
    return lax.all_to_all(array, axes, 0, 0, tiled=True)


def copies(array, axes, count):
    return swap(jnp.broadcast_to(array[None], (count,) + array.shape), axes)


def partner(array):
    return lax.ppermute(array, "c", [(0, 1), (1, 0)])


def along(array, step):
    return lax.ppermute(array, "z", [(place, (place - step) % 4) for place in range(4)])


def angle_tables():
    rates = BASE ** (-np.arange(HEAD_DIM // 2, dtype=np.float64) / (HEAD_DIM // 2))
    rates = np.tile(rates, 4)
    tables = []
    for places in (np.arange(128) * ROWS, np.arange(ROWS)):
        angles = places[:, None] * rates[None, :]
        tables.append(np.concatenate([np.cos(angles), np.sin(angles)], axis=1).astype(np.float32))
    return tables


def local(
    tokens, type_ids, clip_ids, frame_mask, type_table, norm_gain, qkv_weight, out_weight, mlp_gain, up_weight, down_weight, cotangent
):
    base_table, row_table = (jnp.asarray(table) for table in angle_tables())
    gain_one, gain_two = norm_gain[None], mlp_gain[None]
    tokens_here = 2 * ROWS
    sent, start, low = call(
        pre_kernel, "pre", (((2 * HEADS, 112, 128), BF), ((tokens_here, 512), F32), ((tokens_here, 512), BF)),
        (clip_ids, frame_mask, tokens, type_ids, type_table, gain_one, qkv_weight, base_table, row_table),
        scalars=2, scratch=(((tokens_here, 1536), F32), ((16, 512), BF)), megabytes=60,
    )

    got = swap(sent, CHIPS)
    own = got[:, :ROWS].reshape(LOCAL, 128)
    own_other = partner(own)
    up, down, far = along(own, 1), along(own, 3), along(own, 2)
    *state, queries = attend("attend_near", got, ((0, 0), (1, 0)), (own, own_other), flops=2 * 10**10)
    up, *state = lax.optimization_barrier((up, *state))
    up_other = partner(up)
    state = attend("attend_up", got, ((0, 1),), (up,), (*state, queries), flops=10**8)
    down, far, *state = lax.optimization_barrier((down, far, *state))
    down_other = partner(down)
    state = attend("attend_up_down", got, ((1, 1), (0, 3)), (up_other, down), (*state, queries), flops=10**8)
    far_other = partner(far)
    state = attend("attend_down_far", got, ((1, 3), (0, 2)), (down_other, far), (*state, queries), flops=10**8)
    packed, out_t, lse = attend("attend_far", got, ((1, 2),), (far_other,), (*state, queries), last=True)

    heads_out = swap(packed, CHIPS)
    output, grad_packed, grad_mid, mlp_part, acts = call(
        mlp_kernel, "mlp",
        (((2, ROWS, 512), BF), ((2 * HEADS, ROWS // 2, 128), BF), ((tokens_here, 512), F32), ((1, 512), F32), ((2, tokens_here, ACT_WIDTH), BF)),
        (clip_ids, heads_out, start, cotangent, gain_two, out_weight, up_weight, down_weight),
        scratch=(((tokens_here, 512), BF), ((tokens_here, 2048), BF)), flops=3 * 10**9, nbytes=8 * 2**20, exps=300000,
    )
    theirs = partner(acts[1])
    pieces = call(weight_kernel, "weights", (((PIECE_ROWS, 128), BF),) * 4, (acts, theirs), scalars=0)
    pieces, grad_packed = lax.optimization_barrier((pieces, grad_packed))
    arrived = [along(piece, -step) for step, piece in enumerate(pieces) if step]
    grad_out = swap(grad_packed, CHIPS)
    dsame, dother, *back_state = attend_back(
        "attend_back_others", got, grad_out, out_t, lse, (2, 1, 3), (far, far_other, up, up_other, down, down_other)
    )
    summed = (dsame.astype(F32) + partner(dother).astype(F32)).astype(BF)
    moved = [along(summed[at], -offset) for at, offset in enumerate((2, 1, 3))]
    near_same, near_other, dq = attend_back("attend_back_near", got, grad_out, out_t, lse, (0,), (own, own_other), back_state)
    arrived, near_same, near_other = lax.optimization_barrier((arrived, near_same, near_other))
    piece = sum((part.astype(F32) for part in arrived), pieces[0].astype(F32)).astype(BF)
    piece = jnp.sum(swap(piece.reshape(16, PIECE_ROWS // 16, 128), CHIPS).astype(F32), axis=0).astype(BF)
    piece, moved = lax.optimization_barrier((piece, moved))
    gathered = lax.all_gather(piece, ("z", "y", "x", "c"), axis=0).reshape(4, 16, 2, PIECE_ROWS // 16, 128)
    near_sum = near_same[0].astype(F32) + partner(near_other[0]).astype(F32)
    own_grad = sum((part.astype(F32) for part in moved), near_sum).astype(BF)

    back = swap(jnp.concatenate([own_grad.reshape(FRAMES, ROWS, 128), dq], axis=1), CHIPS)
    input_grad, mix_acts = call(
        post_kernel, "post", (((2, ROWS, 512), F32), ((2, tokens_here + 16, 512 + QKV_HALF), BF)),
        (clip_ids, back, start, grad_mid, low, type_ids, mlp_part, gain_one, qkv_weight, base_table, row_table),
        scratch=(((tokens_here, 1536), BF),),
    )
    (pieces,) = call(mix_weight_kernel, "mix_weights", (((64, 16, 512), BF),), (mix_acts, partner(mix_acts[1])), scalars=0)
    mine = jnp.sum(swap(pieces, ("y", "x", "z")).astype(F32), axis=0).astype(BF)
    mixed, gathered = lax.optimization_barrier((copies(mine, ("y", "x", "z"), 64), gathered))
    qkv_sum, table_sum, gain_one_sum, gain_two_sum = call(mix_sum_kernel, "mix_sums", MIXED, (mixed, partner(mixed)), scalars=0)
    down_sum, up_sum, out_sum = spread(gathered)
    return (output, input_grad, table_sum, gain_one_sum[0], qkv_sum, out_sum, gain_two_sum[0], up_sum, down_sum)


def solution(mesh):
    chips = Mesh(mesh.devices.reshape(4, 4, 2, 4), ("y", "x", "c", "z"))
    tm = ("y", "x", "c")
    rows = P(tm, "z", None)
    in_specs = (rows, P(tm, "z"), P(tm), P(tm)) + (P(),) * 7 + (rows,)
    out_specs = (rows, rows) + (P(),) * 7
    return jax.shard_map(local, mesh=chips, in_specs=in_specs, out_specs=out_specs, check_vma=False)
```

```python
import functools

import jax
import jax.numpy as jnp
import numpy as np
from jax import lax
from jax.experimental import pallas as pl
from jax.experimental.pallas import tpu as pltpu
from jax.sharding import Mesh
from jax.sharding import PartitionSpec as P

HEADS = 8
HEAD_DIM = 64
TYPES = 3
TILE = 256
FRAMES = 16
ROWS = 64
LOCAL = FRAMES * ROWS
GROUPS = LOCAL // TILE
MASKED = -1e30
EPS = 1e-05
BASE = 10000.0
BF = jnp.bfloat16
F32 = jnp.float32
CHIPS = ("y", "x")


def mm(a, b):
    return jnp.dot(a, b, preferred_element_type=F32)


def mm_t(a, b):
    return lax.dot_general(a, b, (((0,), (0,)), ((), ())), preferred_element_type=F32)


def write_biases(bias_ref, at, is_other, key_block, row_block, parity, full):
    key = lax.broadcasted_iota(jnp.int32, (TILE, TILE), 0)
    query = lax.broadcasted_iota(jnp.int32, (TILE, TILE), 1)
    late = jnp.where(full, 0.0, MASKED)
    if is_other:
        before = key // ROWS < query // ROWS + parity
        bias_ref[0, at : at + TILE, :] = jnp.where(before, 0.0, MASKED)
        bias_ref[1, at : at + TILE, :] = jnp.where(before, late, MASKED)
        return
    before = key // ROWS < query // ROWS
    row_shift = jnp.where(key_block == row_block, 0, jnp.where(key_block < row_block, ROWS, -ROWS))
    own = (key // ROWS == query // ROWS) & ((key % ROWS) <= (query % ROWS) + row_shift)
    bias_ref[0, at : at + TILE, :] = jnp.where(before | own, 0.0, MASKED)
    bias_ref[1, at : at + TILE, :] = jnp.where(own, 0.0, jnp.where(before, late, MASKED))


def key_tiles(arrays, kb):
    return jnp.concatenate([array[pl.ds(kb * TILE, TILE), :] for array in arrays], axis=0)


def biased(scores, bias_ref, kb):
    bias = bias_ref[0 if kb == 0 else 1]
    if scores.shape[1] == TILE:
        return scores + bias
    return jnp.concatenate([scores[:, :TILE] + bias, scores[:, TILE:]], axis=1)


def strips(full, tile):
    @pl.when(full)
    def _():
        for kb in range(GROUPS):
            tile(kb, LOCAL - kb * TILE)

    @pl.when(jnp.logical_not(full))
    def _():
        for kb in range(GROUPS):
            tile(kb, TILE if kb else LOCAL)


def unfold_pair(first, second):
    return jnp.concatenate([first[:, :HEAD_DIM], first[:, HEAD_DIM:], second[:, :HEAD_DIM], second[:, HEAD_DIM:]], axis=0)


def forward_kernel(blocks, first, last, got_ref, *refs):
    arrays, rest = refs[: len(blocks)], refs[len(blocks) :]
    if first:
        acc_ref, top_ref, qt_ref, bias_ref = rest
        top_ref[...] = jnp.full(top_ref.shape, MASKED, F32)
        acc_ref[...] = jnp.zeros(acc_ref.shape, F32)
        write_queries(got_ref, qt_ref)
    else:
        in_acc, in_top, qt_ref = rest[:3]
        acc_ref, top_ref, bias_ref = rest[6:] if last else rest[3:]
        top_ref[...] = in_top[...]
        acc_ref[...] = in_acc[...]
    full, row_block, parity = places(got_ref)
    for place, (is_other, offset) in enumerate(blocks):
        write_biases(bias_ref, place * TILE, is_other, lax.rem(row_block + offset, 4), row_block, parity, full)

    def tile(kb, width):
        cols = pl.ds(kb * TILE, width)
        keys = key_tiles(arrays, kb)
        flipped = keys.T
        values = jnp.where(lax.broadcasted_iota(jnp.int32, flipped.shape, 0) < HEAD_DIM, jnp.ones((), BF), flipped)
        scores = biased(mm(keys, qt_ref[:, cols]), bias_ref, kb)
        top_old = top_ref[:, cols]
        top_new = jnp.maximum(top_old, jnp.max(scores, axis=0, keepdims=True))
        weights = jnp.exp(scores - top_new).astype(BF)
        acc_ref[:, cols] = acc_ref[:, cols] * jnp.exp(top_old - top_new) + mm(values, weights)
        top_ref[:, cols] = top_new

    strips(full, tile)
    if last:
        packed_ref, ot_ref, lse_ref = rest[3:6]
        total = acc_ref[0:1, :]
        out_t = acc_ref[HEAD_DIM:, :] / total
        ot_ref[...] = out_t
        lse_ref[...] = top_ref[...] + jnp.log(total)
        pack_frames(out_t.astype(BF), packed_ref)


def places(got_ref):
    full = jnp.max(got_ref[FRAMES - 1, ROWS + ROWS // 2 :, :].astype(F32)) > 0.5
    return full, lax.axis_index("z"), lax.axis_index("c")


def pack_frames(flipped, packed_ref):
    half = ROWS // 2
    for pair in range(FRAMES // 2):
        part = flipped[:, pair * 128 : (pair + 1) * 128].T
        packed_ref[2 * pair] = jnp.concatenate([part[:half], part[half:ROWS]], axis=1)
        packed_ref[2 * pair + 1] = jnp.concatenate([part[ROWS : ROWS + half], part[ROWS + half :]], axis=1)


def write_queries(got_ref, qt_ref):
    for pair in range(FRAMES // 2):
        rows = unfold_pair(got_ref[2 * pair, ROWS : ROWS + ROWS // 2, :], got_ref[2 * pair + 1, ROWS : ROWS + ROWS // 2, :])
        qt_ref[:HEAD_DIM, pair * 128 : (pair + 1) * 128] = rows.T
    qt_ref[HEAD_DIM:, :] = jnp.zeros((HEAD_DIM, LOCAL), BF)


def backward_kernel(offsets, first, got_ref, grad_ref, ot_ref, lse_ref, *refs):
    arrays, rest = refs[: 2 * len(offsets)], refs[2 * len(offsets) :]
    if first:
        dsame_ref, dother_ref, dqt_ref, qt_ref, q_ref, dot_ref, do_ref, delta_ref, bias_ref = rest
        write_queries(got_ref, qt_ref)
        blank = jnp.zeros((2 * ROWS, HEAD_DIM), BF)
        for pair in range(FRAMES // 2):
            span = pl.ds(pair * 128, 128)
            query = unfold_pair(got_ref[2 * pair, ROWS : ROWS + ROWS // 2, :], got_ref[2 * pair + 1, ROWS : ROWS + ROWS // 2, :])
            grad = unfold_pair(grad_ref[2 * pair], grad_ref[2 * pair + 1])
            q_ref[span, :] = jnp.concatenate([query, blank], axis=1)
            do_ref[span, :] = jnp.concatenate([blank, grad], axis=1)
            dot_ref[HEAD_DIM:, pair * 128 : (pair + 1) * 128] = grad.T
        dot_ref[:HEAD_DIM, :] = jnp.zeros((HEAD_DIM, LOCAL), BF)
        delta_ref[...] = jnp.sum(dot_ref[HEAD_DIM:, :].astype(F32) * ot_ref[...], axis=0, keepdims=True)
        dqt_ref[...] = jnp.zeros(dqt_ref.shape, F32)
    else:
        in_dqt, qt_ref, q_ref, dot_ref, do_ref, delta_ref, dsame_ref, dother_ref, packed_ref, dqt_ref, bias_ref = rest
        dqt_ref[...] = in_dqt[...]
    full, row_block, parity = places(got_ref)
    for block, offset in enumerate(offsets):
        key_block = lax.rem(row_block + offset, 4)
        for is_other in range(2):
            write_biases(bias_ref, is_other * TILE, is_other, key_block, row_block, parity, full)

        def tile(kb, width):
            cols = pl.ds(kb * TILE, width)
            rows = pl.ds(kb * TILE, TILE)
            keys = key_tiles(arrays[2 * block : 2 * block + 2], kb)
            scores = biased(mm(keys, qt_ref[:, cols]), bias_ref, kb)
            weights = jnp.exp(scores - lse_ref[:, cols])
            slopes = (weights * (mm(keys, dot_ref[:, cols]) - delta_ref[:, cols])).astype(BF)
            dqt_ref[:, cols] += mm(keys[:, :HEAD_DIM].T, slopes)
            both = mm(slopes, q_ref[cols, :]) + mm(weights.astype(BF), do_ref[cols, :])
            dsame_ref[block, rows, :] = both[:TILE, :].astype(BF)
            dother_ref[block, rows, :] = both[TILE:, :].astype(BF)

        strips(full, tile)
    if not first:
        pack_frames((dqt_ref[...] * HEAD_DIM**-0.5).astype(BF), packed_ref)


def norm_parts(hidden):
    centre = jnp.mean(hidden, axis=-1, keepdims=True)
    shifted = hidden - centre
    spread = jnp.mean(shifted * shifted, axis=-1, keepdims=True)
    inverse = lax.rsqrt(spread + EPS)
    return shifted * inverse, inverse


def norm_back(raised, unit, inverse):
    mean = jnp.mean(raised, axis=-1, keepdims=True)
    along = jnp.mean(raised * unit, axis=-1, keepdims=True)
    return (raised - mean - unit * along) * inverse


def turns(base_ref, row_ref):
    place = lax.axis_index(("y", "x", "c")) * 4 + lax.axis_index("z")
    base = base_ref[pl.ds(place, 1), :]
    cos_base, sin_base = base[:, :128], base[:, 128:]
    cos_row, sin_row = row_ref[:, :128], row_ref[:, 128:]
    cosine = cos_base * cos_row - sin_base * sin_row
    sine = sin_base * cos_row + cos_base * sin_row
    first = lax.broadcasted_iota(jnp.int32, sine.shape, 1) % HEAD_DIM < HEAD_DIM // 2
    return cosine, jnp.where(first, -sine, sine)


def turn(pair, cosine, sine):
    half = HEAD_DIM // 2
    first = lax.broadcasted_iota(jnp.int32, pair.shape, 1) % HEAD_DIM < half
    crossed = jnp.where(first, pltpu.roll(pair, 128 - half, 1), pltpu.roll(pair, half, 1))
    return pair * cosine + crossed * sine


def pre_kernel(clip_ref, mask_ref, tok_ref, type_ref, table_ref, gain_ref, w_ref, base_ref, row_ref, sent_ref, start_ref, low_ref, mixed_ref, kinds_ref):
    swapped = clip_ref[0]
    cosine, sine = turns(base_ref, row_ref)
    kinds_ref[...] = jnp.zeros(kinds_ref.shape, BF)
    kinds_ref[:TYPES, :] = table_ref[...]
    for clip in range(2):
        slot = jnp.where(swapped > 0, 1 - clip, clip)
        kinds = type_ref[pl.ds(slot, 1), :]
        onehot = (lax.broadcasted_iota(jnp.int32, (16, ROWS), 0) == kinds).astype(F32).astype(BF)
        hidden = tok_ref[slot].astype(F32) + mm_t(onehot, kinds_ref[...])
        unit, _ = norm_parts(hidden)
        start_ref[clip * ROWS : (clip + 1) * ROWS, :] = hidden
        low_ref[clip * ROWS : (clip + 1) * ROWS, :] = (unit * gain_ref[...]).astype(BF)
    width = 512
    for third in range(3):
        mixed_ref[:, third * width : (third + 1) * width] = mm(low_ref[...], w_ref[:, third * width : (third + 1) * width])
    for clip in range(2):
        slot = jnp.where(swapped > 0, 1 - clip, clip)
        rows = slice(clip * ROWS, (clip + 1) * ROWS)
        real = jnp.full((16, 128), mask_ref[slot], jnp.int32).astype(F32).astype(BF)
        for pair in range(HEADS // 2):
            query = (turn(mixed_ref[rows, pair * 128 : (pair + 1) * 128], cosine, sine).astype(BF) * HEAD_DIM**-0.5).astype(BF)
            key = turn(mixed_ref[rows, width + pair * 128 : width + (pair + 1) * 128], cosine, sine).astype(BF)
            value = mixed_ref[rows, 2 * width + pair * 128 : 2 * width + (pair + 1) * 128].astype(BF)
            for side in range(2):
                to = (2 * pair + side) * 2 + clip
                lanes = slice(side * HEAD_DIM, (side + 1) * HEAD_DIM)
                sent_ref[to, :ROWS, :] = jnp.concatenate([key[:, lanes], value[:, lanes]], axis=1)
                sent_ref[to, ROWS : ROWS + ROWS // 2, :] = jnp.concatenate([query[: ROWS // 2, lanes], query[ROWS // 2 :, lanes]], axis=1)
                sent_ref[to, ROWS + ROWS // 2 :, :] = real


def mm_nt(a, b):
    return lax.dot_general(a, b, (((1,), (1,)), ((), ())), preferred_element_type=F32)


FF_PART = 512
GELU_SCALE = float(np.sqrt(2.0 / np.pi))
GELU_CUBE = 0.044715
G_AT, DU_AT, N2_AT, DY_AT, AT_AT, DA_AT, ACT_WIDTH = 0, 1024, 2048, 2560, 3072, 3328, 3840


def mlp_kernel(
    clip_ref, got_ref, start_ref, cot_ref, gain_ref, wo_ref, wu_ref, wd_ref, out_ref, packed_ref, mid_ref, gaing_ref, acts_ref,
    attn_ref, slope_ref,
):
    swapped, core = clip_ref[0], lax.axis_index("c")
    keep, send = 0, 1
    for clip in range(2):
        for pair in range(HEADS // 2):
            one, two = got_ref[4 * pair + clip], got_ref[4 * pair + 2 + clip]
            attn_ref[clip * ROWS : clip * ROWS + ROWS // 2, pair * 128 : (pair + 1) * 128] = jnp.concatenate([one[:, :HEAD_DIM], two[:, :HEAD_DIM]], axis=1)
            attn_ref[clip * ROWS + ROWS // 2 : (clip + 1) * ROWS, pair * 128 : (pair + 1) * 128] = jnp.concatenate([one[:, HEAD_DIM:], two[:, HEAD_DIM:]], axis=1)
    slots = [jnp.where(swapped > 0, 1 - clip, clip) for clip in range(2)]
    grad_low = jnp.concatenate([cot_ref[slots[0]], cot_ref[slots[1]]], axis=0)
    attn = attn_ref[...]
    middle = start_ref[...] + mm(attn, wo_ref[...])
    unit, inverse = norm_parts(middle)
    low = (unit * gain_ref[...]).astype(BF)
    final = middle
    for part in range(4):
        cols = slice(part * FF_PART, (part + 1) * FF_PART)
        upper = mm(low, wu_ref[:, cols])
        square = upper * upper
        bend = jnp.tanh(GELU_SCALE * (upper + GELU_CUBE * (square * upper)))
        act = (0.5 * upper * (1.0 + bend)).astype(BF)
        rise = 0.5 * (1.0 + bend) + 0.5 * upper * (1.0 - bend * bend) * (GELU_SCALE * (1.0 + 3.0 * GELU_CUBE * square))
        final = final + mm(act, wd_ref[cols, :])
        slope = (mm_nt(grad_low, wd_ref[cols, :]) * rise).astype(BF)
        slope_ref[:, cols] = slope
        side = jnp.where(core == part // 2, keep, send)
        at = (part % 2) * FF_PART
        acts_ref[side, :, G_AT + at : G_AT + at + FF_PART] = act
        acts_ref[side, :, DU_AT + at : DU_AT + at + FF_PART] = slope
    for clip in range(2):
        out_ref[slots[clip]] = final[clip * ROWS : (clip + 1) * ROWS].astype(BF)
    down = mm_nt(slope_ref[...], wu_ref[...])
    gaing_ref[...] = jnp.sum(down * unit, axis=0, keepdims=True)
    grad_mid = grad_low.astype(F32) + norm_back(down * gain_ref[...], unit, inverse)
    mid_ref[...] = grad_mid
    grad_mid_low = grad_mid.astype(BF)
    grad_attn = mm_nt(grad_mid_low, wo_ref[...]).astype(BF)
    for side in (keep, send):
        acts_ref[side, :, N2_AT : N2_AT + 512] = low
        acts_ref[side, :, DY_AT : DY_AT + 512] = grad_low
        acts_ref[side, :, DA_AT : DA_AT + 512] = grad_mid_low
    for half in range(2):
        acts_ref[jnp.where(core == half, keep, send), :, AT_AT : AT_AT + 256] = attn[:, half * 256 : (half + 1) * 256]
    for clip in range(2):
        for pair in range(HEADS // 2):
            rows = grad_attn[clip * ROWS : (clip + 1) * ROWS, pair * 128 : (pair + 1) * 128]
            upper_rows, lower_rows = rows[: ROWS // 2], rows[ROWS // 2 :]
            packed_ref[4 * pair + clip] = jnp.concatenate([upper_rows[:, :HEAD_DIM], lower_rows[:, :HEAD_DIM]], axis=1)
            packed_ref[4 * pair + 2 + clip] = jnp.concatenate([upper_rows[:, HEAD_DIM:], lower_rows[:, HEAD_DIM:]], axis=1)


UP_AT, OUT_AT, PIECE_ROWS = 1024, 2048, 2304


def weight_kernel(acts_ref, theirs_ref, *piece_refs):
    block = lax.axis_index("z")

    def both(at, width):
        return jnp.concatenate([acts_ref[0, :, pl.ds(at, width)], theirs_ref[:, pl.ds(at, width)]], axis=0)

    grad_low, low, attn = both(DY_AT, 512), both(N2_AT, 512), both(AT_AT, 256)
    for step, piece_ref in enumerate(piece_refs):
        piece = lax.rem(block + step, 4)
        units = pl.multiple_of(piece * 256, 256)
        down = mm_t(both(G_AT + units, 256), grad_low).astype(BF)
        for part in range(4):
            piece_ref[part * 256 : (part + 1) * 256, :] = down[:, part * 128 : (part + 1) * 128]
        up = mm_t(low, both(DU_AT + units, 256)).astype(BF)
        for part in range(2):
            piece_ref[UP_AT + part * 512 : UP_AT + (part + 1) * 512, :] = up[:, part * 128 : (part + 1) * 128]
        piece_ref[OUT_AT:, :] = mm_t(attn, both(DA_AT + pl.multiple_of(piece * 128, 128), 128)).astype(BF)


QKV_HALF = 768


def post_kernel(
    clip_ref, back_ref, start_ref, mid_ref, low_ref, type_ref, mlp_ref, gain_ref, w_ref, base_ref, row_ref, grad_ref, acts_ref, raw_ref
):
    swapped, core = clip_ref[0], lax.axis_index("c")
    cosine, sine = turns(base_ref, row_ref)
    half = ROWS // 2

    def unpack(one, two):
        upper_rows = jnp.concatenate([one[:, :HEAD_DIM], two[:, :HEAD_DIM]], axis=1)
        lower_rows = jnp.concatenate([one[:, HEAD_DIM:], two[:, HEAD_DIM:]], axis=1)
        return jnp.concatenate([upper_rows, lower_rows], axis=0)

    for clip in range(2):
        rows = slice(clip * ROWS, (clip + 1) * ROWS)
        for pair in range(HEADS // 2):
            one, two = 4 * pair + clip, 4 * pair + 2 + clip
            query = unpack(back_ref[one, ROWS : ROWS + half, :], back_ref[two, ROWS : ROWS + half, :]).astype(F32)
            first, second = back_ref[one, :ROWS, :], back_ref[two, :ROWS, :]
            key = jnp.concatenate([first[:, :HEAD_DIM], second[:, :HEAD_DIM]], axis=1).astype(F32)
            cols = pair * 128
            raw_ref[rows, cols : cols + 128] = turn(query, cosine, -sine).astype(BF)
            raw_ref[rows, 512 + cols : 512 + cols + 128] = turn(key, cosine, -sine).astype(BF)
            raw_ref[rows, 1024 + cols : 1024 + cols + 128] = jnp.concatenate([first[:, HEAD_DIM:], second[:, HEAD_DIM:]], axis=1)
    raw = raw_ref[...]
    down = mm_nt(raw, w_ref[...])
    unit, inverse = norm_parts(start_ref[...])
    grad = mid_ref[...] + norm_back(down * gain_ref[...], unit, inverse)
    gain_grad = jnp.sum(down * unit, axis=0, keepdims=True)
    slots = [jnp.where(swapped > 0, 1 - clip, clip) for clip in range(2)]
    table = jnp.zeros((8, 512), F32)
    for clip in range(2):
        part = grad[clip * ROWS : (clip + 1) * ROWS]
        grad_ref[slots[clip]] = part
        kinds = type_ref[pl.ds(slots[clip], 1), :]
        onehot = (lax.broadcasted_iota(jnp.int32, (8, ROWS), 0) == kinds).astype(F32)
        table = table + jnp.dot(onehot, part, precision=lax.Precision.HIGHEST, preferred_element_type=F32)
    row = lax.broadcasted_iota(jnp.int32, (16, 512), 0)
    small = jnp.concatenate([table, jnp.zeros((8, 512), F32)], axis=0)
    small = jnp.where(row == 3, gain_grad, jnp.where(row == 4, mlp_ref[...], small)).astype(BF)
    for side in range(2):
        acts_ref[side, :128, :512] = low_ref[...]
        acts_ref[side, 128:, :512] = small
        acts_ref[side, 128:, 512:] = jnp.zeros((16, QKV_HALF), BF)
    for part in range(2):
        side = jnp.where(core == part, 0, 1)
        acts_ref[side, :128, 512:] = raw[:, part * QKV_HALF : (part + 1) * QKV_HALF]


def mix_weight_kernel(acts_ref, theirs_ref, pieces_ref):
    low = jnp.concatenate([acts_ref[0, :128, :512], theirs_ref[:128, :512]], axis=0)
    raw = jnp.concatenate([acts_ref[0, :128, 512:], theirs_ref[:128, 512:]], axis=0)
    small = acts_ref[0, 128:, :512].astype(F32) + theirs_ref[128:, :512].astype(F32)
    for place in range(64):
        pieces_ref[place, :, 384:] = jnp.zeros((16, 128), BF)
    for side in range(2):
        grad = mm_t(low, raw[:, side * 384 : (side + 1) * 384]).astype(BF)
        for strip in range(32):
            pieces_ref[2 * strip + side, :, :384] = grad[strip * 16 : (strip + 1) * 16]
    for row in range(5):
        for part in range(4):
            value = jnp.broadcast_to(small[row : row + 1, part * 128 : (part + 1) * 128], (16, 128))
            pieces_ref[4 * row + part, :, 384:] = value.astype(BF)


def mix_sum_kernel(own_ref, theirs_ref, qkv_ref, table_ref, gain_one_ref, gain_two_ref):
    core = lax.axis_index("c")
    for half in range(2):

        def write(pieces_ref):
            for place in range(64):
                strip, side = place // 2, place % 2
                cols = half * QKV_HALF + side * 384
                qkv_ref[strip * 16 : (strip + 1) * 16, cols : cols + 384] = pieces_ref[place, :, :384].astype(F32)

        pl.when(core == half)(functools.partial(write, own_ref))
        pl.when(core != half)(functools.partial(write, theirs_ref))
    for row in range(5):
        target, line = ((table_ref, row), (table_ref, row), (table_ref, row), (gain_one_ref, 0), (gain_two_ref, 0))[row]
        for part in range(4):
            target[line : line + 1, part * 128 : (part + 1) * 128] = own_ref[4 * row + part, 0:1, 384:].astype(F32)


def spread_kernel(*refs):
    pieces, (down, up, out, low, down_stage, up_stage, out_stage, in_sems, out_sems) = refs[:8], refs[8:]
    reads = [pltpu.make_async_copy(piece, low.at[at], in_sems.at[at]) for at, piece in enumerate(pieces)]
    for read in reads:
        read.start()
    writes = []

    def write(source, target):
        writes.append(pltpu.make_async_copy(source, target, out_sems.at[len(writes)]))
        writes[-1].start()

    for at, read in enumerate(reads):
        read.wait()
        core = lax.axis_index("c") if at < 4 else 1 - lax.axis_index("c")
        piece = lax.rem(lax.axis_index("z") + at, 4)
        units = pl.ds(pl.multiple_of(core * 1024 + piece * 256, 256), 256)
        for part in range(4):
            down_stage[at, :, part * 128 : (part + 1) * 128] = low[at, part * 256 : (part + 1) * 256, :].astype(F32)
        write(down_stage.at[at], down.at[units, :])
        for part in range(2):
            up_stage[at, :, part * 128 : (part + 1) * 128] = low[at, UP_AT + part * 512 : UP_AT + (part + 1) * 512, :].astype(F32)
        write(up_stage.at[at], up.at[:, units])
        out_stage[at] = low[at, OUT_AT:, :].astype(F32)
        write(out_stage.at[at], out.at[pl.ds(core * 256, 256), pl.ds(pl.multiple_of(piece * 128, 128), 128)])
    for copy in writes:
        copy.wait()


VMEM_SPEC = pl.BlockSpec(memory_space=pltpu.VMEM)
SMEM_SPEC = pl.BlockSpec(memory_space=pltpu.SMEM)


def call(kernel, name, outs, args, scalars=1, scratch=(), megabytes=28, flops=10**9, nbytes=4 * 2**20, exps=0):
    shapes = tuple(jax.ShapeDtypeStruct(shape, dtype) for shape, dtype in outs)
    return pl.pallas_call(
        kernel,
        out_shape=shapes,
        in_specs=[SMEM_SPEC] * scalars + [VMEM_SPEC] * (len(args) - scalars),
        out_specs=(VMEM_SPEC,) * len(shapes),
        scratch_shapes=[pltpu.VMEM(shape, dtype) for shape, dtype in scratch],
        compiler_params=pltpu.CompilerParams(vmem_limit_bytes=megabytes * 2**20),
        cost_estimate=pl.CostEstimate(flops=flops, bytes_accessed=nbytes, transcendentals=exps),
        name=name,
    )(*args)


WIDE = ((128, LOCAL), F32)
LINE = ((1, LOCAL), F32)


QUERIES = ((128, LOCAL), BF)
GRADS = ((64, LOCAL), F32)
PACKED = ((FRAMES, ROWS // 2, 128), BF)


def attend(name, got, blocks, arrays, state=(), last=False, flops=10**9):
    first = not state
    outs = (PACKED, GRADS, LINE) if last else (WIDE, LINE) + ((QUERIES,) if first else ())
    scratch = ((WIDE, LINE) if last else ()) + (((2, len(blocks) * TILE, TILE), F32),)
    return call(
        functools.partial(forward_kernel, blocks, first, last), name, outs, (got,) + tuple(arrays) + tuple(state),
        scalars=0, scratch=scratch, flops=flops, nbytes=10**5,
    )


def attend_back(name, got, grad, ot, lse, offsets, arrays, state=(), flops=10**8):
    first, blocks = not state, ((len(offsets), LOCAL, 128), BF)
    flat = ((LOCAL, 128), BF)
    outs = (blocks, blocks) + ((GRADS, QUERIES, flat, QUERIES, flat, LINE) if first else (PACKED,))
    scratch = (() if first else (GRADS,)) + (((2, 2 * TILE, TILE), F32),)
    return call(
        functools.partial(backward_kernel, offsets, first), name, outs, (got, grad, ot, lse) + tuple(arrays) + tuple(state),
        scalars=0, scratch=scratch, megabytes=28, flops=flops, nbytes=10**5,
    )


MIXED = (((512, 1536), F32), ((TYPES, 512), F32), ((1, 512), F32), ((1, 512), F32))


def spread(pieces):
    hbm = pl.BlockSpec(memory_space=pltpu.HBM)
    return pl.pallas_call(
        spread_kernel,
        out_shape=tuple(jax.ShapeDtypeStruct(shape, F32) for shape in ((2048, 512), (512, 2048), (512, 512))),
        in_specs=[hbm] * 8,
        out_specs=(hbm,) * 3,
        scratch_shapes=[
            pltpu.VMEM((8, PIECE_ROWS, 128), BF),
            pltpu.VMEM((8, 256, 512), F32),
            pltpu.VMEM((8, 512, 256), F32),
            pltpu.VMEM((8, 256, 128), F32),
            pltpu.SemaphoreType.DMA((8,)),
            pltpu.SemaphoreType.DMA((24,)),
        ],
        compiler_params=pltpu.CompilerParams(vmem_limit_bytes=40 * 2**20),
        cost_estimate=pl.CostEstimate(flops=10**7, bytes_accessed=15 * 2**20, transcendentals=0),
        name="spread",
    )(*pieces)


def swap(array, axes):
    return lax.all_to_all(array, axes, 0, 0, tiled=True)


def copies(array, axes, count):
    return swap(jnp.broadcast_to(array[None], (count,) + array.shape), axes)


def partner(array):
    return lax.ppermute(array, "c", [(0, 1), (1, 0)])


def along(array, step):
    return lax.ppermute(array, "z", [(place, (place - step) % 4) for place in range(4)])


def angle_tables():
    rates = BASE ** (-np.arange(HEAD_DIM // 2, dtype=np.float64) / (HEAD_DIM // 2))
    rates = np.tile(rates, 4)
    tables = []
    for places in (np.arange(128) * ROWS, np.arange(ROWS)):
        angles = places[:, None] * rates[None, :]
        tables.append(np.concatenate([np.cos(angles), np.sin(angles)], axis=1).astype(np.float32))
    return tables


def local(
    tokens, type_ids, clip_ids, frame_mask, type_table, norm_gain, qkv_weight, out_weight, mlp_gain, up_weight, down_weight, cotangent
):
    base_table, row_table = (jnp.asarray(table) for table in angle_tables())
    gain_one, gain_two = norm_gain[None], mlp_gain[None]
    tokens_here = 2 * ROWS
    sent, start, low = call(
        pre_kernel, "pre", (((2 * HEADS, 112, 128), BF), ((tokens_here, 512), F32), ((tokens_here, 512), BF)),
        (clip_ids, frame_mask, tokens, type_ids, type_table, gain_one, qkv_weight, base_table, row_table),
        scalars=2, scratch=(((tokens_here, 1536), F32), ((16, 512), BF)), megabytes=60,
    )

    got = swap(sent, CHIPS)
    own = got[:, :ROWS].reshape(LOCAL, 128)
    own_other = partner(own)
    up, down, far = along(own, 1), along(own, 3), along(own, 2)
    *state, queries = attend("attend_near", got, ((0, 0), (1, 0)), (own, own_other), flops=2 * 10**10)
    up, *state = lax.optimization_barrier((up, *state))
    up_other = partner(up)
    state = attend("attend_up", got, ((0, 1),), (up,), (*state, queries), flops=10**8)
    down, far, *state = lax.optimization_barrier((down, far, *state))
    down_other = partner(down)
    state = attend("attend_up_down", got, ((1, 1), (0, 3)), (up_other, down), (*state, queries), flops=10**8)
    far_other = partner(far)
    state = attend("attend_down_far", got, ((1, 3), (0, 2)), (down_other, far), (*state, queries), flops=10**8)
    packed, out_t, lse = attend("attend_far", got, ((1, 2),), (far_other,), (*state, queries), last=True)

    heads_out = swap(packed, CHIPS)
    output, grad_packed, grad_mid, mlp_part, acts = call(
        mlp_kernel, "mlp",
        (((2, ROWS, 512), BF), ((2 * HEADS, ROWS // 2, 128), BF), ((tokens_here, 512), F32), ((1, 512), F32), ((2, tokens_here, ACT_WIDTH), BF)),
        (clip_ids, heads_out, start, cotangent, gain_two, out_weight, up_weight, down_weight),
        scratch=(((tokens_here, 512), BF), ((tokens_here, 2048), BF)), flops=3 * 10**9, nbytes=8 * 2**20, exps=300000,
    )
    theirs = partner(acts[1])
    pieces = call(weight_kernel, "weights", (((PIECE_ROWS, 128), BF),) * 4, (acts, theirs), scalars=0)
    pieces, grad_packed = lax.optimization_barrier((pieces, grad_packed))
    arrived = [along(piece, -step) for step, piece in enumerate(pieces) if step]
    grad_out = swap(grad_packed, CHIPS)
    dsame, dother, *back_state = attend_back(
        "attend_back_others", got, grad_out, out_t, lse, (2, 1, 3), (far, far_other, up, up_other, down, down_other)
    )
    summed = (dsame.astype(F32) + partner(dother).astype(F32)).astype(BF)
    near_same, near_other, dq = attend_back("attend_back_near", got, grad_out, out_t, lse, (0,), (own, own_other), back_state)
    arrived, near_same, near_other = lax.optimization_barrier((arrived, near_same, near_other))
    piece = sum((part.astype(F32) for part in arrived), pieces[0].astype(F32)).astype(BF)
    piece, summed = lax.optimization_barrier((piece, summed))
    moved = [along(summed[at], -offset) for at, offset in enumerate((2, 1, 3))]
    piece = jnp.sum(swap(piece.reshape(16, PIECE_ROWS // 16, 128), CHIPS).astype(F32), axis=0).astype(BF)
    near_sum = near_same[0].astype(F32) + partner(near_other[0]).astype(F32)
    own_grad = sum((part.astype(F32) for part in moved), near_sum).astype(BF)

    spread_piece = jnp.broadcast_to(piece[None], (16, PIECE_ROWS // 16, 128))
    back = swap(jnp.concatenate([own_grad.reshape(FRAMES, ROWS, 128), dq, spread_piece], axis=1), CHIPS)
    piece = back[:, ROWS + ROWS // 2 :].reshape(PIECE_ROWS, 128)
    pieces = [piece] + [along(piece, step) for step in (1, 2, 3)]
    def ending(grads):
        input_grad, mix_acts = call(
            post_kernel, "post", (((2, ROWS, 512), F32), ((2, tokens_here + 16, 512 + QKV_HALF), BF)),
            (clip_ids, grads, start, grad_mid, low, type_ids, mlp_part, gain_one, qkv_weight, base_table, row_table),
            scratch=(((tokens_here, 1536), BF),),
        )
        (strips_out,) = call(mix_weight_kernel, "mix_weights", (((64, 16, 512), BF),), (mix_acts, partner(mix_acts[1])), scalars=0)
        mine = jnp.sum(swap(strips_out, ("y", "x", "z")).astype(F32), axis=0).astype(BF)
        return input_grad, mine

    def nothing(grads):
        return jnp.zeros((2, ROWS, 512), F32), jnp.zeros((16, 512), BF)

    input_grad, mine = lax.cond(clip_ids[0] + clip_ids[1] == 1, ending, nothing, back)
    mine, pieces = lax.optimization_barrier((mine, pieces))
    mixed = copies(mine, ("y", "x", "z"), 64)
    sums = spread(pieces + [partner(piece) for piece in pieces])
    mixed, sums = lax.optimization_barrier((mixed, sums))
    qkv_sum, table_sum, gain_one_sum, gain_two_sum = call(mix_sum_kernel, "mix_sums", MIXED, (mixed, partner(mixed)), scalars=0)
    down_sum, up_sum, out_sum = sums
    return (output, input_grad, table_sum, gain_one_sum[0], qkv_sum, out_sum, gain_two_sum[0], up_sum, down_sum)


def solution(mesh):
    chips = Mesh(mesh.devices.reshape(4, 4, 2, 4), ("y", "x", "c", "z"))
    tm = ("y", "x", "c")
    rows = P(tm, "z", None)
    in_specs = (rows, P(tm, "z"), P(tm), P(tm)) + (P(),) * 7 + (rows,)
    out_specs = (rows, rows) + (P(),) * 7
    return jax.shard_map(local, mesh=chips, in_specs=in_specs, out_specs=out_specs, check_vma=False)
```

```python
import functools

import jax
import jax.numpy as jnp
import numpy as np
from jax import lax
from jax.experimental import pallas as pl
from jax.experimental.pallas import tpu as pltpu
from jax.sharding import Mesh
from jax.sharding import PartitionSpec as P

HEADS = 8
HEAD_DIM = 64
TYPES = 3
TILE = 256
FRAMES = 16
ROWS = 64
LOCAL = FRAMES * ROWS
GROUPS = LOCAL // TILE
MASKED = -1e30
EPS = 1e-05
BASE = 10000.0
BF = jnp.bfloat16
F32 = jnp.float32
CHIPS = ("y", "x")


def mm(a, b):
    return jnp.dot(a, b, preferred_element_type=F32)


def mm_t(a, b):
    return lax.dot_general(a, b, (((0,), (0,)), ((), ())), preferred_element_type=F32)


def write_biases(bias_ref, at, is_other, key_block, row_block, parity, full):
    key = lax.broadcasted_iota(jnp.int32, (TILE, TILE), 0)
    query = lax.broadcasted_iota(jnp.int32, (TILE, TILE), 1)
    late = jnp.where(full, 0.0, MASKED)
    if is_other:
        before = key // ROWS < query // ROWS + parity
        bias_ref[0, at : at + TILE, :] = jnp.where(before, 0.0, MASKED)
        bias_ref[1, at : at + TILE, :] = jnp.where(before, late, MASKED)
        return
    before = key // ROWS < query // ROWS
    row_shift = jnp.where(key_block == row_block, 0, jnp.where(key_block < row_block, ROWS, -ROWS))
    own = (key // ROWS == query // ROWS) & ((key % ROWS) <= (query % ROWS) + row_shift)
    bias_ref[0, at : at + TILE, :] = jnp.where(before | own, 0.0, MASKED)
    bias_ref[1, at : at + TILE, :] = jnp.where(own, 0.0, jnp.where(before, late, MASKED))


def key_tiles(arrays, kb):
    return jnp.concatenate([array[pl.ds(kb * TILE, TILE), :] for array in arrays], axis=0)


def biased(scores, bias_ref, kb):
    bias = bias_ref[0 if kb == 0 else 1]
    if scores.shape[1] == TILE:
        return scores + bias
    return jnp.concatenate([scores[:, :TILE] + bias, scores[:, TILE:]], axis=1)


def strips(full, tile):
    @pl.when(full)
    def _():
        for kb in range(GROUPS):
            tile(kb, LOCAL - kb * TILE)

    @pl.when(jnp.logical_not(full))
    def _():
        for kb in range(GROUPS):
            tile(kb, TILE if kb else LOCAL)


def unfold_pair(first, second):
    return jnp.concatenate([first[:, :HEAD_DIM], first[:, HEAD_DIM:], second[:, :HEAD_DIM], second[:, HEAD_DIM:]], axis=0)


def forward_kernel(blocks, first, last, got_ref, *refs):
    arrays, rest = refs[: len(blocks)], refs[len(blocks) :]
    if first:
        acc_ref, top_ref, qt_ref, bias_ref = rest
        top_ref[...] = jnp.full(top_ref.shape, MASKED, F32)
        acc_ref[...] = jnp.zeros(acc_ref.shape, F32)
        write_queries(got_ref, qt_ref)
    else:
        in_acc, in_top, qt_ref = rest[:3]
        acc_ref, top_ref, bias_ref = rest[6:] if last else rest[3:]
        top_ref[...] = in_top[...]
        acc_ref[...] = in_acc[...]
    full, row_block, parity = places(got_ref)
    for place, (is_other, offset) in enumerate(blocks):
        write_biases(bias_ref, place * TILE, is_other, lax.rem(row_block + offset, 4), row_block, parity, full)

    def tile(kb, width):
        cols = pl.ds(kb * TILE, width)
        keys = key_tiles(arrays, kb)
        flipped = keys.T
        values = jnp.where(lax.broadcasted_iota(jnp.int32, flipped.shape, 0) < HEAD_DIM, jnp.ones((), BF), flipped)
        scores = biased(mm(keys, qt_ref[:, cols]), bias_ref, kb)
        top_old = top_ref[:, cols]
        top_new = jnp.maximum(top_old, jnp.max(scores, axis=0, keepdims=True))
        weights = jnp.exp(scores - top_new).astype(BF)
        acc_ref[:, cols] = acc_ref[:, cols] * jnp.exp(top_old - top_new) + mm(values, weights)
        top_ref[:, cols] = top_new

    strips(full, tile)
    if last:
        packed_ref, ot_ref, lse_ref = rest[3:6]
        total = acc_ref[0:1, :]
        out_t = acc_ref[HEAD_DIM:, :] / total
        ot_ref[...] = out_t
        lse_ref[...] = top_ref[...] + jnp.log(total)
        pack_frames(out_t.astype(BF), packed_ref)


def places(got_ref):
    full = jnp.max(got_ref[FRAMES - 1, ROWS + ROWS // 2 :, :].astype(F32)) > 0.5
    return full, lax.axis_index("z"), lax.axis_index("c")


def pack_frames(flipped, packed_ref):
    half = ROWS // 2
    for pair in range(FRAMES // 2):
        part = flipped[:, pair * 128 : (pair + 1) * 128].T
        packed_ref[2 * pair] = jnp.concatenate([part[:half], part[half:ROWS]], axis=1)
        packed_ref[2 * pair + 1] = jnp.concatenate([part[ROWS : ROWS + half], part[ROWS + half :]], axis=1)


def write_queries(got_ref, qt_ref):
    for pair in range(FRAMES // 2):
        rows = unfold_pair(got_ref[2 * pair, ROWS : ROWS + ROWS // 2, :], got_ref[2 * pair + 1, ROWS : ROWS + ROWS // 2, :])
        qt_ref[:HEAD_DIM, pair * 128 : (pair + 1) * 128] = rows.T
    qt_ref[HEAD_DIM:, :] = jnp.zeros((HEAD_DIM, LOCAL), BF)


def backward_kernel(offsets, first, got_ref, grad_ref, ot_ref, lse_ref, *refs):
    arrays, rest = refs[: 2 * len(offsets)], refs[2 * len(offsets) :]
    if first:
        dsame_ref, dother_ref, dqt_ref, qt_ref, q_ref, dot_ref, do_ref, delta_ref, bias_ref = rest
        write_queries(got_ref, qt_ref)
        blank = jnp.zeros((2 * ROWS, HEAD_DIM), BF)
        for pair in range(FRAMES // 2):
            span = pl.ds(pair * 128, 128)
            query = unfold_pair(got_ref[2 * pair, ROWS : ROWS + ROWS // 2, :], got_ref[2 * pair + 1, ROWS : ROWS + ROWS // 2, :])
            grad = unfold_pair(grad_ref[2 * pair], grad_ref[2 * pair + 1])
            q_ref[span, :] = jnp.concatenate([query, blank], axis=1)
            do_ref[span, :] = jnp.concatenate([blank, grad], axis=1)
            dot_ref[HEAD_DIM:, pair * 128 : (pair + 1) * 128] = grad.T
        dot_ref[:HEAD_DIM, :] = jnp.zeros((HEAD_DIM, LOCAL), BF)
        delta_ref[...] = jnp.sum(dot_ref[HEAD_DIM:, :].astype(F32) * ot_ref[...], axis=0, keepdims=True)
        dqt_ref[...] = jnp.zeros(dqt_ref.shape, F32)
    else:
        in_dqt, qt_ref, q_ref, dot_ref, do_ref, delta_ref, dsame_ref, dother_ref, packed_ref, dqt_ref, bias_ref = rest
        dqt_ref[...] = in_dqt[...]
    full, row_block, parity = places(got_ref)
    for block, offset in enumerate(offsets):
        key_block = lax.rem(row_block + offset, 4)
        for is_other in range(2):
            write_biases(bias_ref, is_other * TILE, is_other, key_block, row_block, parity, full)

        def tile(kb, width):
            cols = pl.ds(kb * TILE, width)
            rows = pl.ds(kb * TILE, TILE)
            keys = key_tiles(arrays[2 * block : 2 * block + 2], kb)
            scores = biased(mm(keys, qt_ref[:, cols]), bias_ref, kb)
            weights = jnp.exp(scores - lse_ref[:, cols])
            slopes = (weights * (mm(keys, dot_ref[:, cols]) - delta_ref[:, cols])).astype(BF)
            dqt_ref[:, cols] += mm(keys[:, :HEAD_DIM].T, slopes)
            both = mm(slopes, q_ref[cols, :]) + mm(weights.astype(BF), do_ref[cols, :])
            dsame_ref[block, rows, :] = both[:TILE, :].astype(BF)
            dother_ref[block, rows, :] = both[TILE:, :].astype(BF)

        strips(full, tile)
    if not first:
        pack_frames((dqt_ref[...] * HEAD_DIM**-0.5).astype(BF), packed_ref)


def norm_parts(hidden):
    centre = jnp.mean(hidden, axis=-1, keepdims=True)
    shifted = hidden - centre
    spread = jnp.mean(shifted * shifted, axis=-1, keepdims=True)
    inverse = lax.rsqrt(spread + EPS)
    return shifted * inverse, inverse


def norm_back(raised, unit, inverse):
    mean = jnp.mean(raised, axis=-1, keepdims=True)
    along = jnp.mean(raised * unit, axis=-1, keepdims=True)
    return (raised - mean - unit * along) * inverse


def turns(base_ref, row_ref):
    place = lax.axis_index(("y", "x", "c")) * 4 + lax.axis_index("z")
    base = base_ref[pl.ds(place, 1), :]
    cos_base, sin_base = base[:, :128], base[:, 128:]
    cos_row, sin_row = row_ref[:, :128], row_ref[:, 128:]
    cosine = cos_base * cos_row - sin_base * sin_row
    sine = sin_base * cos_row + cos_base * sin_row
    first = lax.broadcasted_iota(jnp.int32, sine.shape, 1) % HEAD_DIM < HEAD_DIM // 2
    return cosine, jnp.where(first, -sine, sine)


def turn(pair, cosine, sine):
    half = HEAD_DIM // 2
    first = lax.broadcasted_iota(jnp.int32, pair.shape, 1) % HEAD_DIM < half
    crossed = jnp.where(first, pltpu.roll(pair, 128 - half, 1), pltpu.roll(pair, half, 1))
    return pair * cosine + crossed * sine


def pre_kernel(clip_ref, mask_ref, tok_ref, type_ref, table_ref, gain_ref, w_ref, base_ref, row_ref, sent_ref, start_ref, low_ref, mixed_ref, kinds_ref):
    swapped = clip_ref[0]
    cosine, sine = turns(base_ref, row_ref)
    kinds_ref[...] = jnp.zeros(kinds_ref.shape, BF)
    kinds_ref[:TYPES, :] = table_ref[...]
    for clip in range(2):
        slot = jnp.where(swapped > 0, 1 - clip, clip)
        kinds = type_ref[pl.ds(slot, 1), :]
        onehot = (lax.broadcasted_iota(jnp.int32, (16, ROWS), 0) == kinds).astype(F32).astype(BF)
        hidden = tok_ref[slot].astype(F32) + mm_t(onehot, kinds_ref[...])
        unit, _ = norm_parts(hidden)
        start_ref[clip * ROWS : (clip + 1) * ROWS, :] = hidden
        low_ref[clip * ROWS : (clip + 1) * ROWS, :] = (unit * gain_ref[...]).astype(BF)
    width = 512
    for third in range(3):
        mixed_ref[:, third * width : (third + 1) * width] = mm(low_ref[...], w_ref[:, third * width : (third + 1) * width])
    for clip in range(2):
        slot = jnp.where(swapped > 0, 1 - clip, clip)
        rows = slice(clip * ROWS, (clip + 1) * ROWS)
        real = jnp.full((16, 128), mask_ref[slot], jnp.int32).astype(F32).astype(BF)
        for pair in range(HEADS // 2):
            query = (turn(mixed_ref[rows, pair * 128 : (pair + 1) * 128], cosine, sine).astype(BF) * HEAD_DIM**-0.5).astype(BF)
            key = turn(mixed_ref[rows, width + pair * 128 : width + (pair + 1) * 128], cosine, sine).astype(BF)
            value = mixed_ref[rows, 2 * width + pair * 128 : 2 * width + (pair + 1) * 128].astype(BF)
            for side in range(2):
                to = (2 * pair + side) * 2 + clip
                lanes = slice(side * HEAD_DIM, (side + 1) * HEAD_DIM)
                sent_ref[to, :ROWS, :] = jnp.concatenate([key[:, lanes], value[:, lanes]], axis=1)
                sent_ref[to, ROWS : ROWS + ROWS // 2, :] = jnp.concatenate([query[: ROWS // 2, lanes], query[ROWS // 2 :, lanes]], axis=1)
                sent_ref[to, ROWS + ROWS // 2 :, :] = real


def mm_nt(a, b):
    return lax.dot_general(a, b, (((1,), (1,)), ((), ())), preferred_element_type=F32)


FF_PART = 512
GELU_SCALE = float(np.sqrt(2.0 / np.pi))
GELU_CUBE = 0.044715
G_AT, DU_AT, N2_AT, DY_AT, AT_AT, DA_AT, ACT_WIDTH = 0, 1024, 2048, 2560, 3072, 3328, 3840


def mlp_kernel(
    clip_ref, got_ref, start_ref, cot_ref, gain_ref, wo_ref, wu_ref, wd_ref, out_ref, packed_ref, mid_ref, gaing_ref, acts_ref,
    attn_ref, slope_ref,
):
    swapped, core = clip_ref[0], lax.axis_index("c")
    keep, send = 0, 1
    for clip in range(2):
        for pair in range(HEADS // 2):
            one, two = got_ref[4 * pair + clip], got_ref[4 * pair + 2 + clip]
            attn_ref[clip * ROWS : clip * ROWS + ROWS // 2, pair * 128 : (pair + 1) * 128] = jnp.concatenate([one[:, :HEAD_DIM], two[:, :HEAD_DIM]], axis=1)
            attn_ref[clip * ROWS + ROWS // 2 : (clip + 1) * ROWS, pair * 128 : (pair + 1) * 128] = jnp.concatenate([one[:, HEAD_DIM:], two[:, HEAD_DIM:]], axis=1)
    slots = [jnp.where(swapped > 0, 1 - clip, clip) for clip in range(2)]
    grad_low = jnp.concatenate([cot_ref[slots[0]], cot_ref[slots[1]]], axis=0)
    attn = attn_ref[...]
    middle = start_ref[...] + mm(attn, wo_ref[...])
    unit, inverse = norm_parts(middle)
    low = (unit * gain_ref[...]).astype(BF)
    final = middle
    for part in range(4):
        cols = slice(part * FF_PART, (part + 1) * FF_PART)
        upper = mm(low, wu_ref[:, cols])
        square = upper * upper
        bend = jnp.tanh(GELU_SCALE * (upper + GELU_CUBE * (square * upper)))
        act = (0.5 * upper * (1.0 + bend)).astype(BF)
        rise = 0.5 * (1.0 + bend) + 0.5 * upper * (1.0 - bend * bend) * (GELU_SCALE * (1.0 + 3.0 * GELU_CUBE * square))
        final = final + mm(act, wd_ref[cols, :])
        slope = (mm_nt(grad_low, wd_ref[cols, :]) * rise).astype(BF)
        slope_ref[:, cols] = slope
        side = jnp.where(core == part // 2, keep, send)
        at = (part % 2) * FF_PART
        acts_ref[side, :, G_AT + at : G_AT + at + FF_PART] = act
        acts_ref[side, :, DU_AT + at : DU_AT + at + FF_PART] = slope
    for clip in range(2):
        out_ref[slots[clip]] = final[clip * ROWS : (clip + 1) * ROWS].astype(BF)
    down = mm_nt(slope_ref[...], wu_ref[...])
    gaing_ref[...] = jnp.sum(down * unit, axis=0, keepdims=True)
    grad_mid = grad_low.astype(F32) + norm_back(down * gain_ref[...], unit, inverse)
    mid_ref[...] = grad_mid
    grad_mid_low = grad_mid.astype(BF)
    grad_attn = mm_nt(grad_mid_low, wo_ref[...]).astype(BF)
    for side in (keep, send):
        acts_ref[side, :, N2_AT : N2_AT + 512] = low
        acts_ref[side, :, DY_AT : DY_AT + 512] = grad_low
        acts_ref[side, :, DA_AT : DA_AT + 512] = grad_mid_low
    for half in range(2):
        acts_ref[jnp.where(core == half, keep, send), :, AT_AT : AT_AT + 256] = attn[:, half * 256 : (half + 1) * 256]
    for clip in range(2):
        for pair in range(HEADS // 2):
            rows = grad_attn[clip * ROWS : (clip + 1) * ROWS, pair * 128 : (pair + 1) * 128]
            upper_rows, lower_rows = rows[: ROWS // 2], rows[ROWS // 2 :]
            packed_ref[4 * pair + clip] = jnp.concatenate([upper_rows[:, :HEAD_DIM], lower_rows[:, :HEAD_DIM]], axis=1)
            packed_ref[4 * pair + 2 + clip] = jnp.concatenate([upper_rows[:, HEAD_DIM:], lower_rows[:, HEAD_DIM:]], axis=1)


UP_AT, OUT_AT, PIECE_ROWS = 1024, 2048, 2304


def weight_kernel(acts_ref, theirs_ref, *piece_refs):
    block = lax.axis_index("z")

    def both(at, width):
        return jnp.concatenate([acts_ref[0, :, pl.ds(at, width)], theirs_ref[:, pl.ds(at, width)]], axis=0)

    grad_low, low, attn = both(DY_AT, 512), both(N2_AT, 512), both(AT_AT, 256)
    for step, piece_ref in enumerate(piece_refs):
        piece = lax.rem(block + step, 4)
        units = pl.multiple_of(piece * 256, 256)
        down = mm_t(both(G_AT + units, 256), grad_low).astype(BF)
        for part in range(4):
            piece_ref[part * 256 : (part + 1) * 256, :] = down[:, part * 128 : (part + 1) * 128]
        up = mm_t(low, both(DU_AT + units, 256)).astype(BF)
        for part in range(2):
            piece_ref[UP_AT + part * 512 : UP_AT + (part + 1) * 512, :] = up[:, part * 128 : (part + 1) * 128]
        piece_ref[OUT_AT:, :] = mm_t(attn, both(DA_AT + pl.multiple_of(piece * 128, 128), 128)).astype(BF)


QKV_HALF = 768


def turn_back_kernel(back_ref, low_ref, base_ref, row_ref, acts_ref):
    core = lax.axis_index("c")
    cosine, sine = turns(base_ref, row_ref)
    half = ROWS // 2

    def unpack(one, two):
        upper_rows = jnp.concatenate([one[:, :HEAD_DIM], two[:, :HEAD_DIM]], axis=1)
        lower_rows = jnp.concatenate([one[:, HEAD_DIM:], two[:, HEAD_DIM:]], axis=1)
        return jnp.concatenate([upper_rows, lower_rows], axis=0)

    def write(rows, cols, value):
        side = jnp.where(core == cols // QKV_HALF, 0, 1)
        at = 512 + cols % QKV_HALF
        acts_ref[side, rows, at : at + 128] = value

    for clip in range(2):
        rows = slice(clip * ROWS, (clip + 1) * ROWS)
        for pair in range(HEADS // 2):
            one, two = 4 * pair + clip, 4 * pair + 2 + clip
            query = unpack(back_ref[one, ROWS : ROWS + half, :], back_ref[two, ROWS : ROWS + half, :]).astype(F32)
            first, second = back_ref[one, :ROWS, :], back_ref[two, :ROWS, :]
            key = jnp.concatenate([first[:, :HEAD_DIM], second[:, :HEAD_DIM]], axis=1).astype(F32)
            cols = pair * 128
            write(rows, cols, turn(query, cosine, -sine).astype(BF))
            write(rows, 512 + cols, turn(key, cosine, -sine).astype(BF))
            write(rows, 1024 + cols, jnp.concatenate([first[:, HEAD_DIM:], second[:, HEAD_DIM:]], axis=1))
    for side in range(2):
        acts_ref[side, :, :512] = low_ref[...]


def post_kernel(clip_ref, acts_ref, start_ref, mid_ref, type_ref, mlp_ref, gain_ref, w_ref, grad_ref, small_ref):
    swapped, core = clip_ref[0], lax.axis_index("c")
    down = jnp.zeros((2 * ROWS, 512), F32)
    for part in range(2):
        raw = acts_ref[jnp.where(core == part, 0, 1), :, 512:]
        down = down + mm_nt(raw, w_ref[:, part * QKV_HALF : (part + 1) * QKV_HALF])
    unit, inverse = norm_parts(start_ref[...])
    grad = mid_ref[...] + norm_back(down * gain_ref[...], unit, inverse)
    gain_grad = jnp.sum(down * unit, axis=0, keepdims=True)
    table = jnp.zeros((8, 512), F32)
    for clip in range(2):
        slot = jnp.where(swapped > 0, 1 - clip, clip)
        part = grad[clip * ROWS : (clip + 1) * ROWS]
        grad_ref[slot] = part
        kinds = type_ref[pl.ds(slot, 1), :]
        onehot = (lax.broadcasted_iota(jnp.int32, (8, ROWS), 0) == kinds).astype(F32)
        table = table + jnp.dot(onehot, part, precision=lax.Precision.HIGHEST, preferred_element_type=F32)
    row = lax.broadcasted_iota(jnp.int32, (8, 512), 0)
    small_ref[...] = jnp.where(row == 3, gain_grad, jnp.where(row == 4, mlp_ref[...], table))


def mix_weight_kernel(acts_ref, theirs_ref, small_ref, pieces_ref):
    low = jnp.concatenate([acts_ref[0, :, :512], theirs_ref[:, :512]], axis=0)
    raw = jnp.concatenate([acts_ref[0, :, 512:], theirs_ref[:, 512:]], axis=0)
    small = small_ref[...]
    for side in range(2):
        grad = mm_t(low, raw[:, side * 384 : (side + 1) * 384]).astype(BF)
        for strip in range(32):
            for part in range(3):
                block = grad[strip * 16 : (strip + 1) * 16, part * 128 : (part + 1) * 128]
                pieces_ref[2 * strip + side, part * 16 : (part + 1) * 16, :] = block
    for place in range(64):
        row, part = place // 4, place % 4
        value = jnp.zeros((8, 128), F32)
        if row < 5:
            value = jnp.broadcast_to(small[row : row + 1, part * 128 : (part + 1) * 128], (8, 128))
        pieces_ref[place, 48:, :] = value.astype(BF)


def total_kernel(pieces_ref, copies_ref):
    total = pieces_ref[0].astype(F32)
    for place in range(1, 64):
        total = total + pieces_ref[place].astype(F32)
    low = total.astype(BF)
    for place in range(64):
        copies_ref[place] = low


def mix_sum_kernel(own_ref, theirs_ref, qkv_ref, table_ref, gain_one_ref, gain_two_ref):
    core = lax.axis_index("c")
    for half in range(2):

        def write(pieces_ref):
            for place in range(64):
                strip, side = place // 2, place % 2
                cols = half * QKV_HALF + side * 384
                for part in range(3):
                    block = pieces_ref[place, part * 16 : (part + 1) * 16, :].astype(F32)
                    qkv_ref[strip * 16 : (strip + 1) * 16, cols + part * 128 : cols + (part + 1) * 128] = block

        pl.when(core == half)(functools.partial(write, own_ref))
        pl.when(core != half)(functools.partial(write, theirs_ref))
    for row in range(5):
        target, line = ((table_ref, row), (table_ref, row), (table_ref, row), (gain_one_ref, 0), (gain_two_ref, 0))[row]
        for part in range(4):
            both = own_ref[4 * row + part, 48:, :].astype(F32) + theirs_ref[4 * row + part, 48:, :].astype(F32)
            target[line : line + 1, part * 128 : (part + 1) * 128] = both[0:1]


def spread_kernel(*refs):
    pieces, (down, up, out, low, down_stage, up_stage, out_stage, in_sems, out_sems) = refs[:8], refs[8:]
    reads = [pltpu.make_async_copy(piece, low.at[at], in_sems.at[at]) for at, piece in enumerate(pieces)]
    for read in reads:
        read.start()
    writes = []

    def write(source, target):
        writes.append(pltpu.make_async_copy(source, target, out_sems.at[len(writes)]))
        writes[-1].start()

    for at, read in enumerate(reads):
        read.wait()
        core = lax.axis_index("c") if at < 4 else 1 - lax.axis_index("c")
        piece = lax.rem(lax.axis_index("z") + at, 4)
        units = pl.ds(pl.multiple_of(core * 1024 + piece * 256, 256), 256)
        for part in range(4):
            down_stage[at, :, part * 128 : (part + 1) * 128] = low[at, part * 256 : (part + 1) * 256, :].astype(F32)
        write(down_stage.at[at], down.at[units, :])
        for part in range(2):
            up_stage[at, :, part * 128 : (part + 1) * 128] = low[at, UP_AT + part * 512 : UP_AT + (part + 1) * 512, :].astype(F32)
        write(up_stage.at[at], up.at[:, units])
        out_stage[at] = low[at, OUT_AT:, :].astype(F32)
        write(out_stage.at[at], out.at[pl.ds(core * 256, 256), pl.ds(pl.multiple_of(piece * 128, 128), 128)])
    for copy in writes:
        copy.wait()


VMEM_SPEC = pl.BlockSpec(memory_space=pltpu.VMEM)
SMEM_SPEC = pl.BlockSpec(memory_space=pltpu.SMEM)


def call(kernel, name, outs, args, scalars=1, scratch=(), megabytes=28, flops=10**9, nbytes=4 * 2**20, exps=0):
    shapes = tuple(jax.ShapeDtypeStruct(shape, dtype) for shape, dtype in outs)
    return pl.pallas_call(
        kernel,
        out_shape=shapes,
        in_specs=[SMEM_SPEC] * scalars + [VMEM_SPEC] * (len(args) - scalars),
        out_specs=(VMEM_SPEC,) * len(shapes),
        scratch_shapes=[pltpu.VMEM(shape, dtype) for shape, dtype in scratch],
        compiler_params=pltpu.CompilerParams(vmem_limit_bytes=megabytes * 2**20),
        cost_estimate=pl.CostEstimate(flops=flops, bytes_accessed=nbytes, transcendentals=exps),
        name=name,
    )(*args)


WIDE = ((128, LOCAL), F32)
LINE = ((1, LOCAL), F32)


QUERIES = ((128, LOCAL), BF)
GRADS = ((64, LOCAL), F32)
PACKED = ((FRAMES, ROWS // 2, 128), BF)


def attend(name, got, blocks, arrays, state=(), last=False, flops=10**9):
    first = not state
    outs = (PACKED, GRADS, LINE) if last else (WIDE, LINE) + ((QUERIES,) if first else ())
    scratch = ((WIDE, LINE) if last else ()) + (((2, len(blocks) * TILE, TILE), F32),)
    return call(
        functools.partial(forward_kernel, blocks, first, last), name, outs, (got,) + tuple(arrays) + tuple(state),
        scalars=0, scratch=scratch, flops=flops, nbytes=10**5,
    )


def attend_back(name, got, grad, ot, lse, offsets, arrays, state=(), flops=10**8):
    first, blocks = not state, ((len(offsets), LOCAL, 128), BF)
    flat = ((LOCAL, 128), BF)
    outs = (blocks, blocks) + ((GRADS, QUERIES, flat, QUERIES, flat, LINE) if first else (PACKED,))
    scratch = (() if first else (GRADS,)) + (((2, 2 * TILE, TILE), F32),)
    return call(
        functools.partial(backward_kernel, offsets, first), name, outs, (got, grad, ot, lse) + tuple(arrays) + tuple(state),
        scalars=0, scratch=scratch, megabytes=28, flops=flops, nbytes=10**5,
    )


PIECES = ((64, 56, 128), BF)
MIXED = (((512, 1536), F32), ((TYPES, 512), F32), ((1, 512), F32), ((1, 512), F32))


def spread(pieces):
    hbm = pl.BlockSpec(memory_space=pltpu.HBM)
    return pl.pallas_call(
        spread_kernel,
        out_shape=tuple(jax.ShapeDtypeStruct(shape, F32) for shape in ((2048, 512), (512, 2048), (512, 512))),
        in_specs=[hbm] * 8,
        out_specs=(hbm,) * 3,
        scratch_shapes=[
            pltpu.VMEM((8, PIECE_ROWS, 128), BF),
            pltpu.VMEM((8, 256, 512), F32),
            pltpu.VMEM((8, 512, 256), F32),
            pltpu.VMEM((8, 256, 128), F32),
            pltpu.SemaphoreType.DMA((8,)),
            pltpu.SemaphoreType.DMA((24,)),
        ],
        compiler_params=pltpu.CompilerParams(vmem_limit_bytes=40 * 2**20),
        cost_estimate=pl.CostEstimate(flops=10**7, bytes_accessed=15 * 2**20, transcendentals=0),
        name="spread",
    )(*pieces)


def swap(array, axes):
    return lax.all_to_all(array, axes, 0, 0, tiled=True)


def partner(array):
    return lax.ppermute(array, "c", [(0, 1), (1, 0)])


def along(array, step):
    return lax.ppermute(array, "z", [(place, (place - step) % 4) for place in range(4)])


def angle_tables():
    rates = BASE ** (-np.arange(HEAD_DIM // 2, dtype=np.float64) / (HEAD_DIM // 2))
    rates = np.tile(rates, 4)
    tables = []
    for places in (np.arange(128) * ROWS, np.arange(ROWS)):
        angles = places[:, None] * rates[None, :]
        tables.append(np.concatenate([np.cos(angles), np.sin(angles)], axis=1).astype(np.float32))
    return tables


def local(
    tokens, type_ids, clip_ids, frame_mask, type_table, norm_gain, qkv_weight, out_weight, mlp_gain, up_weight, down_weight, cotangent
):
    base_table, row_table = (jnp.asarray(table) for table in angle_tables())
    gain_one, gain_two = norm_gain[None], mlp_gain[None]
    tokens_here = 2 * ROWS
    sent, start, low = call(
        pre_kernel, "pre", (((2 * HEADS, 112, 128), BF), ((tokens_here, 512), F32), ((tokens_here, 512), BF)),
        (clip_ids, frame_mask, tokens, type_ids, type_table, gain_one, qkv_weight, base_table, row_table),
        scalars=2, scratch=(((tokens_here, 1536), F32), ((16, 512), BF)), megabytes=60,
    )

    got = swap(sent, CHIPS)
    own = got[:, :ROWS].reshape(LOCAL, 128)
    own_other = partner(own)
    up, down, far = along(own, 1), along(own, 3), along(own, 2)
    *state, queries = attend("attend_near", got, ((0, 0), (1, 0)), (own, own_other), flops=2 * 10**10)
    clip_later, *state = lax.optimization_barrier((clip_ids, *state))
    one_of_each = clip_later[0] + clip_later[1] == 1
    up, one_of_each, *state = lax.optimization_barrier((up, one_of_each, *state))
    up_other = partner(up)
    state = attend("attend_up", got, ((0, 1),), (up,), (*state, queries), flops=10**8)
    down, far, *state = lax.optimization_barrier((down, far, *state))
    down_other = partner(down)
    state = attend("attend_up_down", got, ((1, 1), (0, 3)), (up_other, down), (*state, queries), flops=10**8)
    far_other = partner(far)
    state = attend("attend_down_far", got, ((1, 3), (0, 2)), (down_other, far), (*state, queries), flops=10**8)
    packed, out_t, lse = attend("attend_far", got, ((1, 2),), (far_other,), (*state, queries), last=True)

    heads_out = swap(packed, CHIPS)
    output, grad_packed, grad_mid, mlp_part, acts = call(
        mlp_kernel, "mlp",
        (((2, ROWS, 512), BF), ((2 * HEADS, ROWS // 2, 128), BF), ((tokens_here, 512), F32), ((1, 512), F32), ((2, tokens_here, ACT_WIDTH), BF)),
        (clip_ids, heads_out, start, cotangent, gain_two, out_weight, up_weight, down_weight),
        scratch=(((tokens_here, 512), BF), ((tokens_here, 2048), BF)), flops=3 * 10**9, nbytes=8 * 2**20, exps=300000,
    )
    theirs = partner(acts[1])
    pieces = call(weight_kernel, "weights", (((PIECE_ROWS, 128), BF),) * 4, (acts, theirs), scalars=0)
    pieces, grad_packed = lax.optimization_barrier((pieces, grad_packed))
    arrived = [along(piece, -step) for step, piece in enumerate(pieces) if step]
    grad_out = swap(grad_packed, CHIPS)
    dsame, dother, *back_state = attend_back(
        "attend_back_others", got, grad_out, out_t, lse, (2, 1, 3), (far, far_other, up, up_other, down, down_other)
    )
    arrived, back_state = lax.optimization_barrier((arrived, back_state))
    summed = (dsame.astype(F32) + partner(dother).astype(F32)).astype(BF)
    piece = sum((part.astype(F32) for part in arrived), pieces[0].astype(F32)).astype(BF)
    piece, summed = lax.optimization_barrier((piece, summed))
    moved = [along(summed[at], -offset) for at, offset in enumerate((2, 1, 3))]
    piece = jnp.sum(swap(piece.reshape(16, PIECE_ROWS // 16, 128), CHIPS).astype(F32), axis=0).astype(BF)
    piece, back_state = lax.optimization_barrier((piece, back_state))
    near_same, near_other, dq = attend_back("attend_back_near", got, grad_out, out_t, lse, (0,), (own, own_other), back_state)
    near_sum = near_same[0].astype(F32) + partner(near_other[0]).astype(F32)
    own_grad = sum((part.astype(F32) for part in moved), near_sum).astype(BF)

    spread_piece = jnp.broadcast_to(piece[None], (16, PIECE_ROWS // 16, 128))
    back = swap(jnp.concatenate([own_grad.reshape(FRAMES, ROWS, 128), dq, spread_piece], axis=1), CHIPS)
    piece = back[:, ROWS + ROWS // 2 :].reshape(PIECE_ROWS, 128)
    pieces = [piece] + [along(piece, step) for step in (1, 2, 3)]

    def ending(grads):
        (mix_acts,) = call(
            turn_back_kernel, "turn_back", (((2, tokens_here, 512 + QKV_HALF), BF),), (grads, low, base_table, row_table), scalars=0
        )
        input_grad, small = call(
            post_kernel, "post", (((2, ROWS, 512), F32), ((8, 512), F32)),
            (clip_ids, mix_acts, start, grad_mid, type_ids, mlp_part, gain_one, qkv_weight),
        )
        (strips_out,) = call(mix_weight_kernel, "mix_weights", (PIECES,), (mix_acts, partner(mix_acts[1]), small), scalars=0)
        return input_grad, *call(total_kernel, "total", (PIECES,), (swap(strips_out, ("y", "x", "z")),), scalars=0)

    def nothing(grads):
        return jnp.zeros((2, ROWS, 512), F32), jnp.zeros(*PIECES)

    input_grad, totals = lax.cond(one_of_each, ending, nothing, back)
    totals, pieces = lax.optimization_barrier((totals, pieces))
    mixed = swap(totals, ("y", "x", "z"))
    sums = spread(pieces + [partner(piece) for piece in pieces])
    mixed, sums = lax.optimization_barrier((mixed, sums))
    qkv_sum, table_sum, gain_one_sum, gain_two_sum = call(mix_sum_kernel, "mix_sums", MIXED, (mixed, partner(mixed)), scalars=0)
    down_sum, up_sum, out_sum = sums
    return (output, input_grad, table_sum, gain_one_sum[0], qkv_sum, out_sum, gain_two_sum[0], up_sum, down_sum)


def solution(mesh):
    chips = Mesh(mesh.devices.reshape(4, 4, 2, 4), ("y", "x", "c", "z"))
    tm = ("y", "x", "c")
    rows = P(tm, "z", None)
    in_specs = (rows, P(tm, "z"), P(tm), P(tm)) + (P(),) * 7 + (rows,)
    out_specs = (rows, rows) + (P(),) * 7
    return jax.shard_map(local, mesh=chips, in_specs=in_specs, out_specs=out_specs, check_vma=False)
```

```python
import functools

import jax
import jax.numpy as jnp
import numpy as np
from jax import lax
from jax.experimental import pallas as pl
from jax.experimental.pallas import tpu as pltpu
from jax.sharding import Mesh
from jax.sharding import PartitionSpec as P

HEADS = 8
HEAD_DIM = 64
TYPES = 3
TILE = 256
FRAMES = 16
ROWS = 64
LOCAL = FRAMES * ROWS
GROUPS = LOCAL // TILE
MASKED = -1e30
ONES = 16
EPS = 1e-05
BASE = 10000.0
BF = jnp.bfloat16
F32 = jnp.float32
CHIPS = ("y", "x")


def mm(a, b):
    return jnp.dot(a, b, preferred_element_type=F32)


def mm_t(a, b):
    return lax.dot_general(a, b, (((0,), (0,)), ((), ())), preferred_element_type=F32)


def write_biases(bias_ref, at, is_other, key_block, row_block, parity, full):
    key = lax.broadcasted_iota(jnp.int32, (TILE, TILE), 0)
    query = lax.broadcasted_iota(jnp.int32, (TILE, TILE), 1)
    late = jnp.where(full, 0.0, MASKED)
    if is_other:
        before = key // ROWS < query // ROWS + parity
        bias_ref[0, at : at + TILE, :] = jnp.where(before, 0.0, MASKED)
        bias_ref[1, at : at + TILE, :] = jnp.where(before, late, MASKED)
        return
    before = key // ROWS < query // ROWS
    row_shift = jnp.where(key_block == row_block, 0, jnp.where(key_block < row_block, ROWS, -ROWS))
    own = (key // ROWS == query // ROWS) & ((key % ROWS) <= (query % ROWS) + row_shift)
    bias_ref[0, at : at + TILE, :] = jnp.where(before | own, 0.0, MASKED)
    bias_ref[1, at : at + TILE, :] = jnp.where(own, 0.0, jnp.where(before, late, MASKED))


def key_tiles(arrays, kb):
    return jnp.concatenate([array[pl.ds(kb * TILE, TILE), :] for array in arrays], axis=0)


def biased(scores, bias_ref, kb):
    bias = bias_ref[0 if kb == 0 else 1]
    if scores.shape[1] == TILE:
        return scores + bias
    return jnp.concatenate([scores[:, :TILE] + bias, scores[:, TILE:]], axis=1)


def strips(full, tile):
    @pl.when(full)
    def _():
        for kb in range(GROUPS):
            tile(kb, LOCAL - kb * TILE)

    @pl.when(jnp.logical_not(full))
    def _():
        for kb in range(GROUPS):
            tile(kb, TILE if kb else LOCAL)


def unfold_pair(first, second):
    return jnp.concatenate([first[:, :HEAD_DIM], first[:, HEAD_DIM:], second[:, :HEAD_DIM], second[:, HEAD_DIM:]], axis=0)


def forward_kernel(blocks, first, last, got_ref, *refs):
    arrays, rest = refs[: len(blocks)], refs[len(blocks) :]
    if first:
        acc_ref, top_ref, qt_ref, bias_ref = rest
        top_ref[...] = jnp.full(top_ref.shape, MASKED, F32)
        acc_ref[...] = jnp.zeros(acc_ref.shape, F32)
        write_queries(got_ref, qt_ref)
    else:
        in_acc, in_top, qt_ref = rest[:3]
        acc_ref, top_ref, bias_ref = rest[6:] if last else rest[3:]
        top_ref[...] = in_top[...]
        acc_ref[...] = in_acc[...]
    full, row_block, parity = places(got_ref)
    for place, (is_other, offset) in enumerate(blocks):
        write_biases(bias_ref, place * TILE, is_other, lax.rem(row_block + offset, 4), row_block, parity, full)

    def tile(kb, width):
        cols = pl.ds(kb * TILE, width)
        keys = key_tiles(arrays, kb)
        values = jnp.concatenate([jnp.ones((ONES, keys.shape[0]), BF), keys.T[HEAD_DIM:]], axis=0)
        scores = biased(mm(keys, qt_ref[:, cols]), bias_ref, kb)
        top_old = top_ref[:, cols]
        top_new = jnp.maximum(top_old, jnp.max(scores, axis=0, keepdims=True))
        weights = jnp.exp(scores - top_new).astype(BF)
        acc_ref[:, cols] = acc_ref[:, cols] * jnp.exp(top_old - top_new) + mm(values, weights)
        top_ref[:, cols] = top_new

    strips(full, tile)
    if last:
        packed_ref, ot_ref, lse_ref = rest[3:6]
        total = acc_ref[0:1, :]
        out_t = acc_ref[ONES:, :] / total
        ot_ref[...] = out_t
        lse_ref[...] = top_ref[...] + jnp.log(total)
        pack_frames(out_t.astype(BF), packed_ref)


def places(got_ref):
    full = jnp.max(got_ref[FRAMES - 1, ROWS + ROWS // 2 :, :].astype(F32)) > 0.5
    return full, lax.axis_index("z"), lax.axis_index("c")


def pack_frames(flipped, packed_ref):
    half = ROWS // 2
    for pair in range(FRAMES // 2):
        part = flipped[:, pair * 128 : (pair + 1) * 128].T
        packed_ref[2 * pair] = jnp.concatenate([part[:half], part[half:ROWS]], axis=1)
        packed_ref[2 * pair + 1] = jnp.concatenate([part[ROWS : ROWS + half], part[ROWS + half :]], axis=1)


def write_queries(got_ref, qt_ref):
    for pair in range(FRAMES // 2):
        rows = unfold_pair(got_ref[2 * pair, ROWS : ROWS + ROWS // 2, :], got_ref[2 * pair + 1, ROWS : ROWS + ROWS // 2, :])
        qt_ref[:HEAD_DIM, pair * 128 : (pair + 1) * 128] = rows.T
    qt_ref[HEAD_DIM:, :] = jnp.zeros((HEAD_DIM, LOCAL), BF)


def backward_kernel(offsets, first, got_ref, grad_ref, ot_ref, lse_ref, *refs):
    arrays, rest = refs[: 2 * len(offsets)], refs[2 * len(offsets) :]
    if first:
        dsame_ref, dother_ref, dqt_ref, qt_ref, q_ref, dot_ref, do_ref, delta_ref, bias_ref = rest
        write_queries(got_ref, qt_ref)
        blank = jnp.zeros((2 * ROWS, HEAD_DIM), BF)
        for pair in range(FRAMES // 2):
            span = pl.ds(pair * 128, 128)
            query = unfold_pair(got_ref[2 * pair, ROWS : ROWS + ROWS // 2, :], got_ref[2 * pair + 1, ROWS : ROWS + ROWS // 2, :])
            grad = unfold_pair(grad_ref[2 * pair], grad_ref[2 * pair + 1])
            q_ref[span, :] = jnp.concatenate([query, blank], axis=1)
            do_ref[span, :] = jnp.concatenate([blank, grad], axis=1)
            dot_ref[HEAD_DIM:, pair * 128 : (pair + 1) * 128] = grad.T
        dot_ref[:HEAD_DIM, :] = jnp.zeros((HEAD_DIM, LOCAL), BF)
        delta_ref[...] = jnp.sum(dot_ref[HEAD_DIM:, :].astype(F32) * ot_ref[...], axis=0, keepdims=True)
        dqt_ref[...] = jnp.zeros(dqt_ref.shape, F32)
    else:
        in_dqt, qt_ref, q_ref, dot_ref, do_ref, delta_ref, dsame_ref, dother_ref, packed_ref, dqt_ref, bias_ref = rest
        dqt_ref[...] = in_dqt[...]
    full, row_block, parity = places(got_ref)
    for block, offset in enumerate(offsets):
        key_block = lax.rem(row_block + offset, 4)
        for is_other in range(2):
            write_biases(bias_ref, is_other * TILE, is_other, key_block, row_block, parity, full)

        def tile(kb, width):
            cols = pl.ds(kb * TILE, width)
            rows = pl.ds(kb * TILE, TILE)
            keys = key_tiles(arrays[2 * block : 2 * block + 2], kb)
            scores = biased(mm(keys, qt_ref[:, cols]), bias_ref, kb)
            weights = jnp.exp(scores - lse_ref[:, cols])
            slopes = (weights * (mm(keys, dot_ref[:, cols]) - delta_ref[:, cols])).astype(BF)
            dqt_ref[:, cols] += mm(keys[:, :HEAD_DIM].T, slopes)
            both = mm(slopes, q_ref[cols, :]) + mm(weights.astype(BF), do_ref[cols, :])
            dsame_ref[block, rows, :] = both[:TILE, :].astype(BF)
            dother_ref[block, rows, :] = both[TILE:, :].astype(BF)

        strips(full, tile)
    if not first:
        pack_frames((dqt_ref[...] * HEAD_DIM**-0.5).astype(BF), packed_ref)


def norm_parts(hidden):
    centre = jnp.mean(hidden, axis=-1, keepdims=True)
    shifted = hidden - centre
    spread = jnp.mean(shifted * shifted, axis=-1, keepdims=True)
    inverse = lax.rsqrt(spread + EPS)
    return shifted * inverse, inverse


def norm_back(raised, unit, inverse):
    mean = jnp.mean(raised, axis=-1, keepdims=True)
    along = jnp.mean(raised * unit, axis=-1, keepdims=True)
    return (raised - mean - unit * along) * inverse


def turns(base_ref, row_ref):
    place = lax.axis_index(("y", "x", "c")) * 4 + lax.axis_index("z")
    base = base_ref[pl.ds(place, 1), :]
    cos_base, sin_base = base[:, :128], base[:, 128:]
    cos_row, sin_row = row_ref[:, :128], row_ref[:, 128:]
    cosine = cos_base * cos_row - sin_base * sin_row
    sine = sin_base * cos_row + cos_base * sin_row
    first = lax.broadcasted_iota(jnp.int32, sine.shape, 1) % HEAD_DIM < HEAD_DIM // 2
    return cosine, jnp.where(first, -sine, sine)


def turn(pair, cosine, sine):
    half = HEAD_DIM // 2
    first = lax.broadcasted_iota(jnp.int32, pair.shape, 1) % HEAD_DIM < half
    crossed = jnp.where(first, pltpu.roll(pair, 128 - half, 1), pltpu.roll(pair, half, 1))
    return pair * cosine + crossed * sine


def pre_kernel(clip_ref, mask_ref, tok_ref, type_ref, table_ref, gain_ref, w_ref, base_ref, row_ref, sent_ref, start_ref, low_ref, mixed_ref, kinds_ref):
    swapped = clip_ref[0]
    cosine, sine = turns(base_ref, row_ref)
    kinds_ref[...] = jnp.zeros(kinds_ref.shape, BF)
    kinds_ref[:TYPES, :] = table_ref[...]
    for clip in range(2):
        slot = jnp.where(swapped > 0, 1 - clip, clip)
        kinds = type_ref[pl.ds(slot, 1), :]
        onehot = (lax.broadcasted_iota(jnp.int32, (16, ROWS), 0) == kinds).astype(F32).astype(BF)
        hidden = tok_ref[slot].astype(F32) + mm_t(onehot, kinds_ref[...])
        unit, _ = norm_parts(hidden)
        start_ref[clip * ROWS : (clip + 1) * ROWS, :] = hidden
        low_ref[clip * ROWS : (clip + 1) * ROWS, :] = (unit * gain_ref[...]).astype(BF)
    width = 512
    for third in range(3):
        mixed_ref[:, third * width : (third + 1) * width] = mm(low_ref[...], w_ref[:, third * width : (third + 1) * width])
    for clip in range(2):
        slot = jnp.where(swapped > 0, 1 - clip, clip)
        rows = slice(clip * ROWS, (clip + 1) * ROWS)
        real = jnp.full((16, 128), mask_ref[slot], jnp.int32).astype(F32).astype(BF)
        for pair in range(HEADS // 2):
            query = (turn(mixed_ref[rows, pair * 128 : (pair + 1) * 128], cosine, sine).astype(BF) * HEAD_DIM**-0.5).astype(BF)
            key = turn(mixed_ref[rows, width + pair * 128 : width + (pair + 1) * 128], cosine, sine).astype(BF)
            value = mixed_ref[rows, 2 * width + pair * 128 : 2 * width + (pair + 1) * 128].astype(BF)
            for side in range(2):
                to = (2 * pair + side) * 2 + clip
                lanes = slice(side * HEAD_DIM, (side + 1) * HEAD_DIM)
                sent_ref[to, :ROWS, :] = jnp.concatenate([key[:, lanes], value[:, lanes]], axis=1)
                sent_ref[to, ROWS : ROWS + ROWS // 2, :] = jnp.concatenate([query[: ROWS // 2, lanes], query[ROWS // 2 :, lanes]], axis=1)
                sent_ref[to, ROWS + ROWS // 2 :, :] = real


def mm_nt(a, b):
    return lax.dot_general(a, b, (((1,), (1,)), ((), ())), preferred_element_type=F32)


FF_PART = 512
GELU_SCALE = float(np.sqrt(2.0 / np.pi))
GELU_CUBE = 0.044715
G_AT, DU_AT, N2_AT, DY_AT, AT_AT, DA_AT, ACT_WIDTH = 0, 1024, 2048, 2560, 3072, 3328, 3840


def mlp_kernel(
    clip_ref, got_ref, start_ref, cot_ref, gain_ref, wo_ref, wu_ref, wd_ref, out_ref, packed_ref, mid_ref, gaing_ref, acts_ref,
    attn_ref, slope_ref,
):
    swapped, core = clip_ref[0], lax.axis_index("c")
    keep, send = 0, 1
    for clip in range(2):
        for pair in range(HEADS // 2):
            one, two = got_ref[4 * pair + clip], got_ref[4 * pair + 2 + clip]
            attn_ref[clip * ROWS : clip * ROWS + ROWS // 2, pair * 128 : (pair + 1) * 128] = jnp.concatenate([one[:, :HEAD_DIM], two[:, :HEAD_DIM]], axis=1)
            attn_ref[clip * ROWS + ROWS // 2 : (clip + 1) * ROWS, pair * 128 : (pair + 1) * 128] = jnp.concatenate([one[:, HEAD_DIM:], two[:, HEAD_DIM:]], axis=1)
    slots = [jnp.where(swapped > 0, 1 - clip, clip) for clip in range(2)]
    grad_low = jnp.concatenate([cot_ref[slots[0]], cot_ref[slots[1]]], axis=0)
    attn = attn_ref[...]
    middle = start_ref[...] + mm(attn, wo_ref[...])
    unit, inverse = norm_parts(middle)
    low = (unit * gain_ref[...]).astype(BF)
    final = middle
    for part in range(4):
        cols = slice(part * FF_PART, (part + 1) * FF_PART)
        upper = mm(low, wu_ref[:, cols])
        square = upper * upper
        bend = jnp.tanh(GELU_SCALE * (upper + GELU_CUBE * (square * upper)))
        act = (0.5 * upper * (1.0 + bend)).astype(BF)
        rise = 0.5 * (1.0 + bend) + 0.5 * upper * (1.0 - bend * bend) * (GELU_SCALE * (1.0 + 3.0 * GELU_CUBE * square))
        final = final + mm(act, wd_ref[cols, :])
        slope = (mm_nt(grad_low, wd_ref[cols, :]) * rise).astype(BF)
        slope_ref[:, cols] = slope
        side = jnp.where(core == part // 2, keep, send)
        at = (part % 2) * FF_PART
        acts_ref[side, :, G_AT + at : G_AT + at + FF_PART] = act
        acts_ref[side, :, DU_AT + at : DU_AT + at + FF_PART] = slope
    for clip in range(2):
        out_ref[slots[clip]] = final[clip * ROWS : (clip + 1) * ROWS].astype(BF)
    down = mm_nt(slope_ref[...], wu_ref[...])
    gaing_ref[...] = jnp.sum(down * unit, axis=0, keepdims=True)
    grad_mid = grad_low.astype(F32) + norm_back(down * gain_ref[...], unit, inverse)
    mid_ref[...] = grad_mid
    grad_mid_low = grad_mid.astype(BF)
    grad_attn = mm_nt(grad_mid_low, wo_ref[...]).astype(BF)
    for side in (keep, send):
        acts_ref[side, :, N2_AT : N2_AT + 512] = low
        acts_ref[side, :, DY_AT : DY_AT + 512] = grad_low
        acts_ref[side, :, DA_AT : DA_AT + 512] = grad_mid_low
    for half in range(2):
        acts_ref[jnp.where(core == half, keep, send), :, AT_AT : AT_AT + 256] = attn[:, half * 256 : (half + 1) * 256]
    for clip in range(2):
        for pair in range(HEADS // 2):
            rows = grad_attn[clip * ROWS : (clip + 1) * ROWS, pair * 128 : (pair + 1) * 128]
            upper_rows, lower_rows = rows[: ROWS // 2], rows[ROWS // 2 :]
            packed_ref[4 * pair + clip] = jnp.concatenate([upper_rows[:, :HEAD_DIM], lower_rows[:, :HEAD_DIM]], axis=1)
            packed_ref[4 * pair + 2 + clip] = jnp.concatenate([upper_rows[:, HEAD_DIM:], lower_rows[:, HEAD_DIM:]], axis=1)


UP_AT, OUT_AT, PIECE_ROWS = 1024, 2048, 2304


def weight_kernel(acts_ref, theirs_ref, *piece_refs):
    block = lax.axis_index("z")

    def both(at, width):
        return jnp.concatenate([acts_ref[0, :, pl.ds(at, width)], theirs_ref[:, pl.ds(at, width)]], axis=0)

    grad_low, low, attn = both(DY_AT, 512), both(N2_AT, 512), both(AT_AT, 256)
    for step, piece_ref in enumerate(piece_refs):
        piece = lax.rem(block + step, 4)
        units = pl.multiple_of(piece * 256, 256)
        down = mm_t(both(G_AT + units, 256), grad_low).astype(BF)
        for part in range(4):
            piece_ref[part * 256 : (part + 1) * 256, :] = down[:, part * 128 : (part + 1) * 128]
        up = mm_t(low, both(DU_AT + units, 256)).astype(BF)
        for part in range(2):
            piece_ref[UP_AT + part * 512 : UP_AT + (part + 1) * 512, :] = up[:, part * 128 : (part + 1) * 128]
        piece_ref[OUT_AT:, :] = mm_t(attn, both(DA_AT + pl.multiple_of(piece * 128, 128), 128)).astype(BF)


QKV_HALF = 768


def turn_back_kernel(back_ref, low_ref, base_ref, row_ref, acts_ref):
    core = lax.axis_index("c")
    cosine, sine = turns(base_ref, row_ref)
    half = ROWS // 2

    def unpack(one, two):
        upper_rows = jnp.concatenate([one[:, :HEAD_DIM], two[:, :HEAD_DIM]], axis=1)
        lower_rows = jnp.concatenate([one[:, HEAD_DIM:], two[:, HEAD_DIM:]], axis=1)
        return jnp.concatenate([upper_rows, lower_rows], axis=0)

    def write(rows, cols, value):
        side = jnp.where(core == cols // QKV_HALF, 0, 1)
        at = 512 + cols % QKV_HALF
        acts_ref[side, rows, at : at + 128] = value

    for clip in range(2):
        rows = slice(clip * ROWS, (clip + 1) * ROWS)
        for pair in range(HEADS // 2):
            one, two = 4 * pair + clip, 4 * pair + 2 + clip
            query = unpack(back_ref[one, ROWS : ROWS + half, :], back_ref[two, ROWS : ROWS + half, :]).astype(F32)
            first, second = back_ref[one, :ROWS, :], back_ref[two, :ROWS, :]
            key = jnp.concatenate([first[:, :HEAD_DIM], second[:, :HEAD_DIM]], axis=1).astype(F32)
            cols = pair * 128
            write(rows, cols, turn(query, cosine, -sine).astype(BF))
            write(rows, 512 + cols, turn(key, cosine, -sine).astype(BF))
            write(rows, 1024 + cols, jnp.concatenate([first[:, HEAD_DIM:], second[:, HEAD_DIM:]], axis=1))
    for side in range(2):
        acts_ref[side, :, :512] = low_ref[...]


def post_kernel(clip_ref, acts_ref, start_ref, mid_ref, type_ref, mlp_ref, gain_ref, w_ref, grad_ref, small_ref):
    swapped, core = clip_ref[0], lax.axis_index("c")
    down = jnp.zeros((2 * ROWS, 512), F32)
    for part in range(2):
        raw = acts_ref[jnp.where(core == part, 0, 1), :, 512:]
        down = down + mm_nt(raw, w_ref[:, part * QKV_HALF : (part + 1) * QKV_HALF])
    unit, inverse = norm_parts(start_ref[...])
    grad = mid_ref[...] + norm_back(down * gain_ref[...], unit, inverse)
    gain_grad = jnp.sum(down * unit, axis=0, keepdims=True)
    table = jnp.zeros((8, 512), F32)
    for clip in range(2):
        slot = jnp.where(swapped > 0, 1 - clip, clip)
        part = grad[clip * ROWS : (clip + 1) * ROWS]
        grad_ref[slot] = part
        kinds = type_ref[pl.ds(slot, 1), :]
        onehot = (lax.broadcasted_iota(jnp.int32, (8, ROWS), 0) == kinds).astype(F32)
        table = table + jnp.dot(onehot, part, precision=lax.Precision.HIGHEST, preferred_element_type=F32)
    row = lax.broadcasted_iota(jnp.int32, (8, 512), 0)
    small_ref[...] = jnp.where(row == 3, gain_grad, jnp.where(row == 4, mlp_ref[...], table))


def mix_weight_kernel(acts_ref, theirs_ref, small_ref, pieces_ref):
    low = jnp.concatenate([acts_ref[0, :, :512], theirs_ref[:, :512]], axis=0)
    raw = jnp.concatenate([acts_ref[0, :, 512:], theirs_ref[:, 512:]], axis=0)
    small = small_ref[...]
    for side in range(2):
        grad = mm_t(low, raw[:, side * 384 : (side + 1) * 384]).astype(BF)
        for strip in range(32):
            for part in range(3):
                block = grad[strip * 16 : (strip + 1) * 16, part * 128 : (part + 1) * 128]
                pieces_ref[2 * strip + side, part * 16 : (part + 1) * 16, :] = block
    for place in range(64):
        row, part = place // 4, place % 4
        value = jnp.zeros((8, 128), F32)
        if row < 5:
            value = jnp.broadcast_to(small[row : row + 1, part * 128 : (part + 1) * 128], (8, 128))
        pieces_ref[place, 48:, :] = value.astype(BF)


def total_kernel(pieces_ref, copies_ref):
    total = pieces_ref[0].astype(F32)
    for place in range(1, 64):
        total = total + pieces_ref[place].astype(F32)
    low = total.astype(BF)
    for place in range(64):
        copies_ref[place] = low


def mix_sum_kernel(own_ref, theirs_ref, qkv_ref, table_ref, gain_one_ref, gain_two_ref):
    core = lax.axis_index("c")
    for half in range(2):

        def write(pieces_ref):
            for place in range(64):
                strip, side = place // 2, place % 2
                cols = half * QKV_HALF + side * 384
                for part in range(3):
                    block = pieces_ref[place, part * 16 : (part + 1) * 16, :].astype(F32)
                    qkv_ref[strip * 16 : (strip + 1) * 16, cols + part * 128 : cols + (part + 1) * 128] = block

        pl.when(core == half)(functools.partial(write, own_ref))
        pl.when(core != half)(functools.partial(write, theirs_ref))
    for row in range(5):
        target, line = ((table_ref, row), (table_ref, row), (table_ref, row), (gain_one_ref, 0), (gain_two_ref, 0))[row]
        for part in range(4):
            both = own_ref[4 * row + part, 48:, :].astype(F32) + theirs_ref[4 * row + part, 48:, :].astype(F32)
            target[line : line + 1, part * 128 : (part + 1) * 128] = both[0:1]


def spread_kernel(*refs):
    pieces, (down, up, out, low, down_stage, up_stage, out_stage, in_sems, out_sems) = refs[:8], refs[8:]
    reads = [pltpu.make_async_copy(piece, low.at[at], in_sems.at[at]) for at, piece in enumerate(pieces)]
    for read in reads:
        read.start()
    writes = []

    def write(source, target):
        writes.append(pltpu.make_async_copy(source, target, out_sems.at[len(writes)]))
        writes[-1].start()

    for at, read in enumerate(reads):
        read.wait()
        core = lax.axis_index("c") if at < 4 else 1 - lax.axis_index("c")
        piece = lax.rem(lax.axis_index("z") + at, 4)
        units = pl.ds(pl.multiple_of(core * 1024 + piece * 256, 256), 256)
        for part in range(4):
            down_stage[at, :, part * 128 : (part + 1) * 128] = low[at, part * 256 : (part + 1) * 256, :].astype(F32)
        write(down_stage.at[at], down.at[units, :])
        for part in range(2):
            up_stage[at, :, part * 128 : (part + 1) * 128] = low[at, UP_AT + part * 512 : UP_AT + (part + 1) * 512, :].astype(F32)
        write(up_stage.at[at], up.at[:, units])
        out_stage[at] = low[at, OUT_AT:, :].astype(F32)
        write(out_stage.at[at], out.at[pl.ds(core * 256, 256), pl.ds(pl.multiple_of(piece * 128, 128), 128)])
    for copy in writes:
        copy.wait()


VMEM_SPEC = pl.BlockSpec(memory_space=pltpu.VMEM)
SMEM_SPEC = pl.BlockSpec(memory_space=pltpu.SMEM)


def call(kernel, name, outs, args, scalars=1, scratch=(), megabytes=28, flops=10**9, nbytes=4 * 2**20, exps=0):
    shapes = tuple(jax.ShapeDtypeStruct(shape, dtype) for shape, dtype in outs)
    return pl.pallas_call(
        kernel,
        out_shape=shapes,
        in_specs=[SMEM_SPEC] * scalars + [VMEM_SPEC] * (len(args) - scalars),
        out_specs=(VMEM_SPEC,) * len(shapes),
        scratch_shapes=[pltpu.VMEM(shape, dtype) for shape, dtype in scratch],
        compiler_params=pltpu.CompilerParams(vmem_limit_bytes=megabytes * 2**20),
        cost_estimate=pl.CostEstimate(flops=flops, bytes_accessed=nbytes, transcendentals=exps),
        name=name,
    )(*args)


WIDE = ((ONES + HEAD_DIM, LOCAL), F32)
LINE = ((1, LOCAL), F32)


QUERIES = ((128, LOCAL), BF)
GRADS = ((64, LOCAL), F32)
PACKED = ((FRAMES, ROWS // 2, 128), BF)


def attend(name, got, blocks, arrays, state=(), last=False, flops=10**9):
    first = not state
    outs = (PACKED, GRADS, LINE) if last else (WIDE, LINE) + ((QUERIES,) if first else ())
    scratch = ((WIDE, LINE) if last else ()) + (((2, len(blocks) * TILE, TILE), F32),)
    return call(
        functools.partial(forward_kernel, blocks, first, last), name, outs, (got,) + tuple(arrays) + tuple(state),
        scalars=0, scratch=scratch, flops=flops, nbytes=10**5,
    )


def attend_back(name, got, grad, ot, lse, offsets, arrays, state=(), flops=10**8):
    first, blocks = not state, ((len(offsets), LOCAL, 128), BF)
    flat = ((LOCAL, 128), BF)
    outs = (blocks, blocks) + ((GRADS, QUERIES, flat, QUERIES, flat, LINE) if first else (PACKED,))
    scratch = (() if first else (GRADS,)) + (((2, 2 * TILE, TILE), F32),)
    return call(
        functools.partial(backward_kernel, offsets, first), name, outs, (got, grad, ot, lse) + tuple(arrays) + tuple(state),
        scalars=0, scratch=scratch, megabytes=28, flops=flops, nbytes=10**5,
    )


PIECES = ((64, 56, 128), BF)
MIXED = (((512, 1536), F32), ((TYPES, 512), F32), ((1, 512), F32), ((1, 512), F32))


def spread(pieces):
    hbm = pl.BlockSpec(memory_space=pltpu.HBM)
    return pl.pallas_call(
        spread_kernel,
        out_shape=tuple(jax.ShapeDtypeStruct(shape, F32) for shape in ((2048, 512), (512, 2048), (512, 512))),
        in_specs=[hbm] * 8,
        out_specs=(hbm,) * 3,
        scratch_shapes=[
            pltpu.VMEM((8, PIECE_ROWS, 128), BF),
            pltpu.VMEM((8, 256, 512), F32),
            pltpu.VMEM((8, 512, 256), F32),
            pltpu.VMEM((8, 256, 128), F32),
            pltpu.SemaphoreType.DMA((8,)),
            pltpu.SemaphoreType.DMA((24,)),
        ],
        compiler_params=pltpu.CompilerParams(vmem_limit_bytes=40 * 2**20),
        cost_estimate=pl.CostEstimate(flops=10**7, bytes_accessed=15 * 2**20, transcendentals=0),
        name="spread",
    )(*pieces)


def swap(array, axes):
    return lax.all_to_all(array, axes, 0, 0, tiled=True)


def partner(array):
    return lax.ppermute(array, "c", [(0, 1), (1, 0)])


def along(array, step):
    return lax.ppermute(array, "z", [(place, (place - step) % 4) for place in range(4)])


def angle_tables():
    rates = BASE ** (-np.arange(HEAD_DIM // 2, dtype=np.float64) / (HEAD_DIM // 2))
    rates = np.tile(rates, 4)
    tables = []
    for places in (np.arange(128) * ROWS, np.arange(ROWS)):
        angles = places[:, None] * rates[None, :]
        tables.append(np.concatenate([np.cos(angles), np.sin(angles)], axis=1).astype(np.float32))
    return tables


def local(
    tokens, type_ids, clip_ids, frame_mask, type_table, norm_gain, qkv_weight, out_weight, mlp_gain, up_weight, down_weight, cotangent
):
    base_table, row_table = (jnp.asarray(table) for table in angle_tables())
    gain_one, gain_two = norm_gain[None], mlp_gain[None]
    tokens_here = 2 * ROWS
    sent, start, low = call(
        pre_kernel, "pre", (((2 * HEADS, 112, 128), BF), ((tokens_here, 512), F32), ((tokens_here, 512), BF)),
        (clip_ids, frame_mask, tokens, type_ids, type_table, gain_one, qkv_weight, base_table, row_table),
        scalars=2, scratch=(((tokens_here, 1536), F32), ((16, 512), BF)), megabytes=60,
    )

    got = swap(sent, CHIPS)
    own = got[:, :ROWS].reshape(LOCAL, 128)
    own_other = partner(own)
    up, down = along(own, 1), along(own, 3)
    *state, queries = attend("attend_near", got, ((0, 0), (1, 0)), (own, own_other), flops=2 * 10**10)
    clip_later, *state = lax.optimization_barrier((clip_ids, *state))
    one_of_each = clip_later[0] + clip_later[1] == 1
    up, down, one_of_each, *state = lax.optimization_barrier((up, down, one_of_each, *state))
    up_other, down_other = partner(up), partner(down)
    halves = along(up[: LOCAL // 2], 1), along(down[LOCAL // 2 :], 3)
    state = attend("attend_same", got, ((0, 1), (0, 3)), (up, down), (*state, queries), flops=10**8)
    state = attend("attend_other", got, ((1, 1), (1, 3)), (up_other, down_other), (*state, queries), flops=10**8)
    halves, state = lax.optimization_barrier((halves, state))
    far = jnp.concatenate(halves, axis=0)
    far_other = partner(far)
    state = attend("attend_far_same", got, ((0, 2),), (far,), (*state, queries), flops=10**8)
    packed, out_t, lse = attend("attend_far", got, ((1, 2),), (far_other,), (*state, queries), last=True)

    heads_out = swap(packed, CHIPS)
    output, grad_packed, grad_mid, mlp_part, acts = call(
        mlp_kernel, "mlp",
        (((2, ROWS, 512), BF), ((2 * HEADS, ROWS // 2, 128), BF), ((tokens_here, 512), F32), ((1, 512), F32), ((2, tokens_here, ACT_WIDTH), BF)),
        (clip_ids, heads_out, start, cotangent, gain_two, out_weight, up_weight, down_weight),
        scratch=(((tokens_here, 512), BF), ((tokens_here, 2048), BF)), flops=3 * 10**9, nbytes=8 * 2**20, exps=300000,
    )
    theirs = partner(acts[1])
    pieces = call(weight_kernel, "weights", (((PIECE_ROWS, 128), BF),) * 4, (acts, theirs), scalars=0)
    pieces, grad_packed = lax.optimization_barrier((pieces, grad_packed))
    arrived = [along(piece, -step) for step, piece in enumerate(pieces) if step]
    grad_out = swap(grad_packed, CHIPS)
    dsame, dother, *back_state = attend_back(
        "attend_back_others", got, grad_out, out_t, lse, (2, 1, 3), (far, far_other, up, up_other, down, down_other)
    )
    arrived, back_state = lax.optimization_barrier((arrived, back_state))
    summed = (dsame.astype(F32) + partner(dother).astype(F32)).astype(BF)
    piece = sum((part.astype(F32) for part in arrived), pieces[0].astype(F32)).astype(BF)
    piece, summed = lax.optimization_barrier((piece, summed))
    moved = [along(summed[at], -offset) for at, offset in enumerate((2, 1, 3))]
    piece = jnp.sum(swap(piece.reshape(16, PIECE_ROWS // 16, 128), CHIPS).astype(F32), axis=0).astype(BF)
    piece, back_state = lax.optimization_barrier((piece, back_state))
    near_same, near_other, dq = attend_back("attend_back_near", got, grad_out, out_t, lse, (0,), (own, own_other), back_state)
    near_sum = near_same[0].astype(F32) + partner(near_other[0]).astype(F32)
    own_grad = sum((part.astype(F32) for part in moved), near_sum).astype(BF)

    spread_piece = jnp.broadcast_to(piece[None], (16, PIECE_ROWS // 16, 128))
    back = swap(jnp.concatenate([own_grad.reshape(FRAMES, ROWS, 128), dq, spread_piece], axis=1), CHIPS)
    piece = back[:, ROWS + ROWS // 2 :].reshape(PIECE_ROWS, 128)
    pieces = [piece, along(piece, 1), along(piece, 3)]

    def ending(grads):
        (mix_acts,) = call(
            turn_back_kernel, "turn_back", (((2, tokens_here, 512 + QKV_HALF), BF),), (grads, low, base_table, row_table), scalars=0
        )
        input_grad, small = call(
            post_kernel, "post", (((2, ROWS, 512), F32), ((8, 512), F32)),
            (clip_ids, mix_acts, start, grad_mid, type_ids, mlp_part, gain_one, qkv_weight),
        )
        (strips_out,) = call(mix_weight_kernel, "mix_weights", (PIECES,), (mix_acts, partner(mix_acts[1]), small), scalars=0)
        return input_grad, *call(total_kernel, "total", (PIECES,), (swap(strips_out, ("y", "x", "z")),), scalars=0)

    def nothing(grads):
        return jnp.zeros((2, ROWS, 512), F32), jnp.zeros(*PIECES)

    input_grad, totals = lax.cond(one_of_each, ending, nothing, back)
    totals, pieces = lax.optimization_barrier((totals, pieces))
    mixed = swap(totals, ("y", "x", "z"))
    halves = along(pieces[1][: PIECE_ROWS // 2], 1), along(pieces[2][PIECE_ROWS // 2 :], 3)
    pieces = [*pieces[:2], jnp.concatenate(halves, axis=0), pieces[2]]
    sums = spread(pieces + [partner(piece) for piece in pieces])
    mixed, sums = lax.optimization_barrier((mixed, sums))
    qkv_sum, table_sum, gain_one_sum, gain_two_sum = call(mix_sum_kernel, "mix_sums", MIXED, (mixed, partner(mixed)), scalars=0)
    down_sum, up_sum, out_sum = sums
    return (output, input_grad, table_sum, gain_one_sum[0], qkv_sum, out_sum, gain_two_sum[0], up_sum, down_sum)


def solution(mesh):
    chips = Mesh(mesh.devices.reshape(4, 4, 2, 4), ("y", "x", "c", "z"))
    tm = ("y", "x", "c")
    rows = P(tm, "z", None)
    in_specs = (rows, P(tm, "z"), P(tm), P(tm)) + (P(),) * 7 + (rows,)
    out_specs = (rows, rows) + (P(),) * 7
    return jax.shard_map(local, mesh=chips, in_specs=in_specs, out_specs=out_specs, check_vma=False)
```

```python
import functools

import jax
import jax.numpy as jnp
import numpy as np
from jax import lax
from jax.experimental import pallas as pl
from jax.experimental.pallas import tpu as pltpu
from jax.sharding import Mesh
from jax.sharding import PartitionSpec as P

HEADS = 8
HEAD_DIM = 64
TYPES = 3
TILE = 256
FRAMES = 16
ROWS = 64
LOCAL = FRAMES * ROWS
GROUPS = LOCAL // TILE
MASKED = -1e30
ONES = 16
EPS = 1e-05
BASE = 10000.0
BF = jnp.bfloat16
F32 = jnp.float32
CHIPS = ("y", "x")


def mm(a, b):
    return jnp.dot(a, b, preferred_element_type=F32)


def mm_t(a, b):
    return lax.dot_general(a, b, (((0,), (0,)), ((), ())), preferred_element_type=F32)


def write_biases(bias_ref, at, is_other, key_block, row_block, parity, full):
    key = lax.broadcasted_iota(jnp.int32, (TILE, TILE), 0)
    query = lax.broadcasted_iota(jnp.int32, (TILE, TILE), 1)
    late = jnp.where(full, 0.0, MASKED)
    if is_other:
        before = key // ROWS < query // ROWS + parity
        bias_ref[0, at : at + TILE, :] = jnp.where(before, 0.0, MASKED)
        bias_ref[1, at : at + TILE, :] = jnp.where(before, late, MASKED)
        return
    before = key // ROWS < query // ROWS
    row_shift = jnp.where(key_block == row_block, 0, jnp.where(key_block < row_block, ROWS, -ROWS))
    own = (key // ROWS == query // ROWS) & ((key % ROWS) <= (query % ROWS) + row_shift)
    bias_ref[0, at : at + TILE, :] = jnp.where(before | own, 0.0, MASKED)
    bias_ref[1, at : at + TILE, :] = jnp.where(own, 0.0, jnp.where(before, late, MASKED))


def key_tiles(arrays, kb):
    return jnp.concatenate([array[pl.ds(kb * TILE, TILE), :] for array in arrays], axis=0)


def biased(scores, bias_ref, kb):
    bias = bias_ref[0 if kb == 0 else 1]
    if scores.shape[1] == TILE:
        return scores + bias
    return jnp.concatenate([scores[:, :TILE] + bias, scores[:, TILE:]], axis=1)


def strips(full, tile):
    @pl.when(full)
    def _():
        for kb in range(GROUPS):
            tile(kb, LOCAL - kb * TILE)

    @pl.when(jnp.logical_not(full))
    def _():
        for kb in range(GROUPS):
            tile(kb, TILE if kb else LOCAL)


def unfold_pair(first, second):
    return jnp.concatenate([first[:, :HEAD_DIM], first[:, HEAD_DIM:], second[:, :HEAD_DIM], second[:, HEAD_DIM:]], axis=0)


def forward_kernel(blocks, first, last, got_ref, *refs):
    arrays, rest = refs[: len(blocks)], refs[len(blocks) :]
    if first:
        acc_ref, top_ref, qt_ref, bias_ref = rest
        top_ref[...] = jnp.full(top_ref.shape, MASKED, F32)
        acc_ref[...] = jnp.zeros(acc_ref.shape, F32)
        write_queries(got_ref, qt_ref)
    else:
        in_acc, in_top, qt_ref = rest[:3]
        acc_ref, top_ref, bias_ref = rest[6:] if last else rest[3:]
        top_ref[...] = in_top[...]
        acc_ref[...] = in_acc[...]
    full, row_block, parity = places(got_ref)
    for place, (is_other, offset) in enumerate(blocks):
        write_biases(bias_ref, place * TILE, is_other, lax.rem(row_block + offset, 4), row_block, parity, full)

    def tile(kb, width):
        cols = pl.ds(kb * TILE, width)
        keys = key_tiles(arrays, kb)
        values = jnp.concatenate([jnp.ones((ONES, keys.shape[0]), BF), keys.T[HEAD_DIM:]], axis=0)
        scores = biased(mm(keys, qt_ref[:, cols]), bias_ref, kb)
        top_old = top_ref[:, cols]
        top_new = jnp.maximum(top_old, jnp.max(scores, axis=0, keepdims=True))
        weights = jnp.exp(scores - top_new).astype(BF)
        acc_ref[:, cols] = acc_ref[:, cols] * jnp.exp(top_old - top_new) + mm(values, weights)
        top_ref[:, cols] = top_new

    strips(full, tile)
    if last:
        packed_ref, ot_ref, lse_ref = rest[3:6]
        total = acc_ref[0:1, :]
        out_t = acc_ref[ONES:, :] / total
        ot_ref[...] = out_t
        lse_ref[...] = top_ref[...] + jnp.log(total)
        pack_frames(out_t.astype(BF), packed_ref)


def places(got_ref):
    full = jnp.max(got_ref[FRAMES - 1, ROWS + ROWS // 2 :, :].astype(F32)) > 0.5
    return full, lax.axis_index("z"), lax.axis_index("c")


def pack_frames(flipped, packed_ref):
    half = ROWS // 2
    for pair in range(FRAMES // 2):
        part = flipped[:, pair * 128 : (pair + 1) * 128].T
        packed_ref[2 * pair] = jnp.concatenate([part[:half], part[half:ROWS]], axis=1)
        packed_ref[2 * pair + 1] = jnp.concatenate([part[ROWS : ROWS + half], part[ROWS + half :]], axis=1)


def write_queries(got_ref, qt_ref):
    for pair in range(FRAMES // 2):
        rows = unfold_pair(got_ref[2 * pair, ROWS : ROWS + ROWS // 2, :], got_ref[2 * pair + 1, ROWS : ROWS + ROWS // 2, :])
        qt_ref[:HEAD_DIM, pair * 128 : (pair + 1) * 128] = rows.T
    qt_ref[HEAD_DIM:, :] = jnp.zeros((HEAD_DIM, LOCAL), BF)


def backward_kernel(offsets, first, got_ref, grad_ref, ot_ref, lse_ref, *refs):
    arrays, rest = refs[: 2 * len(offsets)], refs[2 * len(offsets) :]
    if first:
        dsame_ref, dother_ref, dqt_ref, qt_ref, q_ref, dot_ref, do_ref, delta_ref, bias_ref = rest
        write_queries(got_ref, qt_ref)
        blank = jnp.zeros((2 * ROWS, HEAD_DIM), BF)
        for pair in range(FRAMES // 2):
            span = pl.ds(pair * 128, 128)
            query = unfold_pair(got_ref[2 * pair, ROWS : ROWS + ROWS // 2, :], got_ref[2 * pair + 1, ROWS : ROWS + ROWS // 2, :])
            grad = unfold_pair(grad_ref[2 * pair], grad_ref[2 * pair + 1])
            q_ref[span, :] = jnp.concatenate([query, blank], axis=1)
            do_ref[span, :] = jnp.concatenate([blank, grad], axis=1)
            dot_ref[HEAD_DIM:, pair * 128 : (pair + 1) * 128] = grad.T
        dot_ref[:HEAD_DIM, :] = jnp.zeros((HEAD_DIM, LOCAL), BF)
        delta_ref[...] = jnp.sum(dot_ref[HEAD_DIM:, :].astype(F32) * ot_ref[...], axis=0, keepdims=True)
        dqt_ref[...] = jnp.zeros(dqt_ref.shape, F32)
    else:
        in_dqt, qt_ref, q_ref, dot_ref, do_ref, delta_ref, dsame_ref, dother_ref, packed_ref, dqt_ref, bias_ref = rest
        dqt_ref[...] = in_dqt[...]
    full, row_block, parity = places(got_ref)
    for block, offset in enumerate(offsets):
        key_block = lax.rem(row_block + offset, 4)
        for is_other in range(2):
            write_biases(bias_ref, is_other * TILE, is_other, key_block, row_block, parity, full)

        def tile(kb, width):
            cols = pl.ds(kb * TILE, width)
            rows = pl.ds(kb * TILE, TILE)
            keys = key_tiles(arrays[2 * block : 2 * block + 2], kb)
            scores = biased(mm(keys, qt_ref[:, cols]), bias_ref, kb)
            weights = jnp.exp(scores - lse_ref[:, cols])
            slopes = (weights * (mm(keys, dot_ref[:, cols]) - delta_ref[:, cols])).astype(BF)
            dqt_ref[:, cols] += mm(keys[:, :HEAD_DIM].T, slopes)
            both = mm(slopes, q_ref[cols, :]) + mm(weights.astype(BF), do_ref[cols, :])
            dsame_ref[block, rows, :] = both[:TILE, :].astype(BF)
            dother_ref[block, rows, :] = both[TILE:, :].astype(BF)

        strips(full, tile)
    if not first:
        pack_frames((dqt_ref[...] * HEAD_DIM**-0.5).astype(BF), packed_ref)


def norm_parts(hidden):
    centre = jnp.mean(hidden, axis=-1, keepdims=True)
    shifted = hidden - centre
    spread = jnp.mean(shifted * shifted, axis=-1, keepdims=True)
    inverse = lax.rsqrt(spread + EPS)
    return shifted * inverse, inverse


def norm_back(raised, unit, inverse):
    mean = jnp.mean(raised, axis=-1, keepdims=True)
    along = jnp.mean(raised * unit, axis=-1, keepdims=True)
    return (raised - mean - unit * along) * inverse


def turns(base_ref, row_ref):
    place = lax.axis_index(("y", "x", "c")) * 4 + lax.axis_index("z")
    base = base_ref[pl.ds(place, 1), :]
    cos_base, sin_base = base[:, :128], base[:, 128:]
    cos_row, sin_row = row_ref[:, :128], row_ref[:, 128:]
    cosine = cos_base * cos_row - sin_base * sin_row
    sine = sin_base * cos_row + cos_base * sin_row
    first = lax.broadcasted_iota(jnp.int32, sine.shape, 1) % HEAD_DIM < HEAD_DIM // 2
    return cosine, jnp.where(first, -sine, sine)


def turn(pair, cosine, sine):
    half = HEAD_DIM // 2
    first = lax.broadcasted_iota(jnp.int32, pair.shape, 1) % HEAD_DIM < half
    crossed = jnp.where(first, pltpu.roll(pair, 128 - half, 1), pltpu.roll(pair, half, 1))
    return pair * cosine + crossed * sine


def pre_kernel(clip_ref, mask_ref, tok_ref, type_ref, table_ref, gain_ref, w_ref, base_ref, row_ref, sent_ref, start_ref, low_ref, mixed_ref, kinds_ref):
    swapped = clip_ref[0]
    cosine, sine = turns(base_ref, row_ref)
    kinds_ref[...] = jnp.zeros(kinds_ref.shape, BF)
    kinds_ref[:TYPES, :] = table_ref[...]
    for clip in range(2):
        slot = jnp.where(swapped > 0, 1 - clip, clip)
        kinds = type_ref[pl.ds(slot, 1), :]
        onehot = (lax.broadcasted_iota(jnp.int32, (16, ROWS), 0) == kinds).astype(F32).astype(BF)
        hidden = tok_ref[slot].astype(F32) + mm_t(onehot, kinds_ref[...])
        unit, _ = norm_parts(hidden)
        start_ref[clip * ROWS : (clip + 1) * ROWS, :] = hidden
        low_ref[clip * ROWS : (clip + 1) * ROWS, :] = (unit * gain_ref[...]).astype(BF)
    width = 512
    for third in range(3):
        mixed_ref[:, third * width : (third + 1) * width] = mm(low_ref[...], w_ref[:, third * width : (third + 1) * width])
    for clip in range(2):
        slot = jnp.where(swapped > 0, 1 - clip, clip)
        rows = slice(clip * ROWS, (clip + 1) * ROWS)
        real = jnp.full((16, 128), mask_ref[slot], jnp.int32).astype(F32).astype(BF)
        for pair in range(HEADS // 2):
            query = (turn(mixed_ref[rows, pair * 128 : (pair + 1) * 128], cosine, sine).astype(BF) * HEAD_DIM**-0.5).astype(BF)
            key = turn(mixed_ref[rows, width + pair * 128 : width + (pair + 1) * 128], cosine, sine).astype(BF)
            value = mixed_ref[rows, 2 * width + pair * 128 : 2 * width + (pair + 1) * 128].astype(BF)
            for side in range(2):
                to = (2 * pair + side) * 2 + clip
                lanes = slice(side * HEAD_DIM, (side + 1) * HEAD_DIM)
                sent_ref[to, :ROWS, :] = jnp.concatenate([key[:, lanes], value[:, lanes]], axis=1)
                sent_ref[to, ROWS : ROWS + ROWS // 2, :] = jnp.concatenate([query[: ROWS // 2, lanes], query[ROWS // 2 :, lanes]], axis=1)
                sent_ref[to, ROWS + ROWS // 2 :, :] = real


def mm_nt(a, b):
    return lax.dot_general(a, b, (((1,), (1,)), ((), ())), preferred_element_type=F32)


FF_PART = 512
GELU_SCALE = float(np.sqrt(2.0 / np.pi))
GELU_CUBE = 0.044715
G_AT, DU_AT, N2_AT, DY_AT, AT_AT, DA_AT, ACT_WIDTH = 0, 1024, 2048, 2560, 3072, 3328, 3840


def mlp_kernel(
    clip_ref, got_ref, start_ref, cot_ref, gain_ref, wo_ref, wu_ref, wd_ref, out_ref, packed_ref, mid_ref, gaing_ref, acts_ref,
    attn_ref, slope_ref,
):
    swapped, core = clip_ref[0], lax.axis_index("c")
    keep, send = 0, 1
    for clip in range(2):
        for pair in range(HEADS // 2):
            one, two = got_ref[4 * pair + clip], got_ref[4 * pair + 2 + clip]
            attn_ref[clip * ROWS : clip * ROWS + ROWS // 2, pair * 128 : (pair + 1) * 128] = jnp.concatenate([one[:, :HEAD_DIM], two[:, :HEAD_DIM]], axis=1)
            attn_ref[clip * ROWS + ROWS // 2 : (clip + 1) * ROWS, pair * 128 : (pair + 1) * 128] = jnp.concatenate([one[:, HEAD_DIM:], two[:, HEAD_DIM:]], axis=1)
    slots = [jnp.where(swapped > 0, 1 - clip, clip) for clip in range(2)]
    grad_low = jnp.concatenate([cot_ref[slots[0]], cot_ref[slots[1]]], axis=0)
    attn = attn_ref[...]
    middle = start_ref[...] + mm(attn, wo_ref[...])
    unit, inverse = norm_parts(middle)
    low = (unit * gain_ref[...]).astype(BF)
    final = middle
    for part in range(4):
        cols = slice(part * FF_PART, (part + 1) * FF_PART)
        upper = mm(low, wu_ref[:, cols])
        square = upper * upper
        bend = jnp.tanh(GELU_SCALE * (upper + GELU_CUBE * (square * upper)))
        act = (0.5 * upper * (1.0 + bend)).astype(BF)
        rise = 0.5 * (1.0 + bend) + 0.5 * upper * (1.0 - bend * bend) * (GELU_SCALE * (1.0 + 3.0 * GELU_CUBE * square))
        final = final + mm(act, wd_ref[cols, :])
        slope = (mm_nt(grad_low, wd_ref[cols, :]) * rise).astype(BF)
        slope_ref[:, cols] = slope
        side = jnp.where(core == part // 2, keep, send)
        at = (part % 2) * FF_PART
        acts_ref[side, :, G_AT + at : G_AT + at + FF_PART] = act
        acts_ref[side, :, DU_AT + at : DU_AT + at + FF_PART] = slope
    for clip in range(2):
        out_ref[slots[clip]] = final[clip * ROWS : (clip + 1) * ROWS].astype(BF)
    down = mm_nt(slope_ref[...], wu_ref[...])
    gaing_ref[...] = jnp.sum(down * unit, axis=0, keepdims=True)
    grad_mid = grad_low.astype(F32) + norm_back(down * gain_ref[...], unit, inverse)
    mid_ref[...] = grad_mid
    grad_mid_low = grad_mid.astype(BF)
    grad_attn = mm_nt(grad_mid_low, wo_ref[...]).astype(BF)
    for side in (keep, send):
        acts_ref[side, :, N2_AT : N2_AT + 512] = low
        acts_ref[side, :, DY_AT : DY_AT + 512] = grad_low
        acts_ref[side, :, DA_AT : DA_AT + 512] = grad_mid_low
    for half in range(2):
        acts_ref[jnp.where(core == half, keep, send), :, AT_AT : AT_AT + 256] = attn[:, half * 256 : (half + 1) * 256]
    for clip in range(2):
        for pair in range(HEADS // 2):
            rows = grad_attn[clip * ROWS : (clip + 1) * ROWS, pair * 128 : (pair + 1) * 128]
            upper_rows, lower_rows = rows[: ROWS // 2], rows[ROWS // 2 :]
            packed_ref[4 * pair + clip] = jnp.concatenate([upper_rows[:, :HEAD_DIM], lower_rows[:, :HEAD_DIM]], axis=1)
            packed_ref[4 * pair + 2 + clip] = jnp.concatenate([upper_rows[:, HEAD_DIM:], lower_rows[:, HEAD_DIM:]], axis=1)


UP_AT, OUT_AT, PIECE_ROWS = 1024, 2048, 2304


def weight_kernel(acts_ref, theirs_ref, *piece_refs):
    block = lax.axis_index("z")

    def both(at, width):
        return jnp.concatenate([acts_ref[0, :, pl.ds(at, width)], theirs_ref[:, pl.ds(at, width)]], axis=0)

    grad_low, low, attn = both(DY_AT, 512), both(N2_AT, 512), both(AT_AT, 256)
    for step, piece_ref in enumerate(piece_refs):
        piece = lax.rem(block + step, 4)
        units = pl.multiple_of(piece * 256, 256)
        down = mm_t(both(G_AT + units, 256), grad_low).astype(BF)
        for part in range(4):
            piece_ref[part * 256 : (part + 1) * 256, :] = down[:, part * 128 : (part + 1) * 128]
        up = mm_t(low, both(DU_AT + units, 256)).astype(BF)
        for part in range(2):
            piece_ref[UP_AT + part * 512 : UP_AT + (part + 1) * 512, :] = up[:, part * 128 : (part + 1) * 128]
        piece_ref[OUT_AT:, :] = mm_t(attn, both(DA_AT + pl.multiple_of(piece * 128, 128), 128)).astype(BF)


QKV_HALF = 768


def turn_back_kernel(back_ref, low_ref, base_ref, row_ref, acts_ref):
    core = lax.axis_index("c")
    cosine, sine = turns(base_ref, row_ref)
    half = ROWS // 2

    def unpack(one, two):
        upper_rows = jnp.concatenate([one[:, :HEAD_DIM], two[:, :HEAD_DIM]], axis=1)
        lower_rows = jnp.concatenate([one[:, HEAD_DIM:], two[:, HEAD_DIM:]], axis=1)
        return jnp.concatenate([upper_rows, lower_rows], axis=0)

    def write(rows, cols, value):
        side = jnp.where(core == cols // QKV_HALF, 0, 1)
        at = 512 + cols % QKV_HALF
        acts_ref[side, rows, at : at + 128] = value

    for clip in range(2):
        rows = slice(clip * ROWS, (clip + 1) * ROWS)
        for pair in range(HEADS // 2):
            one, two = 4 * pair + clip, 4 * pair + 2 + clip
            query = unpack(back_ref[one, ROWS : ROWS + half, :], back_ref[two, ROWS : ROWS + half, :]).astype(F32)
            first, second = back_ref[one, :ROWS, :], back_ref[two, :ROWS, :]
            key = jnp.concatenate([first[:, :HEAD_DIM], second[:, :HEAD_DIM]], axis=1).astype(F32)
            cols = pair * 128
            write(rows, cols, turn(query, cosine, -sine).astype(BF))
            write(rows, 512 + cols, turn(key, cosine, -sine).astype(BF))
            write(rows, 1024 + cols, jnp.concatenate([first[:, HEAD_DIM:], second[:, HEAD_DIM:]], axis=1))
    for side in range(2):
        acts_ref[side, :, :512] = low_ref[...]


def post_kernel(clip_ref, acts_ref, start_ref, mid_ref, type_ref, mlp_ref, gain_ref, w_ref, grad_ref, small_ref):
    swapped, core = clip_ref[0], lax.axis_index("c")
    down = jnp.zeros((2 * ROWS, 512), F32)
    for part in range(2):
        raw = acts_ref[jnp.where(core == part, 0, 1), :, 512:]
        down = down + mm_nt(raw, w_ref[:, part * QKV_HALF : (part + 1) * QKV_HALF])
    unit, inverse = norm_parts(start_ref[...])
    grad = mid_ref[...] + norm_back(down * gain_ref[...], unit, inverse)
    gain_grad = jnp.sum(down * unit, axis=0, keepdims=True)
    table = jnp.zeros((8, 512), F32)
    for clip in range(2):
        slot = jnp.where(swapped > 0, 1 - clip, clip)
        part = grad[clip * ROWS : (clip + 1) * ROWS]
        grad_ref[slot] = part
        kinds = type_ref[pl.ds(slot, 1), :]
        onehot = (lax.broadcasted_iota(jnp.int32, (8, ROWS), 0) == kinds).astype(F32)
        table = table + jnp.dot(onehot, part, precision=lax.Precision.HIGHEST, preferred_element_type=F32)
    row = lax.broadcasted_iota(jnp.int32, (8, 512), 0)
    small_ref[...] = jnp.where(row == 3, gain_grad, jnp.where(row == 4, mlp_ref[...], table))


def mix_weight_kernel(acts_ref, theirs_ref, small_ref, pieces_ref):
    low = jnp.concatenate([acts_ref[0, :, :512], theirs_ref[:, :512]], axis=0)
    raw = jnp.concatenate([acts_ref[0, :, 512:], theirs_ref[:, 512:]], axis=0)
    small = small_ref[...]
    for side in range(2):
        grad = mm_t(low, raw[:, side * 384 : (side + 1) * 384]).astype(BF)
        for strip in range(32):
            for part in range(3):
                block = grad[strip * 16 : (strip + 1) * 16, part * 128 : (part + 1) * 128]
                pieces_ref[2 * strip + side, part * 16 : (part + 1) * 16, :] = block
    for place in range(64):
        row, part = place // 4, place % 4
        value = jnp.zeros((8, 128), F32)
        if row < 5:
            value = jnp.broadcast_to(small[row : row + 1, part * 128 : (part + 1) * 128], (8, 128))
        pieces_ref[place, 48:, :] = value.astype(BF)


def total_kernel(pieces_ref, copies_ref):
    total = pieces_ref[0].astype(F32)
    for place in range(1, 64):
        total = total + pieces_ref[place].astype(F32)
    low = total.astype(BF)
    for place in range(64):
        copies_ref[place] = low


def mix_sum_kernel(own_ref, theirs_ref, qkv_ref, table_ref, gain_one_ref, gain_two_ref):
    core = lax.axis_index("c")
    for half in range(2):

        def write(pieces_ref):
            for place in range(64):
                strip, side = place // 2, place % 2
                cols = half * QKV_HALF + side * 384
                for part in range(3):
                    block = pieces_ref[place, part * 16 : (part + 1) * 16, :].astype(F32)
                    qkv_ref[strip * 16 : (strip + 1) * 16, cols + part * 128 : cols + (part + 1) * 128] = block

        pl.when(core == half)(functools.partial(write, own_ref))
        pl.when(core != half)(functools.partial(write, theirs_ref))
    for row in range(5):
        target, line = ((table_ref, row), (table_ref, row), (table_ref, row), (gain_one_ref, 0), (gain_two_ref, 0))[row]
        for part in range(4):
            both = own_ref[4 * row + part, 48:, :].astype(F32) + theirs_ref[4 * row + part, 48:, :].astype(F32)
            target[line : line + 1, part * 128 : (part + 1) * 128] = both[0:1]


def spread_kernel(*refs):
    pieces, (down, up, out, low, down_stage, up_stage, out_stage, in_sems, out_sems) = refs[:8], refs[8:]
    reads = [pltpu.make_async_copy(piece, low.at[at], in_sems.at[at]) for at, piece in enumerate(pieces)]
    for read in reads:
        read.start()
    writes = []

    def write(source, target):
        writes.append(pltpu.make_async_copy(source, target, out_sems.at[len(writes)]))
        writes[-1].start()

    for at, read in enumerate(reads):
        read.wait()
        core = lax.axis_index("c") if at < 4 else 1 - lax.axis_index("c")
        piece = lax.rem(lax.axis_index("z") + at, 4)
        units = pl.ds(pl.multiple_of(core * 1024 + piece * 256, 256), 256)
        for part in range(4):
            down_stage[at, :, part * 128 : (part + 1) * 128] = low[at, part * 256 : (part + 1) * 256, :].astype(F32)
        write(down_stage.at[at], down.at[units, :])
        for part in range(2):
            up_stage[at, :, part * 128 : (part + 1) * 128] = low[at, UP_AT + part * 512 : UP_AT + (part + 1) * 512, :].astype(F32)
        write(up_stage.at[at], up.at[:, units])
        out_stage[at] = low[at, OUT_AT:, :].astype(F32)
        write(out_stage.at[at], out.at[pl.ds(core * 256, 256), pl.ds(pl.multiple_of(piece * 128, 128), 128)])
    for copy in writes:
        copy.wait()


VMEM_SPEC = pl.BlockSpec(memory_space=pltpu.VMEM)
SMEM_SPEC = pl.BlockSpec(memory_space=pltpu.SMEM)


def call(kernel, name, outs, args, scalars=1, scratch=(), megabytes=28, flops=10**9, nbytes=4 * 2**20, exps=0):
    shapes = tuple(jax.ShapeDtypeStruct(shape, dtype) for shape, dtype in outs)
    return pl.pallas_call(
        kernel,
        out_shape=shapes,
        in_specs=[SMEM_SPEC] * scalars + [VMEM_SPEC] * (len(args) - scalars),
        out_specs=(VMEM_SPEC,) * len(shapes),
        scratch_shapes=[pltpu.VMEM(shape, dtype) for shape, dtype in scratch],
        compiler_params=pltpu.CompilerParams(vmem_limit_bytes=megabytes * 2**20),
        cost_estimate=pl.CostEstimate(flops=flops, bytes_accessed=nbytes, transcendentals=exps),
        name=name,
    )(*args)


WIDE = ((ONES + HEAD_DIM, LOCAL), F32)
LINE = ((1, LOCAL), F32)


QUERIES = ((128, LOCAL), BF)
GRADS = ((64, LOCAL), F32)
PACKED = ((FRAMES, ROWS // 2, 128), BF)


def attend(name, got, blocks, arrays, state=(), last=False, flops=10**9):
    first = not state
    outs = (PACKED, GRADS, LINE) if last else (WIDE, LINE) + ((QUERIES,) if first else ())
    scratch = ((WIDE, LINE) if last else ()) + (((2, len(blocks) * TILE, TILE), F32),)
    return call(
        functools.partial(forward_kernel, blocks, first, last), name, outs, (got,) + tuple(arrays) + tuple(state),
        scalars=0, scratch=scratch, flops=flops, nbytes=10**5,
    )


def attend_back(name, got, grad, ot, lse, offsets, arrays, state=(), flops=10**8):
    first, blocks = not state, ((len(offsets), LOCAL, 128), BF)
    flat = ((LOCAL, 128), BF)
    outs = (blocks, blocks) + ((GRADS, QUERIES, flat, QUERIES, flat, LINE) if first else (PACKED,))
    scratch = (() if first else (GRADS,)) + (((2, 2 * TILE, TILE), F32),)
    return call(
        functools.partial(backward_kernel, offsets, first), name, outs, (got, grad, ot, lse) + tuple(arrays) + tuple(state),
        scalars=0, scratch=scratch, megabytes=28, flops=flops, nbytes=10**5,
    )


PIECES = ((64, 56, 128), BF)
MIXED = (((512, 1536), F32), ((TYPES, 512), F32), ((1, 512), F32), ((1, 512), F32))


def spread(pieces):
    hbm = pl.BlockSpec(memory_space=pltpu.HBM)
    return pl.pallas_call(
        spread_kernel,
        out_shape=tuple(jax.ShapeDtypeStruct(shape, F32) for shape in ((2048, 512), (512, 2048), (512, 512))),
        in_specs=[hbm] * 8,
        out_specs=(hbm,) * 3,
        scratch_shapes=[
            pltpu.VMEM((8, PIECE_ROWS, 128), BF),
            pltpu.VMEM((8, 256, 512), F32),
            pltpu.VMEM((8, 512, 256), F32),
            pltpu.VMEM((8, 256, 128), F32),
            pltpu.SemaphoreType.DMA((8,)),
            pltpu.SemaphoreType.DMA((24,)),
        ],
        compiler_params=pltpu.CompilerParams(vmem_limit_bytes=40 * 2**20),
        cost_estimate=pl.CostEstimate(flops=10**7, bytes_accessed=15 * 2**20, transcendentals=0),
        name="spread",
    )(*pieces)


def swap(array, axes):
    return lax.all_to_all(array, axes, 0, 0, tiled=True)


def partner(array):
    return lax.ppermute(array, "c", [(0, 1), (1, 0)])


def along(array, step):
    return lax.ppermute(array, "z", [(place, (place - step) % 4) for place in range(4)])


def angle_tables():
    rates = BASE ** (-np.arange(HEAD_DIM // 2, dtype=np.float64) / (HEAD_DIM // 2))
    rates = np.tile(rates, 4)
    tables = []
    for places in (np.arange(128) * ROWS, np.arange(ROWS)):
        angles = places[:, None] * rates[None, :]
        tables.append(np.concatenate([np.cos(angles), np.sin(angles)], axis=1).astype(np.float32))
    return tables


def local(
    tokens, type_ids, clip_ids, frame_mask, type_table, norm_gain, qkv_weight, out_weight, mlp_gain, up_weight, down_weight, cotangent
):
    base_table, row_table = (jnp.asarray(table) for table in angle_tables())
    gain_one, gain_two = norm_gain[None], mlp_gain[None]
    tokens_here = 2 * ROWS
    sent, start, low = call(
        pre_kernel, "pre", (((2 * HEADS, 112, 128), BF), ((tokens_here, 512), F32), ((tokens_here, 512), BF)),
        (clip_ids, frame_mask, tokens, type_ids, type_table, gain_one, qkv_weight, base_table, row_table),
        scalars=2, scratch=(((tokens_here, 1536), F32), ((16, 512), BF)), megabytes=60,
    )

    got = swap(sent, CHIPS)
    own = got[:, :ROWS].reshape(LOCAL, 128)
    own_other = partner(own)
    up, down = along(own, 1), along(own, 3)
    *state, queries = attend("attend_near", got, ((0, 0), (1, 0)), (own, own_other), flops=2 * 10**10)
    clip_later, *state = lax.optimization_barrier((clip_ids, *state))
    one_of_each = clip_later[0] + clip_later[1] == 1
    up, down, one_of_each, *state = lax.optimization_barrier((up, down, one_of_each, *state))
    up_other, down_other = partner(up), partner(down)
    halves = along(up[: LOCAL // 2], 1), along(down[LOCAL // 2 :], 3)
    state = attend("attend_same", got, ((0, 1), (0, 3)), (up, down), (*state, queries), flops=10**8)
    state = attend("attend_other", got, ((1, 1), (1, 3)), (up_other, down_other), (*state, queries), flops=10**8)
    halves, state = lax.optimization_barrier((halves, state))
    far = jnp.concatenate(halves, axis=0)
    far_other = partner(far)
    state = attend("attend_far_same", got, ((0, 2),), (far,), (*state, queries), flops=10**8)
    packed, out_t, lse = attend("attend_far", got, ((1, 2),), (far_other,), (*state, queries), last=True)

    heads_out = swap(packed, CHIPS)
    output, grad_packed, grad_mid, mlp_part, acts = call(
        mlp_kernel, "mlp",
        (((2, ROWS, 512), BF), ((2 * HEADS, ROWS // 2, 128), BF), ((tokens_here, 512), F32), ((1, 512), F32), ((2, tokens_here, ACT_WIDTH), BF)),
        (clip_ids, heads_out, start, cotangent, gain_two, out_weight, up_weight, down_weight),
        scratch=(((tokens_here, 512), BF), ((tokens_here, 2048), BF)), flops=3 * 10**9, nbytes=8 * 2**20, exps=300000,
    )
    theirs = partner(acts[1])
    pieces = call(weight_kernel, "weights", (((PIECE_ROWS, 128), BF),) * 4, (acts, theirs), scalars=0)
    pieces, grad_packed = lax.optimization_barrier((pieces, grad_packed))
    arrived = [along(piece, -step) for step, piece in enumerate(pieces) if step]
    grad_out = swap(grad_packed, CHIPS)
    dsame, dother, *back_state = attend_back(
        "attend_back_others", got, grad_out, out_t, lse, (2, 1, 3), (far, far_other, up, up_other, down, down_other)
    )
    arrived, back_state = lax.optimization_barrier((arrived, back_state))
    summed = (dsame.astype(F32) + partner(dother).astype(F32)).astype(BF)
    piece = sum((part.astype(F32) for part in arrived), pieces[0].astype(F32)).astype(BF)
    piece, summed = lax.optimization_barrier((piece, summed))
    moved = [along(summed[at], -offset) for at, offset in enumerate((2, 1, 3))]
    piece = jnp.sum(swap(piece.reshape(16, PIECE_ROWS // 16, 128), CHIPS).astype(F32), axis=0).astype(BF)
    piece, back_state = lax.optimization_barrier((piece, back_state))
    near_same, near_other, dq = attend_back("attend_back_near", got, grad_out, out_t, lse, (0,), (own, own_other), back_state)
    near_sum = near_same[0].astype(F32) + partner(near_other[0]).astype(F32)
    own_grad = sum((part.astype(F32) for part in moved), near_sum).astype(BF)

    spread_piece = jnp.broadcast_to(piece[None], (16, PIECE_ROWS // 16, 128))
    back = swap(jnp.concatenate([own_grad.reshape(FRAMES, ROWS, 128), dq, spread_piece], axis=1), CHIPS)
    piece = back[:, ROWS + ROWS // 2 :].reshape(PIECE_ROWS, 128)
    pieces = [piece, along(piece, 1), along(piece, 3)]

    def ending(grads):
        (mix_acts,) = call(
            turn_back_kernel, "turn_back", (((2, tokens_here, 512 + QKV_HALF), BF),), (grads, low, base_table, row_table), scalars=0
        )
        input_grad, small = call(
            post_kernel, "post", (((2, ROWS, 512), F32), ((8, 512), F32)),
            (clip_ids, mix_acts, start, grad_mid, type_ids, mlp_part, gain_one, qkv_weight),
        )
        (strips_out,) = call(mix_weight_kernel, "mix_weights", (PIECES,), (mix_acts, partner(mix_acts[1]), small), scalars=0)
        return input_grad, *call(total_kernel, "total", (PIECES,), (swap(strips_out, ("y", "x", "z")),), scalars=0)

    def nothing(grads):
        return jnp.zeros((2, ROWS, 512), F32), jnp.zeros(*PIECES)

    input_grad, totals = lax.cond(one_of_each, ending, nothing, back[:, : ROWS + ROWS // 2])
    totals, pieces = lax.optimization_barrier((totals, pieces))
    mixed = swap(totals, ("y", "x", "z"))
    halves = along(pieces[1][: PIECE_ROWS // 2], 1), along(pieces[2][PIECE_ROWS // 2 :], 3)
    pieces = [*pieces[:2], jnp.concatenate(halves, axis=0), pieces[2]]
    sums = spread(pieces + [partner(piece) for piece in pieces])
    mixed, sums = lax.optimization_barrier((mixed, sums))
    qkv_sum, table_sum, gain_one_sum, gain_two_sum = call(mix_sum_kernel, "mix_sums", MIXED, (mixed, partner(mixed)), scalars=0)
    down_sum, up_sum, out_sum = sums
    return (output, input_grad, table_sum, gain_one_sum[0], qkv_sum, out_sum, gain_two_sum[0], up_sum, down_sum)


def solution(mesh):
    chips = Mesh(mesh.devices.reshape(4, 4, 2, 4), ("y", "x", "c", "z"))
    tm = ("y", "x", "c")
    rows = P(tm, "z", None)
    in_specs = (rows, P(tm, "z"), P(tm), P(tm)) + (P(),) * 7 + (rows,)
    out_specs = (rows, rows) + (P(),) * 7
    return jax.shard_map(local, mesh=chips, in_specs=in_specs, out_specs=out_specs, check_vma=False)
```

```python
import functools

import jax
import jax.numpy as jnp
import numpy as np
from jax import lax
from jax.experimental import pallas as pl
from jax.experimental.pallas import tpu as pltpu
from jax.sharding import Mesh
from jax.sharding import PartitionSpec as P

HEADS = 8
HEAD_DIM = 64
TYPES = 3
TILE = 256
FRAMES = 16
ROWS = 64
LOCAL = FRAMES * ROWS
GROUPS = LOCAL // TILE
MASKED = -1e30
ONES = 16
EPS = 1e-05
BASE = 10000.0
BF = jnp.bfloat16
F32 = jnp.float32
CHIPS = ("y", "x")


def mm(a, b):
    return jnp.dot(a, b, preferred_element_type=F32)


def mm_t(a, b):
    return lax.dot_general(a, b, (((0,), (0,)), ((), ())), preferred_element_type=F32)


def write_biases(bias_ref, at, is_other, key_block, row_block, parity, full):
    key = lax.broadcasted_iota(jnp.int32, (TILE, TILE), 0)
    query = lax.broadcasted_iota(jnp.int32, (TILE, TILE), 1)
    late = jnp.where(full, 0.0, MASKED)
    if is_other:
        before = key // ROWS < query // ROWS + parity
        bias_ref[0, at : at + TILE, :] = jnp.where(before, 0.0, MASKED)
        bias_ref[1, at : at + TILE, :] = jnp.where(before, late, MASKED)
        return
    before = key // ROWS < query // ROWS
    row_shift = jnp.where(key_block == row_block, 0, jnp.where(key_block < row_block, ROWS, -ROWS))
    own = (key // ROWS == query // ROWS) & ((key % ROWS) <= (query % ROWS) + row_shift)
    bias_ref[0, at : at + TILE, :] = jnp.where(before | own, 0.0, MASKED)
    bias_ref[1, at : at + TILE, :] = jnp.where(own, 0.0, jnp.where(before, late, MASKED))


def key_tiles(arrays, kb):
    return jnp.concatenate([array[pl.ds(kb * TILE, TILE), :] for array in arrays], axis=0)


def biased(scores, bias_ref, kb):
    bias = bias_ref[0 if kb == 0 else 1]
    if scores.shape[1] == TILE:
        return scores + bias
    return jnp.concatenate([scores[:, :TILE] + bias, scores[:, TILE:]], axis=1)


def strips(full, tile):
    @pl.when(full)
    def _():
        for kb in range(GROUPS):
            tile(kb, LOCAL - kb * TILE)

    @pl.when(jnp.logical_not(full))
    def _():
        for kb in range(GROUPS):
            tile(kb, TILE if kb else LOCAL)


def unfold_pair(first, second):
    return jnp.concatenate([first[:, :HEAD_DIM], first[:, HEAD_DIM:], second[:, :HEAD_DIM], second[:, HEAD_DIM:]], axis=0)


def forward_kernel(blocks, first, last, got_ref, *refs):
    arrays, rest = refs[: len(blocks)], refs[len(blocks) :]
    if first:
        acc_ref, top_ref, qt_ref, bias_ref = rest
        top_ref[...] = jnp.full(top_ref.shape, MASKED, F32)
        acc_ref[...] = jnp.zeros(acc_ref.shape, F32)
        write_queries(got_ref, qt_ref)
    else:
        in_acc, in_top, qt_ref = rest[:3]
        acc_ref, top_ref, bias_ref = rest[6:] if last else rest[3:]
        top_ref[...] = in_top[...]
        acc_ref[...] = in_acc[...]
    full, row_block, parity = places(got_ref)
    for place, (is_other, offset) in enumerate(blocks):
        write_biases(bias_ref, place * TILE, is_other, lax.rem(row_block + offset, 4), row_block, parity, full)

    def tile(kb, width):
        cols = pl.ds(kb * TILE, width)
        keys = key_tiles(arrays, kb)
        values = jnp.concatenate([jnp.ones((ONES, keys.shape[0]), BF), keys.T[HEAD_DIM:]], axis=0)
        scores = biased(mm(keys, qt_ref[:, cols]), bias_ref, kb)
        top_old = top_ref[:, cols]
        top_new = jnp.maximum(top_old, jnp.max(scores, axis=0, keepdims=True))
        weights = jnp.exp(scores - top_new).astype(BF)
        acc_ref[:, cols] = acc_ref[:, cols] * jnp.exp(top_old - top_new) + mm(values, weights)
        top_ref[:, cols] = top_new

    strips(full, tile)
    if last:
        packed_ref, ot_ref, lse_ref = rest[3:6]
        total = acc_ref[0:1, :]
        out_t = acc_ref[ONES:, :] / total
        ot_ref[...] = out_t
        lse_ref[...] = top_ref[...] + jnp.log(total)
        pack_frames(out_t.astype(BF), packed_ref)


def places(got_ref):
    full = jnp.max(got_ref[FRAMES - 1, ROWS + ROWS // 2 :, :].astype(F32)) > 0.5
    return full, lax.axis_index("z"), lax.axis_index("c")


def pack_frames(flipped, packed_ref):
    half = ROWS // 2
    for pair in range(FRAMES // 2):
        part = flipped[:, pair * 128 : (pair + 1) * 128].T
        packed_ref[2 * pair] = jnp.concatenate([part[:half], part[half:ROWS]], axis=1)
        packed_ref[2 * pair + 1] = jnp.concatenate([part[ROWS : ROWS + half], part[ROWS + half :]], axis=1)


def write_queries(got_ref, qt_ref):
    for pair in range(FRAMES // 2):
        rows = unfold_pair(got_ref[2 * pair, ROWS : ROWS + ROWS // 2, :], got_ref[2 * pair + 1, ROWS : ROWS + ROWS // 2, :])
        qt_ref[:HEAD_DIM, pair * 128 : (pair + 1) * 128] = rows.T
    qt_ref[HEAD_DIM:, :] = jnp.zeros((HEAD_DIM, LOCAL), BF)


def backward_kernel(offsets, first, got_ref, grad_ref, ot_ref, lse_ref, *refs):
    arrays, rest = refs[: 2 * len(offsets)], refs[2 * len(offsets) :]
    if first:
        dsame_ref, dother_ref, dqt_ref, qt_ref, q_ref, dot_ref, do_ref, delta_ref, bias_ref = rest
        write_queries(got_ref, qt_ref)
        blank = jnp.zeros((2 * ROWS, HEAD_DIM), BF)
        for pair in range(FRAMES // 2):
            span = pl.ds(pair * 128, 128)
            query = unfold_pair(got_ref[2 * pair, ROWS : ROWS + ROWS // 2, :], got_ref[2 * pair + 1, ROWS : ROWS + ROWS // 2, :])
            grad = unfold_pair(grad_ref[2 * pair], grad_ref[2 * pair + 1])
            q_ref[span, :] = jnp.concatenate([query, blank], axis=1)
            do_ref[span, :] = jnp.concatenate([blank, grad], axis=1)
            dot_ref[HEAD_DIM:, pair * 128 : (pair + 1) * 128] = grad.T
        dot_ref[:HEAD_DIM, :] = jnp.zeros((HEAD_DIM, LOCAL), BF)
        delta_ref[...] = jnp.sum(dot_ref[HEAD_DIM:, :].astype(F32) * ot_ref[...], axis=0, keepdims=True)
        dqt_ref[...] = jnp.zeros(dqt_ref.shape, F32)
    else:
        in_dqt, qt_ref, q_ref, dot_ref, do_ref, delta_ref, dsame_ref, dother_ref, packed_ref, dqt_ref, bias_ref = rest
        dqt_ref[...] = in_dqt[...]
    full, row_block, parity = places(got_ref)
    for block, offset in enumerate(offsets):
        key_block = lax.rem(row_block + offset, 4)
        for is_other in range(2):
            write_biases(bias_ref, is_other * TILE, is_other, key_block, row_block, parity, full)

        def tile(kb, width):
            cols = pl.ds(kb * TILE, width)
            rows = pl.ds(kb * TILE, TILE)
            keys = key_tiles(arrays[2 * block : 2 * block + 2], kb)
            scores = biased(mm(keys, qt_ref[:, cols]), bias_ref, kb)
            weights = jnp.exp(scores - lse_ref[:, cols])
            slopes = (weights * (mm(keys, dot_ref[:, cols]) - delta_ref[:, cols])).astype(BF)
            dqt_ref[:, cols] += mm(keys[:, :HEAD_DIM].T, slopes)
            both = mm(slopes, q_ref[cols, :]) + mm(weights.astype(BF), do_ref[cols, :])
            dsame_ref[block, rows, :] = both[:TILE, :].astype(BF)
            dother_ref[block, rows, :] = both[TILE:, :].astype(BF)

        strips(full, tile)
    if not first:
        pack_frames((dqt_ref[...] * HEAD_DIM**-0.5).astype(BF), packed_ref)


def norm_parts(hidden):
    centre = jnp.mean(hidden, axis=-1, keepdims=True)
    shifted = hidden - centre
    spread = jnp.mean(shifted * shifted, axis=-1, keepdims=True)
    inverse = lax.rsqrt(spread + EPS)
    return shifted * inverse, inverse


def norm_back(raised, unit, inverse):
    mean = jnp.mean(raised, axis=-1, keepdims=True)
    along = jnp.mean(raised * unit, axis=-1, keepdims=True)
    return (raised - mean - unit * along) * inverse


def turns(base_ref, row_ref):
    place = lax.axis_index(("y", "x", "c")) * 4 + lax.axis_index("z")
    base = base_ref[pl.ds(place, 1), :]
    cos_base, sin_base = base[:, :128], base[:, 128:]
    cos_row, sin_row = row_ref[:, :128], row_ref[:, 128:]
    cosine = cos_base * cos_row - sin_base * sin_row
    sine = sin_base * cos_row + cos_base * sin_row
    first = lax.broadcasted_iota(jnp.int32, sine.shape, 1) % HEAD_DIM < HEAD_DIM // 2
    return cosine, jnp.where(first, -sine, sine)


def turn(pair, cosine, sine):
    half = HEAD_DIM // 2
    first = lax.broadcasted_iota(jnp.int32, pair.shape, 1) % HEAD_DIM < half
    crossed = jnp.where(first, pltpu.roll(pair, 128 - half, 1), pltpu.roll(pair, half, 1))
    return pair * cosine + crossed * sine


def pre_kernel(clip_ref, mask_ref, tok_ref, type_ref, table_ref, gain_ref, w_ref, base_ref, row_ref, sent_ref, start_ref, low_ref, mixed_ref, kinds_ref):
    swapped = clip_ref[0]
    cosine, sine = turns(base_ref, row_ref)
    kinds_ref[...] = jnp.zeros(kinds_ref.shape, BF)
    kinds_ref[:TYPES, :] = table_ref[...]
    for clip in range(2):
        slot = jnp.where(swapped > 0, 1 - clip, clip)
        kinds = type_ref[pl.ds(slot, 1), :]
        onehot = (lax.broadcasted_iota(jnp.int32, (16, ROWS), 0) == kinds).astype(F32).astype(BF)
        hidden = tok_ref[slot].astype(F32) + mm_t(onehot, kinds_ref[...])
        unit, _ = norm_parts(hidden)
        start_ref[clip * ROWS : (clip + 1) * ROWS, :] = hidden
        low_ref[clip * ROWS : (clip + 1) * ROWS, :] = (unit * gain_ref[...]).astype(BF)
    width = 512
    for third in range(3):
        mixed_ref[:, third * width : (third + 1) * width] = mm(low_ref[...], w_ref[:, third * width : (third + 1) * width])
    for clip in range(2):
        slot = jnp.where(swapped > 0, 1 - clip, clip)
        rows = slice(clip * ROWS, (clip + 1) * ROWS)
        real = jnp.full((16, 128), mask_ref[slot], jnp.int32).astype(F32).astype(BF)
        for pair in range(HEADS // 2):
            query = (turn(mixed_ref[rows, pair * 128 : (pair + 1) * 128], cosine, sine).astype(BF) * HEAD_DIM**-0.5).astype(BF)
            key = turn(mixed_ref[rows, width + pair * 128 : width + (pair + 1) * 128], cosine, sine).astype(BF)
            value = mixed_ref[rows, 2 * width + pair * 128 : 2 * width + (pair + 1) * 128].astype(BF)
            for side in range(2):
                to = (2 * pair + side) * 2 + clip
                lanes = slice(side * HEAD_DIM, (side + 1) * HEAD_DIM)
                sent_ref[to, :ROWS, :] = jnp.concatenate([key[:, lanes], value[:, lanes]], axis=1)
                sent_ref[to, ROWS : ROWS + ROWS // 2, :] = jnp.concatenate([query[: ROWS // 2, lanes], query[ROWS // 2 :, lanes]], axis=1)
                sent_ref[to, ROWS + ROWS // 2 :, :] = real


def mm_nt(a, b):
    return lax.dot_general(a, b, (((1,), (1,)), ((), ())), preferred_element_type=F32)


FF_PART = 512
GELU_SCALE = float(np.sqrt(2.0 / np.pi))
GELU_CUBE = 0.044715
G_AT, DU_AT, N2_AT, DY_AT, AT_AT, DA_AT, ACT_WIDTH = 0, 1024, 2048, 2560, 3072, 3328, 3840


def mlp_kernel(
    clip_ref, got_ref, start_ref, cot_ref, gain_ref, wo_ref, wu_ref, wd_ref, out_ref, packed_ref, mid_ref, gaing_ref, acts_ref,
    attn_ref, slope_ref,
):
    swapped, core = clip_ref[0], lax.axis_index("c")
    keep, send = 0, 1
    for clip in range(2):
        for pair in range(HEADS // 2):
            one, two = got_ref[4 * pair + clip], got_ref[4 * pair + 2 + clip]
            attn_ref[clip * ROWS : clip * ROWS + ROWS // 2, pair * 128 : (pair + 1) * 128] = jnp.concatenate([one[:, :HEAD_DIM], two[:, :HEAD_DIM]], axis=1)
            attn_ref[clip * ROWS + ROWS // 2 : (clip + 1) * ROWS, pair * 128 : (pair + 1) * 128] = jnp.concatenate([one[:, HEAD_DIM:], two[:, HEAD_DIM:]], axis=1)
    slots = [jnp.where(swapped > 0, 1 - clip, clip) for clip in range(2)]
    grad_low = jnp.concatenate([cot_ref[slots[0]], cot_ref[slots[1]]], axis=0)
    attn = attn_ref[...]
    middle = start_ref[...] + mm(attn, wo_ref[...])
    unit, inverse = norm_parts(middle)
    low = (unit * gain_ref[...]).astype(BF)
    final = middle
    for part in range(4):
        cols = slice(part * FF_PART, (part + 1) * FF_PART)
        upper = mm(low, wu_ref[:, cols])
        square = upper * upper
        bend = jnp.tanh(GELU_SCALE * (upper + GELU_CUBE * (square * upper)))
        act = (0.5 * upper * (1.0 + bend)).astype(BF)
        rise = 0.5 * (1.0 + bend) + 0.5 * upper * (1.0 - bend * bend) * (GELU_SCALE * (1.0 + 3.0 * GELU_CUBE * square))
        final = final + mm(act, wd_ref[cols, :])
        slope = (mm_nt(grad_low, wd_ref[cols, :]) * rise).astype(BF)
        slope_ref[:, cols] = slope
        side = jnp.where(core == part // 2, keep, send)
        at = (part % 2) * FF_PART
        acts_ref[side, :, G_AT + at : G_AT + at + FF_PART] = act
        acts_ref[side, :, DU_AT + at : DU_AT + at + FF_PART] = slope
    for clip in range(2):
        out_ref[slots[clip]] = final[clip * ROWS : (clip + 1) * ROWS].astype(BF)
    down = mm_nt(slope_ref[...], wu_ref[...])
    gaing_ref[...] = jnp.sum(down * unit, axis=0, keepdims=True)
    grad_mid = grad_low.astype(F32) + norm_back(down * gain_ref[...], unit, inverse)
    mid_ref[...] = grad_mid
    grad_mid_low = grad_mid.astype(BF)
    grad_attn = mm_nt(grad_mid_low, wo_ref[...]).astype(BF)
    for side in (keep, send):
        acts_ref[side, :, N2_AT : N2_AT + 512] = low
        acts_ref[side, :, DY_AT : DY_AT + 512] = grad_low
        acts_ref[side, :, DA_AT : DA_AT + 512] = grad_mid_low
    for half in range(2):
        acts_ref[jnp.where(core == half, keep, send), :, AT_AT : AT_AT + 256] = attn[:, half * 256 : (half + 1) * 256]
    for clip in range(2):
        for pair in range(HEADS // 2):
            rows = grad_attn[clip * ROWS : (clip + 1) * ROWS, pair * 128 : (pair + 1) * 128]
            upper_rows, lower_rows = rows[: ROWS // 2], rows[ROWS // 2 :]
            packed_ref[4 * pair + clip] = jnp.concatenate([upper_rows[:, :HEAD_DIM], lower_rows[:, :HEAD_DIM]], axis=1)
            packed_ref[4 * pair + 2 + clip] = jnp.concatenate([upper_rows[:, HEAD_DIM:], lower_rows[:, HEAD_DIM:]], axis=1)


UP_AT, OUT_AT, PIECE_ROWS = 1024, 2048, 2304


def weight_kernel(acts_ref, theirs_ref, *piece_refs):
    block = lax.axis_index("z")

    def both(at, width):
        return jnp.concatenate([acts_ref[0, :, pl.ds(at, width)], theirs_ref[:, pl.ds(at, width)]], axis=0)

    grad_low, low, attn = both(DY_AT, 512), both(N2_AT, 512), both(AT_AT, 256)
    for step, piece_ref in enumerate(piece_refs):
        piece = lax.rem(block + step, 4)
        units = pl.multiple_of(piece * 256, 256)
        down = mm_t(both(G_AT + units, 256), grad_low).astype(BF)
        for part in range(4):
            piece_ref[part * 256 : (part + 1) * 256, :] = down[:, part * 128 : (part + 1) * 128]
        up = mm_t(low, both(DU_AT + units, 256)).astype(BF)
        for part in range(2):
            piece_ref[UP_AT + part * 512 : UP_AT + (part + 1) * 512, :] = up[:, part * 128 : (part + 1) * 128]
        piece_ref[OUT_AT:, :] = mm_t(attn, both(DA_AT + pl.multiple_of(piece * 128, 128), 128)).astype(BF)


QKV_HALF = 768


def turn_back_kernel(back_ref, low_ref, base_ref, row_ref, acts_ref):
    core = lax.axis_index("c")
    cosine, sine = turns(base_ref, row_ref)
    half = ROWS // 2

    def unpack(one, two):
        upper_rows = jnp.concatenate([one[:, :HEAD_DIM], two[:, :HEAD_DIM]], axis=1)
        lower_rows = jnp.concatenate([one[:, HEAD_DIM:], two[:, HEAD_DIM:]], axis=1)
        return jnp.concatenate([upper_rows, lower_rows], axis=0)

    def write(rows, cols, value):
        side = jnp.where(core == cols // QKV_HALF, 0, 1)
        at = 512 + cols % QKV_HALF
        acts_ref[side, rows, at : at + 128] = value

    for clip in range(2):
        rows = slice(clip * ROWS, (clip + 1) * ROWS)
        for pair in range(HEADS // 2):
            one, two = 4 * pair + clip, 4 * pair + 2 + clip
            query = unpack(back_ref[one, ROWS : ROWS + half, :], back_ref[two, ROWS : ROWS + half, :]).astype(F32)
            first, second = back_ref[one, :ROWS, :], back_ref[two, :ROWS, :]
            key = jnp.concatenate([first[:, :HEAD_DIM], second[:, :HEAD_DIM]], axis=1).astype(F32)
            cols = pair * 128
            write(rows, cols, turn(query, cosine, -sine).astype(BF))
            write(rows, 512 + cols, turn(key, cosine, -sine).astype(BF))
            write(rows, 1024 + cols, jnp.concatenate([first[:, HEAD_DIM:], second[:, HEAD_DIM:]], axis=1))
    for side in range(2):
        acts_ref[side, :, :512] = low_ref[...]


def post_kernel(clip_ref, acts_ref, start_ref, mid_ref, type_ref, mlp_ref, gain_ref, w_ref, grad_ref, small_ref):
    swapped, core = clip_ref[0], lax.axis_index("c")
    down = jnp.zeros((2 * ROWS, 512), F32)
    for part in range(2):
        raw = acts_ref[jnp.where(core == part, 0, 1), :, 512:]
        down = down + mm_nt(raw, w_ref[:, part * QKV_HALF : (part + 1) * QKV_HALF])
    unit, inverse = norm_parts(start_ref[...])
    grad = mid_ref[...] + norm_back(down * gain_ref[...], unit, inverse)
    gain_grad = jnp.sum(down * unit, axis=0, keepdims=True)
    table = jnp.zeros((8, 512), F32)
    for clip in range(2):
        slot = jnp.where(swapped > 0, 1 - clip, clip)
        part = grad[clip * ROWS : (clip + 1) * ROWS]
        grad_ref[slot] = part
        kinds = type_ref[pl.ds(slot, 1), :]
        onehot = (lax.broadcasted_iota(jnp.int32, (8, ROWS), 0) == kinds).astype(F32)
        table = table + jnp.dot(onehot, part, precision=lax.Precision.HIGHEST, preferred_element_type=F32)
    row = lax.broadcasted_iota(jnp.int32, (8, 512), 0)
    small_ref[...] = jnp.where(row == 3, gain_grad, jnp.where(row == 4, mlp_ref[...], table))


def mix_weight_kernel(acts_ref, theirs_ref, small_ref, pieces_ref):
    low = jnp.concatenate([acts_ref[0, :, :512], theirs_ref[:, :512]], axis=0)
    raw = jnp.concatenate([acts_ref[0, :, 512:], theirs_ref[:, 512:]], axis=0)
    small = small_ref[...]
    for side in range(2):
        grad = mm_t(low, raw[:, side * 384 : (side + 1) * 384]).astype(BF)
        for strip in range(32):
            for part in range(3):
                block = grad[strip * 16 : (strip + 1) * 16, part * 128 : (part + 1) * 128]
                pieces_ref[2 * strip + side, part * 16 : (part + 1) * 16, :] = block
    for place in range(64):
        row, part = place // 4, place % 4
        value = jnp.zeros((8, 128), F32)
        if row < 5:
            value = jnp.broadcast_to(small[row : row + 1, part * 128 : (part + 1) * 128], (8, 128))
        pieces_ref[place, 48:, :] = value.astype(BF)


def total_kernel(pieces_ref, copies_ref):
    total = pieces_ref[0].astype(F32)
    for place in range(1, 64):
        total = total + pieces_ref[place].astype(F32)
    low = total.astype(BF)
    for place in range(64):
        copies_ref[place] = low


def mix_sum_kernel(own_ref, theirs_ref, qkv_ref, table_ref, gain_one_ref, gain_two_ref):
    core = lax.axis_index("c")
    for half in range(2):

        def write(pieces_ref):
            for place in range(64):
                strip, side = place // 2, place % 2
                cols = half * QKV_HALF + side * 384
                for part in range(3):
                    block = pieces_ref[place, part * 16 : (part + 1) * 16, :].astype(F32)
                    qkv_ref[strip * 16 : (strip + 1) * 16, cols + part * 128 : cols + (part + 1) * 128] = block

        pl.when(core == half)(functools.partial(write, own_ref))
        pl.when(core != half)(functools.partial(write, theirs_ref))
    for row in range(5):
        target, line = ((table_ref, row), (table_ref, row), (table_ref, row), (gain_one_ref, 0), (gain_two_ref, 0))[row]
        for part in range(4):
            both = own_ref[4 * row + part, 48:, :].astype(F32) + theirs_ref[4 * row + part, 48:, :].astype(F32)
            target[line : line + 1, part * 128 : (part + 1) * 128] = both[0:1]


def spread_kernel(*refs):
    pieces, (down, up, out, low, down_stage, up_stage, out_stage, in_sems, out_sems) = refs[:8], refs[8:]
    reads = [pltpu.make_async_copy(piece, low.at[at], in_sems.at[at]) for at, piece in enumerate(pieces)]
    for read in reads:
        read.start()
    writes = []

    def write(source, target):
        writes.append(pltpu.make_async_copy(source, target, out_sems.at[len(writes)]))
        writes[-1].start()

    for at, read in enumerate(reads):
        read.wait()
        core = lax.axis_index("c") if at < 4 else 1 - lax.axis_index("c")
        piece = lax.rem(lax.axis_index("z") + at, 4)
        units = pl.ds(pl.multiple_of(core * 1024 + piece * 256, 256), 256)
        for part in range(4):
            down_stage[at, :, part * 128 : (part + 1) * 128] = low[at, part * 256 : (part + 1) * 256, :].astype(F32)
        write(down_stage.at[at], down.at[units, :])
        for part in range(2):
            up_stage[at, :, part * 128 : (part + 1) * 128] = low[at, UP_AT + part * 512 : UP_AT + (part + 1) * 512, :].astype(F32)
        write(up_stage.at[at], up.at[:, units])
        out_stage[at] = low[at, OUT_AT:, :].astype(F32)
        write(out_stage.at[at], out.at[pl.ds(core * 256, 256), pl.ds(pl.multiple_of(piece * 128, 128), 128)])
    for copy in writes:
        copy.wait()


VMEM_SPEC = pl.BlockSpec(memory_space=pltpu.VMEM)
SMEM_SPEC = pl.BlockSpec(memory_space=pltpu.SMEM)


def call(kernel, name, outs, args, scalars=1, scratch=(), megabytes=28, flops=10**9, nbytes=4 * 2**20, exps=0):
    shapes = tuple(jax.ShapeDtypeStruct(shape, dtype) for shape, dtype in outs)
    return pl.pallas_call(
        kernel,
        out_shape=shapes,
        in_specs=[SMEM_SPEC] * scalars + [VMEM_SPEC] * (len(args) - scalars),
        out_specs=(VMEM_SPEC,) * len(shapes),
        scratch_shapes=[pltpu.VMEM(shape, dtype) for shape, dtype in scratch],
        compiler_params=pltpu.CompilerParams(vmem_limit_bytes=megabytes * 2**20),
        cost_estimate=pl.CostEstimate(flops=flops, bytes_accessed=nbytes, transcendentals=exps),
        name=name,
    )(*args)


WIDE = ((ONES + HEAD_DIM, LOCAL), F32)
LINE = ((1, LOCAL), F32)


QUERIES = ((128, LOCAL), BF)
GRADS = ((64, LOCAL), F32)
PACKED = ((FRAMES, ROWS // 2, 128), BF)


def attend(name, got, blocks, arrays, state=(), last=False, flops=10**9):
    first = not state
    outs = (PACKED, GRADS, LINE) if last else (WIDE, LINE) + ((QUERIES,) if first else ())
    scratch = ((WIDE, LINE) if last else ()) + (((2, len(blocks) * TILE, TILE), F32),)
    return call(
        functools.partial(forward_kernel, blocks, first, last), name, outs, (got,) + tuple(arrays) + tuple(state),
        scalars=0, scratch=scratch, flops=flops, nbytes=10**5,
    )


def attend_back(name, got, grad, ot, lse, offsets, arrays, state=(), flops=10**8):
    first, blocks = not state, ((len(offsets), LOCAL, 128), BF)
    flat = ((LOCAL, 128), BF)
    outs = (blocks, blocks) + ((GRADS, QUERIES, flat, QUERIES, flat, LINE) if first else (PACKED,))
    scratch = (() if first else (GRADS,)) + (((2, 2 * TILE, TILE), F32),)
    return call(
        functools.partial(backward_kernel, offsets, first), name, outs, (got, grad, ot, lse) + tuple(arrays) + tuple(state),
        scalars=0, scratch=scratch, megabytes=28, flops=flops, nbytes=10**5,
    )


PIECES = ((64, 56, 128), BF)
MIXED = (((512, 1536), F32), ((TYPES, 512), F32), ((1, 512), F32), ((1, 512), F32))


def spread(pieces):
    hbm = pl.BlockSpec(memory_space=pltpu.HBM)
    return pl.pallas_call(
        spread_kernel,
        out_shape=tuple(jax.ShapeDtypeStruct(shape, F32) for shape in ((2048, 512), (512, 2048), (512, 512))),
        in_specs=[hbm] * 8,
        out_specs=(hbm,) * 3,
        scratch_shapes=[
            pltpu.VMEM((8, PIECE_ROWS, 128), BF),
            pltpu.VMEM((8, 256, 512), F32),
            pltpu.VMEM((8, 512, 256), F32),
            pltpu.VMEM((8, 256, 128), F32),
            pltpu.SemaphoreType.DMA((8,)),
            pltpu.SemaphoreType.DMA((24,)),
        ],
        compiler_params=pltpu.CompilerParams(vmem_limit_bytes=40 * 2**20),
        cost_estimate=pl.CostEstimate(flops=10**7, bytes_accessed=15 * 2**20, transcendentals=0),
        name="spread",
    )(*pieces)


def swap(array, axes):
    return lax.all_to_all(array, axes, 0, 0, tiled=True)


def partner(array):
    return lax.ppermute(array, "c", [(0, 1), (1, 0)])


def along(array, step):
    return lax.ppermute(array, "z", [(place, (place - step) % 4) for place in range(4)])


def angle_tables():
    rates = BASE ** (-np.arange(HEAD_DIM // 2, dtype=np.float64) / (HEAD_DIM // 2))
    rates = np.tile(rates, 4)
    tables = []
    for places in (np.arange(128) * ROWS, np.arange(ROWS)):
        angles = places[:, None] * rates[None, :]
        tables.append(np.concatenate([np.cos(angles), np.sin(angles)], axis=1).astype(np.float32))
    return tables


def local(
    tokens, type_ids, clip_ids, frame_mask, type_table, norm_gain, qkv_weight, out_weight, mlp_gain, up_weight, down_weight, cotangent
):
    base_table, row_table = (jnp.asarray(table) for table in angle_tables())
    gain_one, gain_two = norm_gain[None], mlp_gain[None]
    tokens_here = 2 * ROWS
    sent, start, low = call(
        pre_kernel, "pre", (((2 * HEADS, 112, 128), BF), ((tokens_here, 512), F32), ((tokens_here, 512), BF)),
        (clip_ids, frame_mask, tokens, type_ids, type_table, gain_one, qkv_weight, base_table, row_table),
        scalars=2, scratch=(((tokens_here, 1536), F32), ((16, 512), BF)), megabytes=60,
    )

    got = swap(sent, CHIPS)
    own = got[:, :ROWS].reshape(LOCAL, 128)
    own_other = partner(own)
    up, down = along(own, 1), along(own, 3)
    *state, queries = attend("attend_near", got, ((0, 0), (1, 0)), (own, own_other), flops=2 * 10**10)
    clip_later, *state = lax.optimization_barrier((clip_ids, *state))
    one_of_each = clip_later[0] + clip_later[1] == 1
    up, down, one_of_each, *state = lax.optimization_barrier((up, down, one_of_each, *state))
    up_other, down_other = partner(up), partner(down)
    halves = along(up[: LOCAL // 2], 1), along(down[LOCAL // 2 :], 3)
    state = attend("attend_same", got, ((0, 1), (0, 3)), (up, down), (*state, queries), flops=10**8)
    halves, state = lax.optimization_barrier((halves, state))
    far = jnp.concatenate(halves, axis=0)
    far_other = partner(far)
    state = attend("attend_other", got, ((1, 1), (1, 3), (0, 2)), (up_other, down_other, far), (*state, queries), flops=10**8)
    packed, out_t, lse = attend("attend_far", got, ((1, 2),), (far_other,), (*state, queries), last=True)

    heads_out = swap(packed, CHIPS)
    output, grad_packed, grad_mid, mlp_part, acts = call(
        mlp_kernel, "mlp",
        (((2, ROWS, 512), BF), ((2 * HEADS, ROWS // 2, 128), BF), ((tokens_here, 512), F32), ((1, 512), F32), ((2, tokens_here, ACT_WIDTH), BF)),
        (clip_ids, heads_out, start, cotangent, gain_two, out_weight, up_weight, down_weight),
        scratch=(((tokens_here, 512), BF), ((tokens_here, 2048), BF)), flops=3 * 10**9, nbytes=8 * 2**20, exps=300000,
    )
    theirs = partner(acts[1])
    pieces = call(weight_kernel, "weights", (((PIECE_ROWS, 128), BF),) * 4, (acts, theirs), scalars=0)
    pieces, grad_packed = lax.optimization_barrier((pieces, grad_packed))
    arrived = [along(piece, -step) for step, piece in enumerate(pieces) if step]
    grad_out = swap(grad_packed, CHIPS)
    dsame, dother, *back_state = attend_back(
        "attend_back_others", got, grad_out, out_t, lse, (2, 1, 3), (far, far_other, up, up_other, down, down_other)
    )
    arrived, back_state = lax.optimization_barrier((arrived, back_state))
    summed = (dsame.astype(F32) + partner(dother).astype(F32)).astype(BF)
    piece = sum((part.astype(F32) for part in arrived), pieces[0].astype(F32)).astype(BF)
    piece, summed = lax.optimization_barrier((piece, summed))
    moved = [along(summed[at], -offset) for at, offset in enumerate((2, 1, 3))]
    piece = jnp.sum(swap(piece.reshape(16, PIECE_ROWS // 16, 128), CHIPS).astype(F32), axis=0).astype(BF)
    piece, back_state = lax.optimization_barrier((piece, back_state))
    near_same, near_other, dq = attend_back("attend_back_near", got, grad_out, out_t, lse, (0,), (own, own_other), back_state)
    near_sum = near_same[0].astype(F32) + partner(near_other[0]).astype(F32)
    own_grad = sum((part.astype(F32) for part in moved), near_sum).astype(BF)

    spread_piece = jnp.broadcast_to(piece[None], (16, PIECE_ROWS // 16, 128))
    back = swap(jnp.concatenate([own_grad.reshape(FRAMES, ROWS, 128), dq, spread_piece], axis=1), CHIPS)
    piece = back[:, ROWS + ROWS // 2 :].reshape(PIECE_ROWS, 128)
    pieces = [piece, along(piece, 1), along(piece, 3)]

    def ending(grads):
        (mix_acts,) = call(
            turn_back_kernel, "turn_back", (((2, tokens_here, 512 + QKV_HALF), BF),), (grads, low, base_table, row_table), scalars=0
        )
        input_grad, small = call(
            post_kernel, "post", (((2, ROWS, 512), F32), ((8, 512), F32)),
            (clip_ids, mix_acts, start, grad_mid, type_ids, mlp_part, gain_one, qkv_weight),
        )
        (strips_out,) = call(mix_weight_kernel, "mix_weights", (PIECES,), (mix_acts, partner(mix_acts[1]), small), scalars=0)
        return input_grad, *call(total_kernel, "total", (PIECES,), (swap(strips_out, ("y", "x", "z")),), scalars=0)

    def nothing(grads):
        return jnp.zeros((2, ROWS, 512), F32), jnp.zeros(*PIECES)

    input_grad, totals = lax.cond(one_of_each, ending, nothing, back[:, : ROWS + ROWS // 2])
    totals, pieces = lax.optimization_barrier((totals, pieces))
    mixed = swap(totals, ("y", "x", "z"))
    halves = along(pieces[1][: PIECE_ROWS // 2], 1), along(pieces[2][PIECE_ROWS // 2 :], 3)
    pieces = [*pieces[:2], jnp.concatenate(halves, axis=0), pieces[2]]
    sums = spread(pieces + [partner(piece) for piece in pieces])
    mixed, sums = lax.optimization_barrier((mixed, sums))
    qkv_sum, table_sum, gain_one_sum, gain_two_sum = call(mix_sum_kernel, "mix_sums", MIXED, (mixed, partner(mixed)), scalars=0)
    down_sum, up_sum, out_sum = sums
    return (output, input_grad, table_sum, gain_one_sum[0], qkv_sum, out_sum, gain_two_sum[0], up_sum, down_sum)


def solution(mesh):
    chips = Mesh(mesh.devices.reshape(4, 4, 2, 4), ("y", "x", "c", "z"))
    tm = ("y", "x", "c")
    rows = P(tm, "z", None)
    in_specs = (rows, P(tm, "z"), P(tm), P(tm)) + (P(),) * 7 + (rows,)
    out_specs = (rows, rows) + (P(),) * 7
    return jax.shard_map(local, mesh=chips, in_specs=in_specs, out_specs=out_specs, check_vma=False)
```

```python
import functools

import jax
import jax.numpy as jnp
import numpy as np
from jax import lax
from jax.experimental import pallas as pl
from jax.experimental.pallas import tpu as pltpu
from jax.sharding import Mesh
from jax.sharding import PartitionSpec as P

HEADS = 8
HEAD_DIM = 64
TYPES = 3
TILE = 256
FRAMES = 16
ROWS = 64
LOCAL = FRAMES * ROWS
GROUPS = LOCAL // TILE
MASKED = -1e30
ONES = 16
EPS = 1e-05
BASE = 10000.0
BF = jnp.bfloat16
F32 = jnp.float32
CHIPS = ("y", "x")


def mm(a, b):
    return jnp.dot(a, b, preferred_element_type=F32)


def mm_t(a, b):
    return lax.dot_general(a, b, (((0,), (0,)), ((), ())), preferred_element_type=F32)


def write_biases(bias_ref, at, is_other, key_block, row_block, parity, full):
    key = lax.broadcasted_iota(jnp.int32, (TILE, TILE), 0)
    query = lax.broadcasted_iota(jnp.int32, (TILE, TILE), 1)
    late = jnp.where(full, 0.0, MASKED)
    if is_other:
        before = key // ROWS < query // ROWS + parity
        bias_ref[0, at : at + TILE, :] = jnp.where(before, 0.0, MASKED)
        bias_ref[1, at : at + TILE, :] = jnp.where(before, late, MASKED)
        return
    before = key // ROWS < query // ROWS
    row_shift = jnp.where(key_block == row_block, 0, jnp.where(key_block < row_block, ROWS, -ROWS))
    own = (key // ROWS == query // ROWS) & ((key % ROWS) <= (query % ROWS) + row_shift)
    bias_ref[0, at : at + TILE, :] = jnp.where(before | own, 0.0, MASKED)
    bias_ref[1, at : at + TILE, :] = jnp.where(own, 0.0, jnp.where(before, late, MASKED))


def key_tiles(arrays, kb):
    return jnp.concatenate([array[pl.ds(kb * TILE, TILE), :] for array in arrays], axis=0)


def biased(scores, bias_ref, kb):
    bias = bias_ref[0 if kb == 0 else 1]
    if scores.shape[1] == TILE:
        return scores + bias
    return jnp.concatenate([scores[:, :TILE] + bias, scores[:, TILE:]], axis=1)


def strips(full, tile):
    @pl.when(full)
    def _():
        for kb in range(GROUPS):
            tile(kb, LOCAL - kb * TILE)

    @pl.when(jnp.logical_not(full))
    def _():
        for kb in range(GROUPS):
            tile(kb, TILE if kb else LOCAL)


def unfold_pair(first, second):
    return jnp.concatenate([first[:, :HEAD_DIM], first[:, HEAD_DIM:], second[:, :HEAD_DIM], second[:, HEAD_DIM:]], axis=0)


def forward_kernel(blocks, first, last, got_ref, *refs):
    arrays, rest = refs[: len(blocks)], refs[len(blocks) :]
    if first:
        acc_ref, top_ref, qt_ref, bias_ref = rest
        top_ref[...] = jnp.full(top_ref.shape, MASKED, F32)
        acc_ref[...] = jnp.zeros(acc_ref.shape, F32)
        write_queries(got_ref, qt_ref)
    else:
        in_acc, in_top, qt_ref = rest[:3]
        acc_ref, top_ref, bias_ref = rest[6:] if last else rest[3:]
        top_ref[...] = in_top[...]
        acc_ref[...] = in_acc[...]
    full, row_block, parity = places(got_ref)
    for place, (is_other, offset) in enumerate(blocks):
        write_biases(bias_ref, place * TILE, is_other, lax.rem(row_block + offset, 4), row_block, parity, full)

    def tile(kb, width):
        cols = pl.ds(kb * TILE, width)
        keys = key_tiles(arrays, kb)
        values = jnp.concatenate([jnp.ones((ONES, keys.shape[0]), BF), keys.T[HEAD_DIM:]], axis=0)
        scores = biased(mm(keys, qt_ref[:, cols]), bias_ref, kb)
        top_old = top_ref[:, cols]
        top_new = jnp.maximum(top_old, jnp.max(scores, axis=0, keepdims=True))
        weights = jnp.exp(scores - top_new).astype(BF)
        acc_ref[:, cols] = acc_ref[:, cols] * jnp.exp(top_old - top_new) + mm(values, weights)
        top_ref[:, cols] = top_new

    strips(full, tile)
    if last:
        packed_ref, ot_ref, lse_ref = rest[3:6]
        total = acc_ref[0:1, :]
        out_t = acc_ref[ONES:, :] / total
        ot_ref[...] = out_t
        lse_ref[...] = top_ref[...] + jnp.log(total)
        pack_frames(out_t.astype(BF), packed_ref)


def places(got_ref):
    full = jnp.max(got_ref[FRAMES - 1, ROWS + ROWS // 2 :, :].astype(F32)) > 0.5
    return full, lax.axis_index("z"), lax.axis_index("c")


def pack_frames(flipped, packed_ref):
    half = ROWS // 2
    for pair in range(FRAMES // 2):
        part = flipped[:, pair * 128 : (pair + 1) * 128].T
        packed_ref[2 * pair] = jnp.concatenate([part[:half], part[half:ROWS]], axis=1)
        packed_ref[2 * pair + 1] = jnp.concatenate([part[ROWS : ROWS + half], part[ROWS + half :]], axis=1)


def write_queries(got_ref, qt_ref):
    for pair in range(FRAMES // 2):
        rows = unfold_pair(got_ref[2 * pair, ROWS : ROWS + ROWS // 2, :], got_ref[2 * pair + 1, ROWS : ROWS + ROWS // 2, :])
        qt_ref[:HEAD_DIM, pair * 128 : (pair + 1) * 128] = rows.T
    qt_ref[HEAD_DIM:, :] = jnp.zeros((HEAD_DIM, LOCAL), BF)


def backward_kernel(offsets, first, got_ref, grad_ref, ot_ref, lse_ref, *refs):
    arrays, rest = refs[: 2 * len(offsets)], refs[2 * len(offsets) :]
    if first:
        dsame_ref, dother_ref, dqt_ref, qt_ref, q_ref, dot_ref, do_ref, delta_ref, bias_ref = rest
        write_queries(got_ref, qt_ref)
        blank = jnp.zeros((2 * ROWS, HEAD_DIM), BF)
        for pair in range(FRAMES // 2):
            span = pl.ds(pair * 128, 128)
            query = unfold_pair(got_ref[2 * pair, ROWS : ROWS + ROWS // 2, :], got_ref[2 * pair + 1, ROWS : ROWS + ROWS // 2, :])
            grad = unfold_pair(grad_ref[2 * pair], grad_ref[2 * pair + 1])
            q_ref[span, :] = jnp.concatenate([query, blank], axis=1)
            do_ref[span, :] = jnp.concatenate([blank, grad], axis=1)
            dot_ref[HEAD_DIM:, pair * 128 : (pair + 1) * 128] = grad.T
        dot_ref[:HEAD_DIM, :] = jnp.zeros((HEAD_DIM, LOCAL), BF)
        delta_ref[...] = jnp.sum(dot_ref[HEAD_DIM:, :].astype(F32) * ot_ref[...], axis=0, keepdims=True)
        dqt_ref[...] = jnp.zeros(dqt_ref.shape, F32)
    else:
        in_dqt, qt_ref, q_ref, dot_ref, do_ref, delta_ref, dsame_ref, dother_ref, packed_ref, dqt_ref, bias_ref = rest
        dqt_ref[...] = in_dqt[...]
    full, row_block, parity = places(got_ref)
    for block, offset in enumerate(offsets):
        key_block = lax.rem(row_block + offset, 4)
        for is_other in range(2):
            write_biases(bias_ref, is_other * TILE, is_other, key_block, row_block, parity, full)

        def tile(kb, width):
            cols = pl.ds(kb * TILE, width)
            rows = pl.ds(kb * TILE, TILE)
            keys = key_tiles(arrays[2 * block : 2 * block + 2], kb)
            scores = biased(mm(keys, qt_ref[:, cols]), bias_ref, kb)
            weights = jnp.exp(scores - lse_ref[:, cols])
            slopes = (weights * (mm(keys, dot_ref[:, cols]) - delta_ref[:, cols])).astype(BF)
            dqt_ref[:, cols] += mm(keys[:, :HEAD_DIM].T, slopes)
            both = mm(slopes, q_ref[cols, :]) + mm(weights.astype(BF), do_ref[cols, :])
            dsame_ref[block, rows, :] = both[:TILE, :].astype(BF)
            dother_ref[block, rows, :] = both[TILE:, :].astype(BF)

        strips(full, tile)
    if not first:
        pack_frames((dqt_ref[...] * HEAD_DIM**-0.5).astype(BF), packed_ref)


def norm_parts(hidden):
    centre = jnp.mean(hidden, axis=-1, keepdims=True)
    shifted = hidden - centre
    spread = jnp.mean(shifted * shifted, axis=-1, keepdims=True)
    inverse = lax.rsqrt(spread + EPS)
    return shifted * inverse, inverse


def norm_back(raised, unit, inverse):
    mean = jnp.mean(raised, axis=-1, keepdims=True)
    along = jnp.mean(raised * unit, axis=-1, keepdims=True)
    return (raised - mean - unit * along) * inverse


def turns(base_ref, row_ref):
    place = lax.axis_index(("y", "x", "c")) * 4 + lax.axis_index("z")
    base = base_ref[pl.ds(place, 1), :]
    cos_base, sin_base = base[:, :128], base[:, 128:]
    cos_row, sin_row = row_ref[:, :128], row_ref[:, 128:]
    cosine = cos_base * cos_row - sin_base * sin_row
    sine = sin_base * cos_row + cos_base * sin_row
    first = lax.broadcasted_iota(jnp.int32, sine.shape, 1) % HEAD_DIM < HEAD_DIM // 2
    return cosine, jnp.where(first, -sine, sine)


def turn(pair, cosine, sine):
    half = HEAD_DIM // 2
    first = lax.broadcasted_iota(jnp.int32, pair.shape, 1) % HEAD_DIM < half
    crossed = jnp.where(first, pltpu.roll(pair, 128 - half, 1), pltpu.roll(pair, half, 1))
    return pair * cosine + crossed * sine


def pre_kernel(clip_ref, mask_ref, tok_ref, type_ref, table_ref, gain_ref, w_ref, base_ref, row_ref, sent_ref, start_ref, low_ref, mixed_ref, kinds_ref):
    swapped = clip_ref[0]
    cosine, sine = turns(base_ref, row_ref)
    kinds_ref[...] = jnp.zeros(kinds_ref.shape, BF)
    kinds_ref[:TYPES, :] = table_ref[...]
    for clip in range(2):
        slot = jnp.where(swapped > 0, 1 - clip, clip)
        kinds = type_ref[pl.ds(slot, 1), :]
        onehot = (lax.broadcasted_iota(jnp.int32, (16, ROWS), 0) == kinds).astype(F32).astype(BF)
        hidden = tok_ref[slot].astype(F32) + mm_t(onehot, kinds_ref[...])
        unit, _ = norm_parts(hidden)
        start_ref[clip * ROWS : (clip + 1) * ROWS, :] = hidden
        low_ref[clip * ROWS : (clip + 1) * ROWS, :] = (unit * gain_ref[...]).astype(BF)
    width = 512
    for third in range(3):
        mixed_ref[:, third * width : (third + 1) * width] = mm(low_ref[...], w_ref[:, third * width : (third + 1) * width])
    for clip in range(2):
        slot = jnp.where(swapped > 0, 1 - clip, clip)
        rows = slice(clip * ROWS, (clip + 1) * ROWS)
        real = jnp.full((16, 128), mask_ref[slot], jnp.int32).astype(F32).astype(BF)
        for pair in range(HEADS // 2):
            query = (turn(mixed_ref[rows, pair * 128 : (pair + 1) * 128], cosine, sine).astype(BF) * HEAD_DIM**-0.5).astype(BF)
            key = turn(mixed_ref[rows, width + pair * 128 : width + (pair + 1) * 128], cosine, sine).astype(BF)
            value = mixed_ref[rows, 2 * width + pair * 128 : 2 * width + (pair + 1) * 128].astype(BF)
            for side in range(2):
                to = (2 * pair + side) * 2 + clip
                lanes = slice(side * HEAD_DIM, (side + 1) * HEAD_DIM)
                sent_ref[to, :ROWS, :] = jnp.concatenate([key[:, lanes], value[:, lanes]], axis=1)
                sent_ref[to, ROWS : ROWS + ROWS // 2, :] = jnp.concatenate([query[: ROWS // 2, lanes], query[ROWS // 2 :, lanes]], axis=1)
                sent_ref[to, ROWS + ROWS // 2 :, :] = real


def mm_nt(a, b):
    return lax.dot_general(a, b, (((1,), (1,)), ((), ())), preferred_element_type=F32)


FF_PART = 512
GELU_SCALE = float(np.sqrt(2.0 / np.pi))
GELU_CUBE = 0.044715
G_AT, DU_AT, N2_AT, DY_AT, AT_AT, DA_AT, ACT_WIDTH = 0, 1024, 2048, 2560, 3072, 3328, 3840


def mlp_kernel(
    clip_ref, got_ref, start_ref, cot_ref, gain_ref, wo_ref, wu_ref, wd_ref, out_ref, packed_ref, mid_ref, gaing_ref, acts_ref,
    attn_ref, slope_ref,
):
    swapped, core = clip_ref[0], lax.axis_index("c")
    keep, send = 0, 1
    for clip in range(2):
        for pair in range(HEADS // 2):
            one, two = got_ref[4 * pair + clip], got_ref[4 * pair + 2 + clip]
            attn_ref[clip * ROWS : clip * ROWS + ROWS // 2, pair * 128 : (pair + 1) * 128] = jnp.concatenate([one[:, :HEAD_DIM], two[:, :HEAD_DIM]], axis=1)
            attn_ref[clip * ROWS + ROWS // 2 : (clip + 1) * ROWS, pair * 128 : (pair + 1) * 128] = jnp.concatenate([one[:, HEAD_DIM:], two[:, HEAD_DIM:]], axis=1)
    slots = [jnp.where(swapped > 0, 1 - clip, clip) for clip in range(2)]
    grad_low = jnp.concatenate([cot_ref[slots[0]], cot_ref[slots[1]]], axis=0)
    attn = attn_ref[...]
    middle = start_ref[...] + mm(attn, wo_ref[...])
    unit, inverse = norm_parts(middle)
    low = (unit * gain_ref[...]).astype(BF)
    final = middle
    for part in range(4):
        cols = slice(part * FF_PART, (part + 1) * FF_PART)
        upper = mm(low, wu_ref[:, cols])
        square = upper * upper
        bend = jnp.tanh(GELU_SCALE * (upper + GELU_CUBE * (square * upper)))
        act = (0.5 * upper * (1.0 + bend)).astype(BF)
        rise = 0.5 * (1.0 + bend) + 0.5 * upper * (1.0 - bend * bend) * (GELU_SCALE * (1.0 + 3.0 * GELU_CUBE * square))
        final = final + mm(act, wd_ref[cols, :])
        slope = (mm_nt(grad_low, wd_ref[cols, :]) * rise).astype(BF)
        slope_ref[:, cols] = slope
        side = jnp.where(core == part // 2, keep, send)
        at = (part % 2) * FF_PART
        acts_ref[side, :, G_AT + at : G_AT + at + FF_PART] = act
        acts_ref[side, :, DU_AT + at : DU_AT + at + FF_PART] = slope
    for clip in range(2):
        out_ref[slots[clip]] = final[clip * ROWS : (clip + 1) * ROWS].astype(BF)
    down = mm_nt(slope_ref[...], wu_ref[...])
    gaing_ref[...] = jnp.sum(down * unit, axis=0, keepdims=True)
    grad_mid = grad_low.astype(F32) + norm_back(down * gain_ref[...], unit, inverse)
    mid_ref[...] = grad_mid
    grad_mid_low = grad_mid.astype(BF)
    grad_attn = mm_nt(grad_mid_low, wo_ref[...]).astype(BF)
    for side in (keep, send):
        acts_ref[side, :, N2_AT : N2_AT + 512] = low
        acts_ref[side, :, DY_AT : DY_AT + 512] = grad_low
        acts_ref[side, :, DA_AT : DA_AT + 512] = grad_mid_low
    for half in range(2):
        acts_ref[jnp.where(core == half, keep, send), :, AT_AT : AT_AT + 256] = attn[:, half * 256 : (half + 1) * 256]
    for clip in range(2):
        for pair in range(HEADS // 2):
            rows = grad_attn[clip * ROWS : (clip + 1) * ROWS, pair * 128 : (pair + 1) * 128]
            upper_rows, lower_rows = rows[: ROWS // 2], rows[ROWS // 2 :]
            packed_ref[4 * pair + clip] = jnp.concatenate([upper_rows[:, :HEAD_DIM], lower_rows[:, :HEAD_DIM]], axis=1)
            packed_ref[4 * pair + 2 + clip] = jnp.concatenate([upper_rows[:, HEAD_DIM:], lower_rows[:, HEAD_DIM:]], axis=1)


UP_AT, OUT_AT, PIECE_ROWS = 1024, 2048, 2304


def weight_kernel(acts_ref, theirs_ref, *piece_refs):
    block = lax.axis_index("z")

    def both(at, width):
        return jnp.concatenate([acts_ref[0, :, pl.ds(at, width)], theirs_ref[:, pl.ds(at, width)]], axis=0)

    grad_low, low, attn = both(DY_AT, 512), both(N2_AT, 512), both(AT_AT, 256)
    for step, piece_ref in enumerate(piece_refs):
        piece = lax.rem(block + step, 4)
        units = pl.multiple_of(piece * 256, 256)
        down = mm_t(both(G_AT + units, 256), grad_low).astype(BF)
        for part in range(4):
            piece_ref[part * 256 : (part + 1) * 256, :] = down[:, part * 128 : (part + 1) * 128]
        up = mm_t(low, both(DU_AT + units, 256)).astype(BF)
        for part in range(2):
            piece_ref[UP_AT + part * 512 : UP_AT + (part + 1) * 512, :] = up[:, part * 128 : (part + 1) * 128]
        piece_ref[OUT_AT:, :] = mm_t(attn, both(DA_AT + pl.multiple_of(piece * 128, 128), 128)).astype(BF)


QKV_HALF = 768


def turn_back_kernel(back_ref, low_ref, base_ref, row_ref, acts_ref):
    core = lax.axis_index("c")
    cosine, sine = turns(base_ref, row_ref)
    half = ROWS // 2

    def unpack(one, two):
        upper_rows = jnp.concatenate([one[:, :HEAD_DIM], two[:, :HEAD_DIM]], axis=1)
        lower_rows = jnp.concatenate([one[:, HEAD_DIM:], two[:, HEAD_DIM:]], axis=1)
        return jnp.concatenate([upper_rows, lower_rows], axis=0)

    def write(rows, cols, value):
        side = jnp.where(core == cols // QKV_HALF, 0, 1)
        at = 512 + cols % QKV_HALF
        acts_ref[side, rows, at : at + 128] = value

    for clip in range(2):
        rows = slice(clip * ROWS, (clip + 1) * ROWS)
        for pair in range(HEADS // 2):
            one, two = 4 * pair + clip, 4 * pair + 2 + clip
            query = unpack(back_ref[one, ROWS : ROWS + half, :], back_ref[two, ROWS : ROWS + half, :]).astype(F32)
            first, second = back_ref[one, :ROWS, :], back_ref[two, :ROWS, :]
            key = jnp.concatenate([first[:, :HEAD_DIM], second[:, :HEAD_DIM]], axis=1).astype(F32)
            cols = pair * 128
            write(rows, cols, turn(query, cosine, -sine).astype(BF))
            write(rows, 512 + cols, turn(key, cosine, -sine).astype(BF))
            write(rows, 1024 + cols, jnp.concatenate([first[:, HEAD_DIM:], second[:, HEAD_DIM:]], axis=1))
    for side in range(2):
        acts_ref[side, :, :512] = low_ref[...]


def post_kernel(clip_ref, acts_ref, start_ref, mid_ref, type_ref, mlp_ref, gain_ref, w_ref, grad_ref, small_ref):
    swapped, core = clip_ref[0], lax.axis_index("c")
    down = jnp.zeros((2 * ROWS, 512), F32)
    for part in range(2):
        raw = acts_ref[jnp.where(core == part, 0, 1), :, 512:]
        down = down + mm_nt(raw, w_ref[:, part * QKV_HALF : (part + 1) * QKV_HALF])
    unit, inverse = norm_parts(start_ref[...])
    grad = mid_ref[...] + norm_back(down * gain_ref[...], unit, inverse)
    gain_grad = jnp.sum(down * unit, axis=0, keepdims=True)
    table = jnp.zeros((8, 512), F32)
    for clip in range(2):
        slot = jnp.where(swapped > 0, 1 - clip, clip)
        part = grad[clip * ROWS : (clip + 1) * ROWS]
        grad_ref[slot] = part
        kinds = type_ref[pl.ds(slot, 1), :]
        onehot = (lax.broadcasted_iota(jnp.int32, (8, ROWS), 0) == kinds).astype(F32)
        table = table + jnp.dot(onehot, part, precision=lax.Precision.HIGHEST, preferred_element_type=F32)
    row = lax.broadcasted_iota(jnp.int32, (8, 512), 0)
    small_ref[...] = jnp.where(row == 3, gain_grad, jnp.where(row == 4, mlp_ref[...], table))


def mix_weight_kernel(acts_ref, theirs_ref, small_ref, pieces_ref):
    low = jnp.concatenate([acts_ref[0, :, :512], theirs_ref[:, :512]], axis=0)
    raw = jnp.concatenate([acts_ref[0, :, 512:], theirs_ref[:, 512:]], axis=0)
    small = small_ref[...]
    for side in range(2):
        grad = mm_t(low, raw[:, side * 384 : (side + 1) * 384]).astype(BF)
        for strip in range(32):
            for part in range(3):
                block = grad[strip * 16 : (strip + 1) * 16, part * 128 : (part + 1) * 128]
                pieces_ref[2 * strip + side, part * 16 : (part + 1) * 16, :] = block
    for place in range(64):
        row, part = place // 4, place % 4
        value = jnp.zeros((8, 128), F32)
        if row < 5:
            value = jnp.broadcast_to(small[row : row + 1, part * 128 : (part + 1) * 128], (8, 128))
        pieces_ref[place, 48:, :] = value.astype(BF)


def total_kernel(pieces_ref, copies_ref):
    total = pieces_ref[0].astype(F32)
    for place in range(1, 64):
        total = total + pieces_ref[place].astype(F32)
    low = total.astype(BF)
    for place in range(64):
        copies_ref[place] = low


def mix_sum_kernel(own_ref, theirs_ref, qkv_ref, table_ref, gain_one_ref, gain_two_ref, stage_ref, sems):
    core = lax.axis_index("c")
    moves = []
    for group in range(8):
        for strip in range(4 * group, 4 * group + 4):
            for pieces_ref, half in ((own_ref, core), (theirs_ref, 1 - core)):
                for place in (2 * strip, 2 * strip + 1):
                    for part in range(3):
                        cols = pl.ds(pl.multiple_of(half * QKV_HALF, 128) + place % 2 * 384 + part * 128, 128)
                        stage_ref[strip * 16 : (strip + 1) * 16, cols] = pieces_ref[place, part * 16 : (part + 1) * 16, :].astype(F32)
        rows = pl.ds(group * 64, 64)
        moves.append(pltpu.make_async_copy(stage_ref.at[rows, :], qkv_ref.at[rows, :], sems.at[group]))
        moves[-1].start()
    for row in range(5):
        target, line = ((table_ref, row), (table_ref, row), (table_ref, row), (gain_one_ref, 0), (gain_two_ref, 0))[row]
        for part in range(4):
            both = own_ref[4 * row + part, 48:, :].astype(F32) + theirs_ref[4 * row + part, 48:, :].astype(F32)
            target[line : line + 1, part * 128 : (part + 1) * 128] = both[0:1]
    for move in moves:
        move.wait()


def spread_kernel(*refs):
    pieces, (down, up, out, low, down_stage, up_stage, out_stage, in_sems, out_sems) = refs[:8], refs[8:]
    reads = [pltpu.make_async_copy(piece, low.at[at], in_sems.at[at]) for at, piece in enumerate(pieces)]
    for read in reads:
        read.start()
    writes = []

    def write(source, target):
        writes.append(pltpu.make_async_copy(source, target, out_sems.at[len(writes)]))
        writes[-1].start()

    for at, read in enumerate(reads):
        read.wait()
        core = lax.axis_index("c") if at < 4 else 1 - lax.axis_index("c")
        piece = lax.rem(lax.axis_index("z") + at, 4)
        units = pl.ds(pl.multiple_of(core * 1024 + piece * 256, 256), 256)
        for part in range(4):
            down_stage[at, :, part * 128 : (part + 1) * 128] = low[at, part * 256 : (part + 1) * 256, :].astype(F32)
        write(down_stage.at[at], down.at[units, :])
        for part in range(2):
            up_stage[at, :, part * 128 : (part + 1) * 128] = low[at, UP_AT + part * 512 : UP_AT + (part + 1) * 512, :].astype(F32)
        write(up_stage.at[at], up.at[:, units])
        out_stage[at] = low[at, OUT_AT:, :].astype(F32)
        write(out_stage.at[at], out.at[pl.ds(core * 256, 256), pl.ds(pl.multiple_of(piece * 128, 128), 128)])
    for copy in writes:
        copy.wait()


VMEM_SPEC = pl.BlockSpec(memory_space=pltpu.VMEM)
SMEM_SPEC = pl.BlockSpec(memory_space=pltpu.SMEM)


def call(kernel, name, outs, args, scalars=1, scratch=(), megabytes=28, flops=10**9, nbytes=4 * 2**20, exps=0):
    shapes = tuple(jax.ShapeDtypeStruct(shape, dtype) for shape, dtype in outs)
    return pl.pallas_call(
        kernel,
        out_shape=shapes,
        in_specs=[SMEM_SPEC] * scalars + [VMEM_SPEC] * (len(args) - scalars),
        out_specs=(VMEM_SPEC,) * len(shapes),
        scratch_shapes=[pltpu.VMEM(shape, dtype) for shape, dtype in scratch],
        compiler_params=pltpu.CompilerParams(vmem_limit_bytes=megabytes * 2**20),
        cost_estimate=pl.CostEstimate(flops=flops, bytes_accessed=nbytes, transcendentals=exps),
        name=name,
    )(*args)


WIDE = ((ONES + HEAD_DIM, LOCAL), F32)
LINE = ((1, LOCAL), F32)


QUERIES = ((128, LOCAL), BF)
GRADS = ((64, LOCAL), F32)
PACKED = ((FRAMES, ROWS // 2, 128), BF)


def attend(name, got, blocks, arrays, state=(), last=False, flops=10**9):
    first = not state
    outs = (PACKED, GRADS, LINE) if last else (WIDE, LINE) + ((QUERIES,) if first else ())
    scratch = ((WIDE, LINE) if last else ()) + (((2, len(blocks) * TILE, TILE), F32),)
    return call(
        functools.partial(forward_kernel, blocks, first, last), name, outs, (got,) + tuple(arrays) + tuple(state),
        scalars=0, scratch=scratch, flops=flops, nbytes=10**5,
    )


def attend_back(name, got, grad, ot, lse, offsets, arrays, state=(), flops=10**8):
    first, blocks = not state, ((len(offsets), LOCAL, 128), BF)
    flat = ((LOCAL, 128), BF)
    outs = (blocks, blocks) + ((GRADS, QUERIES, flat, QUERIES, flat, LINE) if first else (PACKED,))
    scratch = (() if first else (GRADS,)) + (((2, 2 * TILE, TILE), F32),)
    return call(
        functools.partial(backward_kernel, offsets, first), name, outs, (got, grad, ot, lse) + tuple(arrays) + tuple(state),
        scalars=0, scratch=scratch, megabytes=28, flops=flops, nbytes=10**5,
    )


PIECES = ((64, 56, 128), BF)
MIXED = (((512, 1536), F32), ((TYPES, 512), F32), ((1, 512), F32), ((1, 512), F32))


def spread(pieces):
    hbm = pl.BlockSpec(memory_space=pltpu.HBM)
    return pl.pallas_call(
        spread_kernel,
        out_shape=tuple(jax.ShapeDtypeStruct(shape, F32) for shape in ((2048, 512), (512, 2048), (512, 512))),
        in_specs=[hbm] * 8,
        out_specs=(hbm,) * 3,
        scratch_shapes=[
            pltpu.VMEM((8, PIECE_ROWS, 128), BF),
            pltpu.VMEM((8, 256, 512), F32),
            pltpu.VMEM((8, 512, 256), F32),
            pltpu.VMEM((8, 256, 128), F32),
            pltpu.SemaphoreType.DMA((8,)),
            pltpu.SemaphoreType.DMA((24,)),
        ],
        compiler_params=pltpu.CompilerParams(vmem_limit_bytes=40 * 2**20),
        cost_estimate=pl.CostEstimate(flops=10**7, bytes_accessed=15 * 2**20, transcendentals=0),
        name="spread",
    )(*pieces)


def mix_sums(own, theirs):
    return pl.pallas_call(
        mix_sum_kernel,
        out_shape=tuple(jax.ShapeDtypeStruct(shape, dtype) for shape, dtype in MIXED),
        in_specs=[VMEM_SPEC] * 2,
        out_specs=(pl.BlockSpec(memory_space=pltpu.HBM),) + (VMEM_SPEC,) * 3,
        scratch_shapes=[pltpu.VMEM(MIXED[0][0], F32), pltpu.SemaphoreType.DMA((8,))],
        compiler_params=pltpu.CompilerParams(vmem_limit_bytes=28 * 2**20),
        cost_estimate=pl.CostEstimate(flops=10**9, bytes_accessed=4 * 2**20, transcendentals=0),
        name="mix_sums",
    )(own, theirs)


def swap(array, axes):
    return lax.all_to_all(array, axes, 0, 0, tiled=True)


def partner(array):
    return lax.ppermute(array, "c", [(0, 1), (1, 0)])


def along(array, step):
    return lax.ppermute(array, "z", [(place, (place - step) % 4) for place in range(4)])


def angle_tables():
    rates = BASE ** (-np.arange(HEAD_DIM // 2, dtype=np.float64) / (HEAD_DIM // 2))
    rates = np.tile(rates, 4)
    tables = []
    for places in (np.arange(128) * ROWS, np.arange(ROWS)):
        angles = places[:, None] * rates[None, :]
        tables.append(np.concatenate([np.cos(angles), np.sin(angles)], axis=1).astype(np.float32))
    return tables


def local(
    tokens, type_ids, clip_ids, frame_mask, type_table, norm_gain, qkv_weight, out_weight, mlp_gain, up_weight, down_weight, cotangent
):
    base_table, row_table = (jnp.asarray(table) for table in angle_tables())
    gain_one, gain_two = norm_gain[None], mlp_gain[None]
    tokens_here = 2 * ROWS
    sent, start, low = call(
        pre_kernel, "pre", (((2 * HEADS, 112, 128), BF), ((tokens_here, 512), F32), ((tokens_here, 512), BF)),
        (clip_ids, frame_mask, tokens, type_ids, type_table, gain_one, qkv_weight, base_table, row_table),
        scalars=2, scratch=(((tokens_here, 1536), F32), ((16, 512), BF)), megabytes=60,
    )

    got = swap(sent, CHIPS)
    own = got[:, :ROWS].reshape(LOCAL, 128)
    own_other = partner(own)
    up, down = along(own, 1), along(own, 3)
    *state, queries = attend("attend_near", got, ((0, 0), (1, 0)), (own, own_other), flops=2 * 10**10)
    clip_later, *state = lax.optimization_barrier((clip_ids, *state))
    one_of_each = clip_later[0] + clip_later[1] == 1
    up, down, one_of_each, *state = lax.optimization_barrier((up, down, one_of_each, *state))
    up_other, down_other = partner(up), partner(down)
    halves = along(up[: LOCAL // 2], 1), along(down[LOCAL // 2 :], 3)
    state = attend("attend_same", got, ((0, 1), (0, 3)), (up, down), (*state, queries), flops=10**8)
    halves, state = lax.optimization_barrier((halves, state))
    far = jnp.concatenate(halves, axis=0)
    far_other = partner(far)
    state = attend("attend_other", got, ((1, 1), (1, 3), (0, 2)), (up_other, down_other, far), (*state, queries), flops=10**8)
    packed, out_t, lse = attend("attend_far", got, ((1, 2),), (far_other,), (*state, queries), last=True)

    heads_out = swap(packed, CHIPS)
    output, grad_packed, grad_mid, mlp_part, acts = call(
        mlp_kernel, "mlp",
        (((2, ROWS, 512), BF), ((2 * HEADS, ROWS // 2, 128), BF), ((tokens_here, 512), F32), ((1, 512), F32), ((2, tokens_here, ACT_WIDTH), BF)),
        (clip_ids, heads_out, start, cotangent, gain_two, out_weight, up_weight, down_weight),
        scratch=(((tokens_here, 512), BF), ((tokens_here, 2048), BF)), flops=3 * 10**9, nbytes=8 * 2**20, exps=300000,
    )
    theirs = partner(acts[1])
    pieces = call(weight_kernel, "weights", (((PIECE_ROWS, 128), BF),) * 4, (acts, theirs), scalars=0)
    pieces, grad_packed = lax.optimization_barrier((pieces, grad_packed))
    arrived = [along(piece, -step) for step, piece in enumerate(pieces) if step]
    grad_out = swap(grad_packed, CHIPS)
    dsame, dother, *back_state = attend_back(
        "attend_back_others", got, grad_out, out_t, lse, (2, 1, 3), (far, far_other, up, up_other, down, down_other)
    )
    arrived, back_state = lax.optimization_barrier((arrived, back_state))
    summed = (dsame.astype(F32) + partner(dother).astype(F32)).astype(BF)
    piece = sum((part.astype(F32) for part in arrived), pieces[0].astype(F32)).astype(BF)
    piece, summed = lax.optimization_barrier((piece, summed))
    moved = [along(summed[at], -offset) for at, offset in enumerate((2, 1, 3))]
    piece = jnp.sum(swap(piece.reshape(16, PIECE_ROWS // 16, 128), CHIPS).astype(F32), axis=0).astype(BF)
    piece, back_state = lax.optimization_barrier((piece, back_state))
    near_same, near_other, dq = attend_back("attend_back_near", got, grad_out, out_t, lse, (0,), (own, own_other), back_state)
    near_sum = near_same[0].astype(F32) + partner(near_other[0]).astype(F32)
    own_grad = sum((part.astype(F32) for part in moved), near_sum).astype(BF)

    spread_piece = jnp.broadcast_to(piece[None], (16, PIECE_ROWS // 16, 128))
    back = swap(jnp.concatenate([own_grad.reshape(FRAMES, ROWS, 128), dq, spread_piece], axis=1), CHIPS)
    piece = back[:, ROWS + ROWS // 2 :].reshape(PIECE_ROWS, 128)
    pieces = [piece, along(piece, 1), along(piece, 3)]

    def ending(grads):
        (mix_acts,) = call(
            turn_back_kernel, "turn_back", (((2, tokens_here, 512 + QKV_HALF), BF),), (grads, low, base_table, row_table), scalars=0
        )
        input_grad, small = call(
            post_kernel, "post", (((2, ROWS, 512), F32), ((8, 512), F32)),
            (clip_ids, mix_acts, start, grad_mid, type_ids, mlp_part, gain_one, qkv_weight),
        )
        (strips_out,) = call(mix_weight_kernel, "mix_weights", (PIECES,), (mix_acts, partner(mix_acts[1]), small), scalars=0)
        return input_grad, *call(total_kernel, "total", (PIECES,), (swap(strips_out, ("y", "x", "z")),), scalars=0)

    def nothing(grads):
        return jnp.zeros((2, ROWS, 512), F32), jnp.zeros(*PIECES)

    input_grad, totals = lax.cond(one_of_each, ending, nothing, back[:, : ROWS + ROWS // 2])
    totals, pieces = lax.optimization_barrier((totals, pieces))
    mixed = swap(totals, ("y", "x", "z"))
    halves = along(pieces[1][: PIECE_ROWS // 2], 1), along(pieces[2][PIECE_ROWS // 2 :], 3)
    pieces = [*pieces[:2], jnp.concatenate(halves, axis=0), pieces[2]]
    sums = spread(pieces + [partner(piece) for piece in pieces])
    mixed, sums = lax.optimization_barrier((mixed, sums))
    qkv_sum, table_sum, gain_one_sum, gain_two_sum = mix_sums(mixed, partner(mixed))
    down_sum, up_sum, out_sum = sums
    return (output, input_grad, table_sum, gain_one_sum[0], qkv_sum, out_sum, gain_two_sum[0], up_sum, down_sum)


def solution(mesh):
    chips = Mesh(mesh.devices.reshape(4, 4, 2, 4), ("y", "x", "c", "z"))
    tm = ("y", "x", "c")
    rows = P(tm, "z", None)
    in_specs = (rows, P(tm, "z"), P(tm), P(tm)) + (P(),) * 7 + (rows,)
    out_specs = (rows, rows) + (P(),) * 7
    return jax.shard_map(local, mesh=chips, in_specs=in_specs, out_specs=out_specs, check_vma=False)
```
